32 devices in a mesh: groups: 2 (over y), scen: 8 (over z, x), lane: 1, dep: 2 (over core).
Axes of the slice: x: 2, y: 2, z: 4, core: 2. Of those that a mesh axis runs over, the one named last changes fastest.
Arguments:
- tiles: bfloat16 [32, 1, 2, 8, 128, 128], P(('groups', 'scen'), 'lane', 'dep'), parts along dimension 0, may hold values from -0.5 to 0.5
- row_index: int32 [32, 1, 2, 8], P(('groups', 'scen'), 'lane', 'dep'), parts along dimension 0, may hold values from 0 to 15
- col_index: int32 [32, 1, 2, 8], P(('groups', 'scen'), 'lane', 'dep'), parts along dimension 0, may hold values from 0 to 15
- tile_count: int32 [32, 1, 2], P(('groups', 'scen'), 'lane', 'dep'), parts along dimension 0, may hold values from 4 to 8, as said below
- demand: float32 [32, 2048], P(('groups', 'scen'), 'lane'), parts along dimension 0, may hold values from -12 to 12
- root_cost: float32 [8192], P(('groups', 'dep')), parts along dimension 0, may hold values from -1 to 0.5
- branch_cost: float32 [32, 4096], P(('groups', 'scen'), 'dep'), parts along dimension 0, may hold values from -0.8 to 0.4
- dispatch_cost: float32 [32, 4096], P(('groups', 'scen'), 'dep'), parts along dimension 0, may hold values from -0.6 to 0.3
- branch_of: int32 [32], P(('groups', 'scen')), parts along dimension 0, may hold values from 0 to 7, as said below
Outputs:
- fleet_plan: float32 [32, 4096], P(('groups', 'scen'), 'dep'), parts along dimension 0
- assign_plan: float32 [32, 4096], P(('groups', 'scen'), 'dep'), parts along dimension 0
- dispatch_plan: float32 [32, 4096], P(('groups', 'scen'), 'dep'), parts along dimension 0
- cover_dual: float32 [32, 2048], P(('groups', 'scen'), 'lane'), parts along dimension 0
- fleet_price: float32 [32, 4096], P(('groups', 'scen'), 'dep'), parts along dimension 0
- assign_price: float32 [32, 4096], P(('groups', 'scen'), 'dep'), parts along dimension 0
The draws below stay inside these ranges and needn't reach their ends.
There are 2 independent parts, one for each index of `groups`. The reference program is written for one: setup_inputs(seed, part) draws one part's arguments, and reference() takes and returns one part's arrays. A program takes and returns all parts, laid end to end along the dimension named above; each array names one. Nothing has to cross between parts.
Inputs may be any that keep to these rules, and one draw needn't show every extreme that they name: `tile_count`: at least half of the 8 slots of each block are live, and some block has all of them live. `branch_of`: every branch holds exactly 2 scenarios.
All inputs are finite; a program needn't handle non-finite values.
Results may differ from the reference program's by a relative error of at most 0.0022.
Values may be sent and summed in bfloat16 or wider, within the bound.
A program may use at most 64 MiB of HBM per device.

```python
import jax
import jax.numpy as jnp
from jax import lax

TILE = 128
TYPES = 64
DEP_DEV = 32
ROW_TILES = 16
SLOTS = 8
BRANCHES = 8
ITERS = 2
STEPS = 4
COL_TILES = 16
SCEN = 16
LANES = 2048
COLS = 4096
N_LANE = 1
N_DEP = 2


def draw_tile_count(key, part):
    key = jax.random.fold_in(key, 11)
    first_key, second_key = jax.random.split(key)
    total = SCEN * N_LANE * N_DEP
    counts = jax.random.randint(first_key, (total,), SLOTS // 2, SLOTS + 1)
    chosen = jax.random.randint(second_key, (), 0, total)
    flat_counts = jnp.where(jnp.arange(total) == chosen, SLOTS, counts)
    return flat_counts.reshape(SCEN, N_LANE, N_DEP).astype(jnp.int32)


def draw_branch_of(key, part):
    key = jax.random.fold_in(key, 17)
    shuffled = jax.random.permutation(key, SCEN)
    return (shuffled // (SCEN // BRANCHES)).astype(jnp.int32)


def draw_demand(key, part):
    key = jax.random.fold_in(key, 23)
    rough_key, scale_key = jax.random.split(key)
    row_place = jnp.arange(LANES, dtype=jnp.float32) / LANES
    row_scale = 1.0 + 2.0 * row_place
    scen_scale = jax.random.uniform(scale_key, (SCEN, 1), jnp.float32, 0.4, 1.0)
    rough_part = jax.random.normal(rough_key, (SCEN, LANES), jnp.float32) * 2.0
    return jnp.clip(rough_part * row_scale[None, :] * scen_scale, -12.0, 12.0)


def with_ends(entries, rng, least, top_value):
    extent = entries.shape
    index_at = [jax.random.randint(jax.random.fold_in(rng, axis), (), 0, extent[axis]) for axis in range(len(extent))]
    entries = entries.at[tuple(index_at)].set(least)
    longest = extent.index(max(extent))
    index_at[longest] = (index_at[longest] + 1) % extent[longest]
    return entries.at[tuple(index_at)].set(top_value)


def levels(rng, shape, pieces, smallest, high):
    level, own = 1.0, jax.random.fold_in(rng, 6)
    for axis_at, shards_of in pieces:
        heights = jnp.exp(jax.random.uniform(jax.random.fold_in(own, axis_at), (shards_of,), jnp.float32, smallest / len(pieces), high / len(pieces)))
        level = level * jnp.repeat(heights, shape[axis_at] // shards_of).reshape([-1 if axis == axis_at else 1 for axis in range(len(shape))])
    return level


def centred(key, extent, scale, bound, cuts=(), held_as=jnp.bfloat16):
    result = scale * jax.random.normal(key, extent, jnp.float32)
    if cuts:
        result = result * levels(key, extent, cuts, -0.22, 0.18)
    return jnp.clip(result, -bound, bound).astype(held_as)


def setup_inputs(seed: int = 0, part: int = 0) -> dict:
    key_of = jax.random.split(jax.random.key(seed), 10)
    part_keys = jax.random.split(jax.random.fold_in(key_of[9], part), 10)
    tiles = centred(part_keys[0], (SCEN, N_LANE, N_DEP, SLOTS, TILE, TILE), (TILE * N_DEP * SLOTS // ROW_TILES) ** -0.5, 0.5, ((0, 8), (2, 2)))
    row_index = with_ends(jax.random.randint(part_keys[1], (SCEN, N_LANE, N_DEP, SLOTS), 0, ROW_TILES), jax.random.fold_in(part_keys[1], 1), 0, ROW_TILES - 1).astype(jnp.int32)
    col_index = with_ends(jax.random.randint(part_keys[2], (SCEN, N_LANE, N_DEP, SLOTS), 0, COL_TILES), jax.random.fold_in(part_keys[2], 1), 0, COL_TILES - 1).astype(jnp.int32)
    tile_count = draw_tile_count(jax.random.fold_in(jax.random.fold_in(key_of[9], part), 71), part)
    demand = draw_demand(jax.random.fold_in(jax.random.fold_in(key_of[9], part), 71), part)
    root_cost = jnp.clip(-1.0 + 1.5 * jax.random.uniform(part_keys[5], (COLS,), jnp.float32) ** levels(part_keys[5], (COLS,), ((0, 2),), -0.2, 0.2), -1.0, 0.5)
    branch_cost = jnp.clip(-0.8 + 1.2 * jax.random.uniform(part_keys[6], (SCEN, COLS), jnp.float32) ** levels(part_keys[6], (SCEN, COLS), ((0, 8), (1, 2)), -0.2, 0.2), -0.8, 0.4)
    dispatch_cost = jnp.clip(-0.6 + 0.90000004 * jax.random.uniform(part_keys[7], (SCEN, COLS), jnp.float32) ** levels(part_keys[7], (SCEN, COLS), ((0, 8), (1, 2)), -0.2, 0.2), -0.6, 0.3)
    branch_of = draw_branch_of(jax.random.fold_in(jax.random.fold_in(key_of[9], part), 71), part)
    return dict(tiles=tiles, row_index=row_index, col_index=col_index, tile_count=tile_count, demand=demand, root_cost=root_cost, branch_cost=branch_cost, dispatch_cost=dispatch_cost, branch_of=branch_of)


step_scale = 0.2
penalty = 1.0
epsilon = 1e-06

def reweigh(weight_ratio, primal_moves, dual_moves):
    primal_rate = primal_moves / (3.0 * COLS)
    dual_rate = dual_moves / (LANES + 2.0 * COLS)
    target = jnp.sqrt((primal_rate + epsilon) / (dual_rate + epsilon))
    return jnp.sqrt(weight_ratio * target)

def reference(tiles, row_index, col_index, tile_count, demand, root_cost, branch_cost, dispatch_cost, branch_of):
    col_blocks = DEP_DEV * TYPES // TILE
    highest = lax.Precision.HIGHEST
    live_mask = (jnp.arange(SLOTS, dtype=jnp.int32) < tile_count[..., None]).astype(jnp.float32)
    row_table = (row_index[..., None] == jnp.arange(ROW_TILES, dtype=jnp.int32)).astype(jnp.float32) * live_mask[..., None]
    col_table = (col_index[..., None] == jnp.arange(col_blocks, dtype=jnp.int32)).astype(jnp.float32) * live_mask[..., None]

    def forward(extrap):
        shaped = extrap.reshape(SCEN, N_DEP, col_blocks, TILE)

        def per_scenario(items):
            blocks, col_ids, row_tab, values = items
            picked = values[jnp.arange(N_DEP)[None, :, None], col_ids]
            products = jnp.einsum('ldnij,ldnj->ldni', blocks.astype(jnp.float32), picked.astype(jnp.float32), precision=highest)
            return jnp.einsum('ldnr,ldni->lri', row_tab, products, precision=highest).reshape(LANES)
        return lax.map(per_scenario, (tiles, col_index, row_table, shaped))

    def backward(duals):
        shaped = duals.reshape(SCEN, N_LANE, ROW_TILES, TILE)

        def per_scenario(items):
            blocks, row_ids, col_tab, values = items
            picked = values[jnp.arange(N_LANE)[:, None, None], row_ids]
            products = jnp.einsum('ldnij,ldni->ldnj', blocks.astype(jnp.float32), picked.astype(jnp.float32), precision=highest)
            return jnp.einsum('ldnc,ldnj->dcj', col_tab, products, precision=highest).reshape(COLS)
        return lax.map(per_scenario, (tiles, row_index, col_table, shaped))
    zeros_cols = jnp.zeros((SCEN, COLS), jnp.float32)
    fleet_plan = zeros_cols
    assign_plan = zeros_cols
    dispatch_plan = zeros_cols
    fleet_dual = zeros_cols
    assign_dual = zeros_cols
    fleet_price = zeros_cols
    assign_price = zeros_cols
    assign_mean = zeros_cols
    fleet_mean = jnp.zeros((COLS,), jnp.float32)
    cover_dual = jnp.zeros((SCEN, LANES), jnp.float32)
    weight_ratio = jnp.ones((SCEN,), jnp.float32)
    branch_table = (branch_of[:, None] == jnp.arange(BRANCHES, dtype=jnp.int32)).astype(jnp.float32)
    for hedge_round in range(ITERS):
        penalty_now = 0.0 if hedge_round == 0 else penalty
        for inner_step in range(STEPS):
            closing = hedge_round == ITERS - 1 and inner_step == STEPS - 1
            pulled = backward(cover_dual.astype(jnp.bfloat16))
            primal_step = step_scale / weight_ratio[:, None]
            dual_step = step_scale * weight_ratio[:, None]
            fleet_new = jnp.maximum(0.0, fleet_plan - primal_step * (root_cost[None, :] + fleet_price + penalty_now * (fleet_plan - fleet_mean[None, :]) - fleet_dual))
            assign_new = jnp.maximum(0.0, assign_plan - primal_step * (branch_cost + assign_price + penalty_now * (assign_plan - assign_mean) + fleet_dual - assign_dual))
            dispatch_new = jnp.maximum(0.0, dispatch_plan - primal_step * (dispatch_cost + assign_dual - pulled))
            fleet_ext = 2.0 * fleet_new - fleet_plan
            assign_ext = 2.0 * assign_new - assign_plan
            dispatch_ext = 2.0 * dispatch_new - dispatch_plan
            assign_dual_new = jnp.maximum(0.0, assign_dual + dual_step * (dispatch_ext - assign_ext))
            fleet_dual_new = jnp.maximum(0.0, fleet_dual + dual_step * (assign_ext - fleet_ext))
            lane_load = forward(dispatch_ext.astype(jnp.bfloat16))
            cover_new = jnp.maximum(0.0, cover_dual + dual_step * (demand - lane_load))
            if not closing:
                primal_moves = lax.optimization_barrier(jnp.sum((fleet_new - fleet_plan) ** 2 + (assign_new - assign_plan) ** 2 + (dispatch_new - dispatch_plan) ** 2, axis=1))
                dual_moves = lax.optimization_barrier(jnp.sum((cover_new - cover_dual) ** 2, axis=1)) + lax.optimization_barrier(jnp.sum((assign_dual_new - assign_dual) ** 2 + (fleet_dual_new - fleet_dual) ** 2, axis=1))
                weight_ratio = reweigh(weight_ratio, primal_moves, dual_moves)
            fleet_plan, assign_plan, dispatch_plan = (fleet_new, assign_new, dispatch_new)
            fleet_dual, assign_dual, cover_dual = (fleet_dual_new, assign_dual_new, cover_new)
        fleet_mean = lax.optimization_barrier(jnp.sum(fleet_plan, axis=0)) / SCEN
        branch_means = jnp.dot(branch_table.T, assign_plan, precision=highest) / (SCEN // BRANCHES)
        assign_mean = jnp.dot(branch_table, branch_means, precision=highest)
        fleet_price = fleet_price + penalty * (fleet_plan - fleet_mean[None, :])
        assign_price = assign_price + penalty * (assign_plan - assign_mean)
    return (fleet_plan, assign_plan, dispatch_plan, cover_dual, fleet_price, assign_price)
```

```python
import functools

import jax
import jax.numpy as jnp
from jax import lax
from jax.experimental import pallas as pl
from jax.experimental.pallas import tpu as pltpu
from jax.sharding import PartitionSpec as P

BRANCHES = 8
ITERS = 2
STEPS = 4


step_scale = 0.2
penalty = 1.0
epsilon = 1e-06


def reweigh(weight_ratio, totals, col_total, lane_total):
    primal_rate = totals[:, 0] / (3.0 * col_total)
    dual_rate = totals[:, 1] / (lane_total + 2.0 * col_total)
    target = jnp.sqrt((primal_rate + epsilon) / (dual_rate + epsilon))
    return jnp.sqrt(weight_ratio * target)


def pick_rows(source, places):
    return source[places]


def local(
    tiles,
    row_index,
    col_index,
    tile_count,
    demand,
    root_cost,
    branch_cost,
    dispatch_cost,
    branch_of,
):
    highest = lax.Precision.HIGHEST
    scen_here = tiles.shape[0]
    slots = tiles.shape[3]
    tile_size = tiles.shape[5]
    blocks = tiles.reshape(scen_here, slots, tile_size, tile_size)
    row_ids = row_index.reshape(scen_here, slots)
    col_ids = col_index.reshape(scen_here, slots)
    live_count = tile_count.reshape(scen_here)
    width = root_cost.shape[0]
    lane_rows = demand.shape[1]
    col_blocks = width // tile_size
    row_blocks = lane_rows // tile_size
    lane_count = lax.axis_size("lane")
    col_total = float(width * lax.axis_size("dep"))
    lane_total = float(lane_rows * lane_count)
    slot_iota = lax.broadcasted_iota(jnp.int32, (scen_here, slots), 1)
    live_mask = (slot_iota < live_count[:, None]).astype(jnp.float32)
    row_table = (row_ids[:, :, None] == jnp.arange(row_blocks, dtype=jnp.int32)).astype(
        jnp.float32
    ) * live_mask[:, :, None]
    col_table = (col_ids[:, :, None] == jnp.arange(col_blocks, dtype=jnp.int32)).astype(
        jnp.float32
    ) * live_mask[:, :, None]
    single_copy = (lax.axis_index("lane") == 0).astype(jnp.float32)
    dep_first = (lax.axis_index("dep") == 0).astype(jnp.float32)
    zeros_cols = jnp.zeros((scen_here, width), jnp.float32)
    fleet_plan = zeros_cols
    assign_plan = zeros_cols
    dispatch_plan = zeros_cols
    fleet_dual = zeros_cols
    assign_dual = zeros_cols
    fleet_price = zeros_cols
    assign_price = zeros_cols
    assign_mean = zeros_cols
    fleet_mean = jnp.zeros((width,), jnp.float32)
    cover_dual = jnp.zeros((scen_here, lane_rows), jnp.float32)
    weight_ratio = jnp.ones((scen_here,), jnp.float32)
    branch_table = (branch_of[:, None] == jnp.arange(BRANCHES, dtype=jnp.int32)).astype(jnp.float32)
    total_scen = scen_here * lax.axis_size("scen")
    per_branch = total_scen // BRANCHES
    for hedge_round in range(ITERS):
        penalty_now = 0.0 if hedge_round == 0 else penalty
        for inner_step in range(STEPS):
            closing = hedge_round == ITERS - 1 and inner_step == STEPS - 1
            picked = jax.vmap(pick_rows)(
                cover_dual.astype(jnp.bfloat16).reshape(scen_here, row_blocks, tile_size), row_ids
            )
            products = jnp.einsum(
                "snij,sni->snj", blocks, picked, preferred_element_type=jnp.float32
            )
            partial_value = jnp.einsum(
                "snc,snj->scj", col_table, products, precision=highest
            ).reshape(scen_here, width)
            pulled = lax.psum(partial_value, "lane")
            primal_step = step_scale / weight_ratio[:, None]
            dual_step = step_scale * weight_ratio[:, None]
            fleet_new = jnp.maximum(
                0.0,
                fleet_plan
                - primal_step
                * (
                    root_cost[None, :]
                    + fleet_price
                    + penalty_now * (fleet_plan - fleet_mean[None, :])
                    - fleet_dual
                ),
            )
            assign_new = jnp.maximum(
                0.0,
                assign_plan
                - primal_step
                * (
                    branch_cost
                    + assign_price
                    + penalty_now * (assign_plan - assign_mean)
                    + fleet_dual
                    - assign_dual
                ),
            )
            dispatch_new = jnp.maximum(
                0.0, dispatch_plan - primal_step * (dispatch_cost + assign_dual - pulled)
            )
            fleet_ext = 2.0 * fleet_new - fleet_plan
            assign_ext = 2.0 * assign_new - assign_plan
            dispatch_ext = 2.0 * dispatch_new - dispatch_plan
            assign_dual_new = jnp.maximum(
                0.0, assign_dual + dual_step * (dispatch_ext - assign_ext)
            )
            fleet_dual_new = jnp.maximum(0.0, fleet_dual + dual_step * (assign_ext - fleet_ext))
            extrap_bf = dispatch_ext.astype(jnp.bfloat16)
            forward_picked = jax.vmap(pick_rows)(
                extrap_bf.reshape(scen_here, col_blocks, tile_size), col_ids
            )
            forward_products = jnp.einsum(
                "snij,snj->sni", blocks, forward_picked, preferred_element_type=jnp.float32
            )
            load_part = jnp.einsum(
                "snr,sni->sri", row_table, forward_products, precision=highest
            ).reshape(scen_here, lane_rows)
            primal_moves = single_copy * jnp.sum(
                (fleet_new - fleet_plan) ** 2
                + (assign_new - assign_plan) ** 2
                + (dispatch_new - dispatch_plan) ** 2,
                axis=1,
            )
            pair_moves = single_copy * jnp.sum(
                (assign_dual_new - assign_dual) ** 2 + (fleet_dual_new - fleet_dual) ** 2, axis=1
            )
            lane_load = lax.psum(load_part, "dep")
            cover_new = jnp.maximum(0.0, cover_dual + dual_step * (demand - lane_load))
            cover_moves = jnp.sum((cover_new - cover_dual) ** 2, axis=1)
            if not closing:
                totals = lax.psum(
                    jnp.stack([primal_moves, pair_moves + dep_first * cover_moves], axis=1),
                    ("lane", "dep"),
                )
                weight_ratio = reweigh(weight_ratio, totals, col_total, lane_total)
            fleet_plan, assign_plan, dispatch_plan = (fleet_new, assign_new, dispatch_new)
            fleet_dual, assign_dual, cover_dual = (fleet_dual_new, assign_dual_new, cover_new)
        root_local = jnp.sum(fleet_plan, axis=0)
        branch_local = jnp.dot(branch_table.T, assign_plan, precision=highest)
        root_total, branch_total = lax.psum((root_local, branch_local), "scen")
        fleet_mean = root_total / total_scen
        branch_means = branch_total / per_branch
        assign_mean = jnp.dot(branch_table, branch_means, precision=highest)
        fleet_price = fleet_price + penalty * (fleet_plan - fleet_mean[None, :])
        assign_price = assign_price + penalty * (assign_plan - assign_mean)
    return (fleet_plan, assign_plan, dispatch_plan, cover_dual, fleet_price, assign_price)


MESH = pl.DeviceIdType.MESH


def dot(a, b):
    return jnp.dot(a, b, preferred_element_type=jnp.float32)


def dot_t(a, b):
    return lax.dot_general(a, b, (((1,), (1,)), ((), ())), preferred_element_type=jnp.float32)


def total(x):
    return jnp.sum(x, axis=(0, 1), keepdims=True)


def fused(
    n_scen,
    tiles,
    row_index,
    col_index,
    tile_count,
    demand,
    root_cost,
    branch_cost,
    dispatch_cost,
    branch_of,
    fleet_out,
    assign_out,
    dispatch_out,
    cover_out,
    fleet_price_out,
    assign_price_out,
    blocks,
    costs_out,
    costs,
    ids_out,
    ids_in,
    cover_rows,
    dispatch_rows,
    gather_out,
    gather_in,
    reply_out,
    reply_in,
    early_out,
    early_in,
    late_out,
    late_in,
    local_sem,
    pair_send,
    pair_recv,
    group_send,
    group_recv,
):
    here = lax.axis_index("dep")
    other = 1 - here
    chip = lax.axis_index("scen")
    me = 2 * chip + here
    members = 2 * n_scen
    slots = tiles.shape[1]
    tile = tiles.shape[2]
    lane_rows = demand.shape[1]
    width = branch_cost.shape[1]
    row_blocks = lane_rows // tile
    col_blocks = width // tile
    col_total = float(2 * width)
    lane_total = float(lane_rows)
    total_scen = float(members)
    per_branch = float(members // BRANCHES)

    def member(k):
        to = lax.rem(me + k, members)
        return to, {"scen": to // 2, "dep": lax.rem(to, 2)}

    barrier = pltpu.get_barrier_semaphore()
    for k in range(1, members):
        _, device = member(k)
        pl.semaphore_signal(barrier, inc=1, device_id=device, device_id_type=MESH)

    own_tiles = pltpu.make_async_copy(tiles.at[here], blocks.at[0], local_sem)
    own_tiles.start()

    def put_rows(own, far, source):
        for c in range(source.shape[1] // tile):
            row_0 = source[0:1, c * tile : (c + 1) * tile]
            row_1 = source[1:2, c * tile : (c + 1) * tile]
            own[c : c + 1, :] = jnp.where(here == 0, row_0, row_1)
            if far is not None:
                far[c : c + 1, :] = jnp.where(here == 0, row_1, row_0)

    put_rows(costs.at[0, 0], costs_out.at[0], branch_cost)
    put_rows(costs.at[0, 1], costs_out.at[1], dispatch_cost)
    costs_out[2] = root_cost[...]
    costs[0, 2] = root_cost[...]
    for j in range(slots):
        ids_out[j] = row_index[other, 0, 0, j]
        ids_out[slots + j] = col_index[other, 0, 0, j]
    ids_out[2 * slots] = tile_count[other, 0, 0]

    def pair(source, target, at):
        return pltpu.make_async_remote_copy(
            src_ref=source,
            dst_ref=target,
            send_sem=pair_send.at[at],
            recv_sem=pair_recv.at[at],
            device_id={"dep": other},
            device_id_type=MESH,
        )

    pl.semaphore_wait(barrier, members - 1)
    ids_copy = pair(ids_out, ids_in, 0)
    ids_copy.start()
    costs_copy = pair(costs_out, costs.at[1], 1)
    costs_copy.start()
    tiles_copy = pair(tiles.at[other], blocks.at[1], 2)
    tiles_copy.start()

    put_rows(cover_rows, None, demand)
    demand_here = cover_rows[...]

    row_ids, col_ids, row_marks, col_marks = [], [], [], []

    def take_ids(row_of, col_of, count):
        for j in range(slots):
            row, col = row_of(j), col_of(j)
            row_ids.append(row)
            col_ids.append(col)
            row_marks.append(jnp.where(j < count, row, -1))
            col_marks.append(jnp.where(j < count, col, -1))

    take_ids(
        lambda j: row_index[here, 0, 0, j],
        lambda j: col_index[here, 0, 0, j],
        tile_count[here, 0, 0],
    )
    ids_copy.wait()
    take_ids(lambda j: ids_in[j], lambda j: ids_in[slots + j], ids_in[2 * slots])

    lane_iota = lax.broadcasted_iota(jnp.int32, (row_blocks, tile), 0)
    col_iota = lax.broadcasted_iota(jnp.int32, (col_blocks, tile), 0)

    def spread(row, iota, mark):
        return jnp.where(iota == mark, jnp.broadcast_to(row, iota.shape), 0.0).astype(jnp.bfloat16)

    def backward(cover):
        cover_rows[...] = cover
        halves = []
        for half in range(2):
            acc = None
            for j in range(slots):
                n = half * slots + j
                row = cover_rows[pl.ds(row_ids[n], 1), :]
                part = dot(spread(row, col_iota, col_marks[n]), blocks[half, j])
                acc = part if acc is None else acc + part
            halves.append(acc)
        return jnp.concatenate(halves, axis=0)

    def forward(extrap):
        dispatch_rows[...] = extrap
        acc = None
        for half in range(2):
            for j in range(slots):
                n = half * slots + j
                row = dispatch_rows[pl.ds(half * col_blocks + col_ids[n], 1), :]
                part = dot_t(spread(row, lane_iota, row_marks[n]), blocks[half, j])
                acc = part if acc is None else acc + part
        return acc

    def group(source, target, k, at):
        to, device = member(k)
        return pltpu.make_async_remote_copy(
            src_ref=source.at[pl.ds(pl.multiple_of(8 * to, 8), 8)],
            dst_ref=target.at[pl.ds(pl.multiple_of(8 * me, 8), 8)],
            send_sem=group_send.at[at],
            recv_sem=group_recv.at[at],
            device_id=device,
            device_id_type=MESH,
        )

    def group_start(source, target, at):
        for k in range(1, members):
            group(source, target, k, at).start()
        mine = pl.ds(pl.multiple_of(8 * me, 8), 8)
        target[mine, :] = source[mine, :]

    def group_all(source, target, at):
        part = pl.ds(0, 8 * (members - 1))
        return pltpu.make_async_remote_copy(
            src_ref=source.at[part],
            dst_ref=target.at[part],
            send_sem=group_send.at[at],
            recv_sem=group_recv.at[at],
            device_id={"dep": other},
            device_id_type=MESH,
        )

    def in_order(x):
        own, far = x[:col_blocks], x[col_blocks:]
        first = here == 0
        return jnp.where(first, own, far), jnp.where(first, far, own)

    def kind(k):
        return pl.ds(k, members, stride=8)

    def gather_start(hedge_round, fleet, assign):
        buffer = gather_out.at[hedge_round]
        values = in_order(fleet) + in_order(assign)
        for k, value in enumerate(values):
            buffer[kind(k), :] = value
        branch = branch_of[here].astype(jnp.float32)
        buffer[kind(4), :] = jnp.full((members, tile), branch, jnp.float32)
        for k in range(5, 8):
            buffer[kind(k), :] = jnp.zeros((members, tile), jnp.float32)
        group_start(buffer, gather_in.at[hedge_round], hedge_round)

    def reply_start(hedge_round):
        group_all(gather_out.at[hedge_round], gather_in.at[hedge_round], hedge_round).wait_recv()
        buffer = gather_in.at[hedge_round]
        lanes = lax.broadcasted_iota(jnp.int32, (members, tile), 1).astype(jnp.float32)
        hot = (buffer[kind(4), :] == lanes).astype(jnp.bfloat16)
        same = dot_t(hot, hot).astype(jnp.bfloat16)
        parts = []
        for k in (2, 3):
            value = buffer[kind(k), :]
            high = value.astype(jnp.bfloat16)
            rest = value - high.astype(jnp.float32)
            middle = rest.astype(jnp.bfloat16)
            low = (rest - middle.astype(jnp.float32)).astype(jnp.bfloat16)
            parts += [high, middle, low]
        sums = dot(same, jnp.concatenate(parts, axis=1))
        pieces = [sums[:, i * tile : (i + 1) * tile] for i in range(6)]
        mean_0 = ((pieces[2] + pieces[1]) + pieces[0]) / per_branch
        mean_1 = ((pieces[5] + pieces[4]) + pieces[3]) / per_branch
        fleet_0, fleet_1 = (
            jnp.broadcast_to(
                jnp.sum(buffer[kind(k), :], axis=0, keepdims=True) / total_scen, (members, tile)
            )
            for k in (0, 1)
        )
        if hedge_round < ITERS - 1:
            values = [fleet_0, fleet_1, mean_0, mean_1]
        else:
            even = lax.rem(lax.broadcasted_iota(jnp.int32, (members, tile), 0), 2) == 0
            down = jnp.concatenate([mean_1[-1:], mean_1[:-1]], axis=0)
            up = jnp.concatenate([mean_0[1:], mean_0[:1]], axis=0)
            values = [
                jnp.where(even, fleet_0, fleet_1),
                jnp.where(even, mean_0, down),
                jnp.where(even, up, mean_1),
            ]
        out = reply_out.at[hedge_round]
        for k in range(8):
            out[kind(k), :] = values[k] if k < len(values) else jnp.zeros((members, tile), jnp.float32)
        group_start(out, reply_in.at[hedge_round], ITERS + hedge_round)

    def reply_wait(hedge_round):
        group_all(reply_out.at[hedge_round], reply_in.at[hedge_round], ITERS + hedge_round).wait_recv()

    zeros = jnp.zeros((2 * col_blocks, tile), jnp.float32)
    fleet = assign = dispatch = fleet_dual = assign_dual = fleet_price = assign_price = zeros
    fleet_mean = assign_mean = zeros
    cover = jnp.zeros((row_blocks, tile), jnp.float32)
    ratio = jnp.ones((1, 1), jnp.float32)
    costs_copy.wait()
    branch_c = jnp.concatenate([costs[0, 0], costs[1, 0]], axis=0)
    dispatch_c = jnp.concatenate([costs[0, 1], costs[1, 1]], axis=0)
    root_c = jnp.concatenate([costs[0, 2], costs[1, 2]], axis=0)
    own_tiles.wait()
    tiles_copy.wait()

    for hedge_round in range(ITERS):
        penalty_now = 0.0 if hedge_round == 0 else penalty
        for inner_step in range(STEPS):
            ends = inner_step == STEPS - 1
            closing = hedge_round == ITERS - 1 and ends
            waits = hedge_round > 0 and inner_step == 0
            primal_step = step_scale / ratio
            dual_step = step_scale * ratio

            def plans():
                pull_f = root_c + fleet_price - fleet_dual
                pull_a = branch_c + assign_price + fleet_dual - assign_dual
                if penalty_now:
                    pull_f = pull_f + penalty_now * (fleet - fleet_mean)
                    pull_a = pull_a + penalty_now * (assign - assign_mean)
                return (
                    jnp.maximum(0.0, fleet - primal_step * pull_f),
                    jnp.maximum(0.0, assign - primal_step * pull_a),
                )

            if not waits:
                fleet_new, assign_new = plans()
            if ends:
                gather_start(hedge_round, fleet_new, assign_new)
            if closing:
                for k, x in enumerate((fleet_new, assign_new, fleet_price, assign_price)):
                    early_out[k] = x[col_blocks:]
                early_copy = pair(early_out, early_in, 3)
                early_copy.start()
            first = hedge_round == 0 and inner_step == 0
            pulled = zeros if first else backward(cover)
            dispatch_new = jnp.maximum(0.0, dispatch - primal_step * (dispatch_c + assign_dual - pulled))
            dispatch_ext = 2.0 * dispatch_new - dispatch
            load = forward(dispatch_ext)
            cover_new = jnp.maximum(0.0, cover + dual_step * (demand_here - load))
            if closing:
                late_out[0] = dispatch_new[col_blocks:]
                late_out[1] = cover_new
                late_copy = pair(late_out, late_in, 4)
                late_copy.start()
            if waits:
                reply_wait(hedge_round - 1)
                back = reply_in.at[hedge_round - 1]
                fleet_mean = jnp.concatenate(in_order(jnp.concatenate([back[kind(0), :], back[kind(1), :]], axis=0)), axis=0)
                assign_mean = jnp.concatenate(in_order(jnp.concatenate([back[kind(2), :], back[kind(3), :]], axis=0)), axis=0)
                fleet_price = fleet_price + penalty * (fleet - fleet_mean)
                assign_price = assign_price + penalty * (assign - assign_mean)
                fleet_new, assign_new = plans()
            if not closing:
                fleet_ext = 2.0 * fleet_new - fleet
                assign_ext = 2.0 * assign_new - assign
                assign_dual_new = jnp.maximum(0.0, assign_dual + dual_step * (dispatch_ext - assign_ext))
                fleet_dual_new = jnp.maximum(0.0, fleet_dual + dual_step * (assign_ext - fleet_ext))
                primal_moves = total(
                    (fleet_new - fleet) ** 2 + (assign_new - assign) ** 2 + (dispatch_new - dispatch) ** 2
                )
                pair_moves = total((assign_dual_new - assign_dual) ** 2 + (fleet_dual_new - fleet_dual) ** 2)
                cover_moves = total((cover_new - cover) ** 2)
                primal_rate = primal_moves / (3.0 * col_total)
                dual_rate = (cover_moves + pair_moves) / (lane_total + 2.0 * col_total)
                target = jnp.sqrt((primal_rate + epsilon) / (dual_rate + epsilon))
                ratio = jnp.sqrt(ratio * target)
                fleet_dual, assign_dual = fleet_dual_new, assign_dual_new
            fleet, assign, dispatch, cover = fleet_new, assign_new, dispatch_new, cover_new
            if ends:
                reply_start(hedge_round)

    def put_out(ref, own, far):
        row_0, row_1 = jnp.where(here == 0, own, far), jnp.where(here == 0, far, own)
        for c in range(own.shape[0]):
            ref[0:1, c * tile : (c + 1) * tile] = row_0[c : c + 1]
            ref[1:2, c * tile : (c + 1) * tile] = row_1[c : c + 1]

    early_copy.wait()
    put_out(fleet_out, fleet[:col_blocks], early_in[0])
    put_out(assign_out, assign[:col_blocks], early_in[1])
    late_copy.wait()
    put_out(dispatch_out, dispatch[:col_blocks], late_in[0])
    put_out(cover_out, cover, late_in[1])
    reply_wait(ITERS - 1)
    back = reply_in.at[ITERS - 1]
    last_fleet = back[kind(0), :]
    even_mean, odd_mean = back[kind(1), :], back[kind(2), :]
    own_mean = jnp.where(here == 0, even_mean, odd_mean)
    far_mean = jnp.where(here == 0, odd_mean, even_mean)
    put_out(
        fleet_price_out,
        fleet_price[:col_blocks] + penalty * (fleet[:col_blocks] - last_fleet),
        early_in[2] + penalty * (early_in[0] - last_fleet),
    )
    put_out(
        assign_price_out,
        assign_price[:col_blocks] + penalty * (assign[:col_blocks] - own_mean),
        early_in[3] + penalty * (early_in[1] - far_mean),
    )
    for r in range(ITERS):
        group_all(gather_out.at[r], gather_in.at[r], r).wait_send()
        group_all(reply_out.at[r], reply_in.at[r], ITERS + r).wait_send()


def fused_local(
    n_scen,
    tiles,
    row_index,
    col_index,
    tile_count,
    demand,
    root_cost,
    branch_cost,
    dispatch_cost,
    branch_of,
):
    slots, tile = tiles.shape[3], tiles.shape[5]
    lane_rows, width = demand.shape[1], branch_cost.shape[1]
    rows, cols, members = lane_rows // tile, width // tile, 2 * n_scen
    f32 = jnp.float32
    vmem = pl.BlockSpec(memory_space=pltpu.VMEM)
    smem = pl.BlockSpec(memory_space=pltpu.SMEM)
    col_shape = jax.ShapeDtypeStruct((2, width), f32)
    lane_shape = jax.ShapeDtypeStruct((2, lane_rows), f32)
    return pl.pallas_call(
        functools.partial(fused, n_scen),
        out_shape=(col_shape, col_shape, col_shape, lane_shape, col_shape, col_shape),
        in_specs=[pl.BlockSpec(memory_space=pl.ANY), smem, smem, smem, vmem, vmem, vmem, vmem, smem],
        out_specs=(vmem,) * 6,
        scratch_shapes=[
            pltpu.VMEM((2, slots, tile, tile), jnp.bfloat16),
            pltpu.VMEM((3, cols, tile), f32),
            pltpu.VMEM((2, 3, cols, tile), f32),
            pltpu.SMEM((4 * slots,), jnp.int32),
            pltpu.SMEM((4 * slots,), jnp.int32),
            pltpu.VMEM((rows, tile), f32),
            pltpu.VMEM((2 * cols, tile), f32),
            pltpu.VMEM((ITERS, 8 * members, tile), f32),
            pltpu.VMEM((ITERS, 8 * members, tile), f32),
            pltpu.VMEM((ITERS, 8 * members, tile), f32),
            pltpu.VMEM((ITERS, 8 * members, tile), f32),
            pltpu.VMEM((4, cols, tile), f32),
            pltpu.VMEM((4, cols, tile), f32),
            pltpu.VMEM((2, cols, tile), f32),
            pltpu.VMEM((2, cols, tile), f32),
            pltpu.SemaphoreType.DMA,
            pltpu.SemaphoreType.DMA((5,)),
            pltpu.SemaphoreType.DMA((5,)),
            pltpu.SemaphoreType.DMA((2 * ITERS,)),
            pltpu.SemaphoreType.DMA((2 * ITERS,)),
        ],
        compiler_params=pltpu.CompilerParams(
            collective_id=0, has_side_effects=True, vmem_limit_bytes=16 * 1024 * 1024
        ),
    )(
        tiles.reshape(2, slots, tile, tile),
        row_index,
        col_index,
        tile_count,
        demand,
        root_cost.reshape(cols, tile),
        branch_cost,
        dispatch_cost,
        branch_of,
    )


def solution_body(mesh):
    n_scen = mesh.shape["scen"]
    fits = mesh.shape["lane"] == 1 and mesh.shape["dep"] == 2 and (2 * n_scen) % BRANCHES == 0

    def body(*args):
        tiles, demand, root_cost = args[0], args[4], args[5]
        tile = tiles.shape[5]
        cols, rows = root_cost.shape[0] // tile, demand.shape[1] // tile
        if fits and tiles.shape[0] == 2 and tile == 128 and cols == rows == 2 * n_scen and cols % 8 == 0:
            return fused_local(n_scen, *args)
        return local(*args)

    return body


def solution(mesh):
    in_specs = (
        P(("groups", "scen"), "lane", "dep", None, None, None),
        P(("groups", "scen"), "lane", "dep", None),
        P(("groups", "scen"), "lane", "dep", None),
        P(("groups", "scen"), "lane", "dep"),
        P(("groups", "scen"), "lane"),
        P(("groups", "dep")),
        P(("groups", "scen"), "dep"),
        P(("groups", "scen"), "dep"),
        P(("groups", "scen")),
    )
    out_specs = (
        P(("groups", "scen"), "dep"),
        P(("groups", "scen"), "dep"),
        P(("groups", "scen"), "dep"),
        P(("groups", "scen"), "lane"),
        P(("groups", "scen"), "dep"),
        P(("groups", "scen"), "dep"),
    )
    body = solution_body(mesh)
    return jax.shard_map(body, mesh=mesh, in_specs=in_specs, out_specs=out_specs, check_vma=False)
```

```python
import functools

import jax
import jax.numpy as jnp
from jax import lax
from jax.experimental import pallas as pl
from jax.experimental.pallas import tpu as pltpu
from jax.sharding import PartitionSpec as P

BRANCHES = 8
ITERS = 2
STEPS = 4


step_scale = 0.2
penalty = 1.0
epsilon = 1e-06


def reweigh(weight_ratio, totals, col_total, lane_total):
    primal_rate = totals[:, 0] / (3.0 * col_total)
    dual_rate = totals[:, 1] / (lane_total + 2.0 * col_total)
    target = jnp.sqrt((primal_rate + epsilon) / (dual_rate + epsilon))
    return jnp.sqrt(weight_ratio * target)


def pick_rows(source, places):
    return source[places]


def local(
    tiles,
    row_index,
    col_index,
    tile_count,
    demand,
    root_cost,
    branch_cost,
    dispatch_cost,
    branch_of,
):
    highest = lax.Precision.HIGHEST
    scen_here = tiles.shape[0]
    slots = tiles.shape[3]
    tile_size = tiles.shape[5]
    blocks = tiles.reshape(scen_here, slots, tile_size, tile_size)
    row_ids = row_index.reshape(scen_here, slots)
    col_ids = col_index.reshape(scen_here, slots)
    live_count = tile_count.reshape(scen_here)
    width = root_cost.shape[0]
    lane_rows = demand.shape[1]
    col_blocks = width // tile_size
    row_blocks = lane_rows // tile_size
    lane_count = lax.axis_size("lane")
    col_total = float(width * lax.axis_size("dep"))
    lane_total = float(lane_rows * lane_count)
    slot_iota = lax.broadcasted_iota(jnp.int32, (scen_here, slots), 1)
    live_mask = (slot_iota < live_count[:, None]).astype(jnp.float32)
    row_table = (row_ids[:, :, None] == jnp.arange(row_blocks, dtype=jnp.int32)).astype(
        jnp.float32
    ) * live_mask[:, :, None]
    col_table = (col_ids[:, :, None] == jnp.arange(col_blocks, dtype=jnp.int32)).astype(
        jnp.float32
    ) * live_mask[:, :, None]
    single_copy = (lax.axis_index("lane") == 0).astype(jnp.float32)
    dep_first = (lax.axis_index("dep") == 0).astype(jnp.float32)
    zeros_cols = jnp.zeros((scen_here, width), jnp.float32)
    fleet_plan = zeros_cols
    assign_plan = zeros_cols
    dispatch_plan = zeros_cols
    fleet_dual = zeros_cols
    assign_dual = zeros_cols
    fleet_price = zeros_cols
    assign_price = zeros_cols
    assign_mean = zeros_cols
    fleet_mean = jnp.zeros((width,), jnp.float32)
    cover_dual = jnp.zeros((scen_here, lane_rows), jnp.float32)
    weight_ratio = jnp.ones((scen_here,), jnp.float32)
    branch_table = (branch_of[:, None] == jnp.arange(BRANCHES, dtype=jnp.int32)).astype(jnp.float32)
    total_scen = scen_here * lax.axis_size("scen")
    per_branch = total_scen // BRANCHES
    for hedge_round in range(ITERS):
        penalty_now = 0.0 if hedge_round == 0 else penalty
        for inner_step in range(STEPS):
            closing = hedge_round == ITERS - 1 and inner_step == STEPS - 1
            picked = jax.vmap(pick_rows)(
                cover_dual.astype(jnp.bfloat16).reshape(scen_here, row_blocks, tile_size), row_ids
            )
            products = jnp.einsum(
                "snij,sni->snj", blocks, picked, preferred_element_type=jnp.float32
            )
            partial_value = jnp.einsum(
                "snc,snj->scj", col_table, products, precision=highest
            ).reshape(scen_here, width)
            pulled = lax.psum(partial_value, "lane")
            primal_step = step_scale / weight_ratio[:, None]
            dual_step = step_scale * weight_ratio[:, None]
            fleet_new = jnp.maximum(
                0.0,
                fleet_plan
                - primal_step
                * (
                    root_cost[None, :]
                    + fleet_price
                    + penalty_now * (fleet_plan - fleet_mean[None, :])
                    - fleet_dual
                ),
            )
            assign_new = jnp.maximum(
                0.0,
                assign_plan
                - primal_step
                * (
                    branch_cost
                    + assign_price
                    + penalty_now * (assign_plan - assign_mean)
                    + fleet_dual
                    - assign_dual
                ),
            )
            dispatch_new = jnp.maximum(
                0.0, dispatch_plan - primal_step * (dispatch_cost + assign_dual - pulled)
            )
            fleet_ext = 2.0 * fleet_new - fleet_plan
            assign_ext = 2.0 * assign_new - assign_plan
            dispatch_ext = 2.0 * dispatch_new - dispatch_plan
            assign_dual_new = jnp.maximum(
                0.0, assign_dual + dual_step * (dispatch_ext - assign_ext)
            )
            fleet_dual_new = jnp.maximum(0.0, fleet_dual + dual_step * (assign_ext - fleet_ext))
            extrap_bf = dispatch_ext.astype(jnp.bfloat16)
            forward_picked = jax.vmap(pick_rows)(
                extrap_bf.reshape(scen_here, col_blocks, tile_size), col_ids
            )
            forward_products = jnp.einsum(
                "snij,snj->sni", blocks, forward_picked, preferred_element_type=jnp.float32
            )
            load_part = jnp.einsum(
                "snr,sni->sri", row_table, forward_products, precision=highest
            ).reshape(scen_here, lane_rows)
            primal_moves = single_copy * jnp.sum(
                (fleet_new - fleet_plan) ** 2
                + (assign_new - assign_plan) ** 2
                + (dispatch_new - dispatch_plan) ** 2,
                axis=1,
            )
            pair_moves = single_copy * jnp.sum(
                (assign_dual_new - assign_dual) ** 2 + (fleet_dual_new - fleet_dual) ** 2, axis=1
            )
            lane_load = lax.psum(load_part, "dep")
            cover_new = jnp.maximum(0.0, cover_dual + dual_step * (demand - lane_load))
            cover_moves = jnp.sum((cover_new - cover_dual) ** 2, axis=1)
            if not closing:
                totals = lax.psum(
                    jnp.stack([primal_moves, pair_moves + dep_first * cover_moves], axis=1),
                    ("lane", "dep"),
                )
                weight_ratio = reweigh(weight_ratio, totals, col_total, lane_total)
            fleet_plan, assign_plan, dispatch_plan = (fleet_new, assign_new, dispatch_new)
            fleet_dual, assign_dual, cover_dual = (fleet_dual_new, assign_dual_new, cover_new)
        root_local = jnp.sum(fleet_plan, axis=0)
        branch_local = jnp.dot(branch_table.T, assign_plan, precision=highest)
        root_total, branch_total = lax.psum((root_local, branch_local), "scen")
        fleet_mean = root_total / total_scen
        branch_means = branch_total / per_branch
        assign_mean = jnp.dot(branch_table, branch_means, precision=highest)
        fleet_price = fleet_price + penalty * (fleet_plan - fleet_mean[None, :])
        assign_price = assign_price + penalty * (assign_plan - assign_mean)
    return (fleet_plan, assign_plan, dispatch_plan, cover_dual, fleet_price, assign_price)


MESH = pl.DeviceIdType.MESH


def dot(a, b):
    return jnp.dot(a, b, preferred_element_type=jnp.float32)


def dot_t(a, b):
    return lax.dot_general(a, b, (((1,), (1,)), ((), ())), preferred_element_type=jnp.float32)


def total(x):
    return jnp.sum(x, axis=(0, 1), keepdims=True)


def fused(
    n_scen,
    tiles,
    row_index_in,
    col_index_in,
    tile_count_in,
    demand_in,
    root_cost_in,
    branch_cost_in,
    dispatch_cost_in,
    branch_of_in,
    packed,
    row_index,
    col_index,
    tile_count,
    branch_of,
    demand,
    root_cost,
    branch_cost,
    dispatch_cost,
    blocks,
    flipped,
    costs_out,
    costs,
    ids_out,
    ids_in,
    cover_rows,
    dispatch_rows,
    gather_out,
    gather_in,
    reply_out,
    reply_in,
    early_out,
    early_in,
    late_out,
    late_in,
    local_sem,
    load_sem,
    pair_send,
    pair_recv,
    group_send,
    group_recv,
):
    here = lax.axis_index("dep")
    other = 1 - here
    chip = lax.axis_index("scen")
    me = 2 * chip + here
    members = 2 * n_scen
    slots = tiles.shape[1]
    tile = tiles.shape[2]
    lane_rows = demand.shape[1]
    width = branch_cost.shape[1]
    row_blocks = lane_rows // tile
    col_blocks = width // tile
    col_total = float(2 * width)
    lane_total = float(lane_rows)
    total_scen = float(members)
    per_branch = float(members // BRANCHES)

    def member(k):
        to = lax.rem(me + k, members)
        return to, {"scen": to // 2, "dep": lax.rem(to, 2)}

    def load(source, target, at):
        copy = pltpu.make_async_copy(source, target, load_sem.at[at])
        copy.start()
        return copy

    loads = [
        load(row_index_in, row_index, 0),
        load(col_index_in, col_index, 1),
        load(tile_count_in, tile_count, 2),
        load(branch_cost_in, branch_cost, 3),
        load(dispatch_cost_in, dispatch_cost, 4),
        load(root_cost_in, root_cost, 5),
        load(demand_in, demand, 6),
        load(branch_of_in, branch_of, 7),
    ]
    barrier = pltpu.get_barrier_semaphore()
    for k in range(1, members):
        _, device = member(k)
        pl.semaphore_signal(barrier, inc=1, device_id=device, device_id_type=MESH)

    own_tiles = pltpu.make_async_copy(tiles.at[here], blocks.at[0], local_sem)
    own_tiles.start()

    def put_rows(own, far, source):
        for c in range(source.shape[1] // tile):
            row_0 = source[0:1, c * tile : (c + 1) * tile]
            row_1 = source[1:2, c * tile : (c + 1) * tile]
            own[c : c + 1, :] = jnp.where(here == 0, row_0, row_1)
            if far is not None:
                far[c : c + 1, :] = jnp.where(here == 0, row_1, row_0)

    for copy in loads:
        copy.wait()
    put_rows(costs.at[0, 0], costs_out.at[0], branch_cost)
    put_rows(costs.at[0, 1], costs_out.at[1], dispatch_cost)
    costs_out[2] = root_cost[...]
    costs[0, 2] = root_cost[...]
    for j in range(slots):
        ids_out[j] = row_index[other, 0, 0, j]
        ids_out[slots + j] = col_index[other, 0, 0, j]
    ids_out[2 * slots] = tile_count[other]

    def pair(source, target, at):
        return pltpu.make_async_remote_copy(
            src_ref=source,
            dst_ref=target,
            send_sem=pair_send.at[at],
            recv_sem=pair_recv.at[at],
            device_id={"dep": other},
            device_id_type=MESH,
        )

    pl.semaphore_wait(barrier, members - 1)
    ids_copy = pair(ids_out, ids_in, 0)
    ids_copy.start()
    costs_copy = pair(costs_out, costs.at[1], 1)
    costs_copy.start()
    tiles_copy = pair(tiles.at[other], blocks.at[1], 2)
    tiles_copy.start()

    put_rows(cover_rows, None, demand)
    demand_here = cover_rows[...]

    row_ids, col_ids, row_marks, col_marks = [], [], [], []

    def take_ids(row_of, col_of, count):
        for j in range(slots):
            row, col = row_of(j), col_of(j)
            row_ids.append(row)
            col_ids.append(col)
            row_marks.append(jnp.where(j < count, row, -1))
            col_marks.append(jnp.where(j < count, col, -1))

    take_ids(
        lambda j: row_index[here, 0, 0, j],
        lambda j: col_index[here, 0, 0, j],
        tile_count[here],
    )
    ids_copy.wait()
    take_ids(lambda j: ids_in[j], lambda j: ids_in[slots + j], ids_in[2 * slots])

    lane_iota = lax.broadcasted_iota(jnp.int32, (row_blocks, tile), 0)
    col_iota = lax.broadcasted_iota(jnp.int32, (col_blocks, tile), 0)

    def spread(row, iota, mark):
        return jnp.where(iota == mark, jnp.broadcast_to(row, iota.shape), 0.0).astype(jnp.bfloat16)

    def backward(cover):
        cover_rows[...] = cover
        halves = []
        for half in range(2):
            left = []
            for n in range(half * slots, (half + 1) * slots):
                row = cover_rows[pl.ds(row_ids[n], 1), :]
                left.append(spread(row, col_iota, col_marks[n]))
            halves.append(dot(jnp.concatenate(left, axis=1), blocks[half].reshape(slots * tile, tile)))
        return jnp.concatenate(halves, axis=0)

    def forward(extrap):
        dispatch_rows[...] = extrap
        left = []
        for n in range(2 * slots):
            row = dispatch_rows[pl.ds(n // slots * col_blocks + col_ids[n], 1), :]
            left.append(spread(row, lane_iota, row_marks[n]))
        return dot(jnp.concatenate(left, axis=1), flipped[...].reshape(2 * slots * tile, tile))

    def flip(half):
        for j in range(slots):
            flipped[half, j] = blocks[half, j].T

    def group(source, target, k, at):
        to, device = member(k)
        return pltpu.make_async_remote_copy(
            src_ref=source.at[pl.ds(pl.multiple_of(8 * to, 8), 8)],
            dst_ref=target.at[pl.ds(pl.multiple_of(8 * me, 8), 8)],
            send_sem=group_send.at[at],
            recv_sem=group_recv.at[at],
            device_id=device,
            device_id_type=MESH,
        )

    def group_start(source, target, at):
        for k in range(1, members):
            group(source, target, k, at).start()
        mine = pl.ds(pl.multiple_of(8 * me, 8), 8)
        target[mine, :] = source[mine, :]

    def group_all(source, target, at):
        part = pl.ds(0, 8 * (members - 1))
        return pltpu.make_async_remote_copy(
            src_ref=source.at[part],
            dst_ref=target.at[part],
            send_sem=group_send.at[at],
            recv_sem=group_recv.at[at],
            device_id={"dep": other},
            device_id_type=MESH,
        )

    def in_order(x):
        own, far = x[:col_blocks], x[col_blocks:]
        first = here == 0
        return jnp.where(first, own, far), jnp.where(first, far, own)

    def kind(k):
        return pl.ds(k, members, stride=8)

    def gather_start(hedge_round, fleet, assign):
        buffer = gather_out.at[hedge_round]
        values = in_order(fleet) + in_order(assign)
        for k, value in enumerate(values):
            buffer[kind(k), :] = value
        branch = branch_of[here].astype(jnp.float32)
        buffer[kind(4), :] = jnp.full((members, tile), branch, jnp.float32)
        for k in range(5, 8):
            buffer[kind(k), :] = jnp.zeros((members, tile), jnp.float32)
        group_start(buffer, gather_in.at[hedge_round], hedge_round)

    def reply_start(hedge_round):
        group_all(gather_out.at[hedge_round], gather_in.at[hedge_round], hedge_round).wait_recv()
        buffer = gather_in.at[hedge_round]
        lanes = lax.broadcasted_iota(jnp.int32, (members, tile), 1).astype(jnp.float32)
        hot = (buffer[kind(4), :] == lanes).astype(jnp.bfloat16)
        same = dot_t(hot, hot).astype(jnp.bfloat16)
        parts = []
        for k in (2, 3):
            value = buffer[kind(k), :]
            high = value.astype(jnp.bfloat16)
            rest = value - high.astype(jnp.float32)
            middle = rest.astype(jnp.bfloat16)
            low = (rest - middle.astype(jnp.float32)).astype(jnp.bfloat16)
            parts += [high, middle, low]
        sums = dot(same, jnp.concatenate(parts, axis=1))
        pieces = [sums[:, i * tile : (i + 1) * tile] for i in range(6)]
        mean_0 = ((pieces[2] + pieces[1]) + pieces[0]) / per_branch
        mean_1 = ((pieces[5] + pieces[4]) + pieces[3]) / per_branch
        fleet_0, fleet_1 = (
            jnp.broadcast_to(
                jnp.sum(buffer[kind(k), :], axis=0, keepdims=True) / total_scen, (members, tile)
            )
            for k in (0, 1)
        )
        if hedge_round < ITERS - 1:
            values = [fleet_0, fleet_1, mean_0, mean_1]
        else:
            even = lax.rem(lax.broadcasted_iota(jnp.int32, (members, tile), 0), 2) == 0
            down = jnp.concatenate([mean_1[-1:], mean_1[:-1]], axis=0)
            up = jnp.concatenate([mean_0[1:], mean_0[:1]], axis=0)
            values = [
                jnp.where(even, fleet_0, fleet_1),
                jnp.where(even, mean_0, down),
                jnp.where(even, up, mean_1),
            ]
        out = reply_out.at[hedge_round]
        for k in range(8):
            out[kind(k), :] = values[k] if k < len(values) else jnp.zeros((members, tile), jnp.float32)
        group_start(out, reply_in.at[hedge_round], ITERS + hedge_round)

    def reply_wait(hedge_round):
        group_all(reply_out.at[hedge_round], reply_in.at[hedge_round], ITERS + hedge_round).wait_recv()

    zeros = jnp.zeros((2 * col_blocks, tile), jnp.float32)
    fleet = assign = dispatch = fleet_dual = assign_dual = fleet_price = assign_price = zeros
    fleet_mean = assign_mean = zeros
    cover = jnp.zeros((row_blocks, tile), jnp.float32)
    ratio = jnp.ones((1, 1), jnp.float32)
    costs_copy.wait()
    branch_c = jnp.concatenate([costs[0, 0], costs[1, 0]], axis=0)
    dispatch_c = jnp.concatenate([costs[0, 1], costs[1, 1]], axis=0)
    root_c = jnp.concatenate([costs[0, 2], costs[1, 2]], axis=0)
    own_tiles.wait()
    flip(0)
    tiles_copy.wait()
    flip(1)

    for hedge_round in range(ITERS):
        penalty_now = 0.0 if hedge_round == 0 else penalty
        for inner_step in range(STEPS):
            ends = inner_step == STEPS - 1
            closing = hedge_round == ITERS - 1 and ends
            waits = hedge_round > 0 and inner_step == 0
            primal_step = step_scale / ratio
            dual_step = step_scale * ratio

            def plans():
                pull_f = root_c + fleet_price - fleet_dual
                pull_a = branch_c + assign_price + fleet_dual - assign_dual
                if penalty_now:
                    pull_f = pull_f + penalty_now * (fleet - fleet_mean)
                    pull_a = pull_a + penalty_now * (assign - assign_mean)
                return (
                    jnp.maximum(0.0, fleet - primal_step * pull_f),
                    jnp.maximum(0.0, assign - primal_step * pull_a),
                )

            if not waits:
                fleet_new, assign_new = plans()
            if ends:
                gather_start(hedge_round, fleet_new, assign_new)
            if closing:
                for k, x in enumerate((fleet_new, assign_new, fleet_price, assign_price)):
                    early_out[k] = x[col_blocks:]
                early_copy = pair(early_out, early_in, 3)
                early_copy.start()
            first = hedge_round == 0 and inner_step == 0
            pulled = zeros if first else backward(cover)
            dispatch_new = jnp.maximum(0.0, dispatch - primal_step * (dispatch_c + assign_dual - pulled))
            dispatch_ext = 2.0 * dispatch_new - dispatch
            load = forward(dispatch_ext)
            cover_new = jnp.maximum(0.0, cover + dual_step * (demand_here - load))
            if closing:
                late_out[0] = dispatch_new[col_blocks:]
                late_out[1] = cover_new
                late_copy = pair(late_out, late_in, 4)
                late_copy.start()
            if waits:
                reply_wait(hedge_round - 1)
                back = reply_in.at[hedge_round - 1]
                fleet_mean = jnp.concatenate(in_order(jnp.concatenate([back[kind(0), :], back[kind(1), :]], axis=0)), axis=0)
                assign_mean = jnp.concatenate(in_order(jnp.concatenate([back[kind(2), :], back[kind(3), :]], axis=0)), axis=0)
                fleet_price = fleet_price + penalty * (fleet - fleet_mean)
                assign_price = assign_price + penalty * (assign - assign_mean)
                fleet_new, assign_new = plans()
            if not closing:
                fleet_ext = 2.0 * fleet_new - fleet
                assign_ext = 2.0 * assign_new - assign
                assign_dual_new = jnp.maximum(0.0, assign_dual + dual_step * (dispatch_ext - assign_ext))
                fleet_dual_new = jnp.maximum(0.0, fleet_dual + dual_step * (assign_ext - fleet_ext))
                primal_moves = total(
                    (fleet_new - fleet) ** 2 + (assign_new - assign) ** 2 + (dispatch_new - dispatch) ** 2
                )
                pair_moves = total((assign_dual_new - assign_dual) ** 2 + (fleet_dual_new - fleet_dual) ** 2)
                cover_moves = total((cover_new - cover) ** 2)
                primal_rate = primal_moves / (3.0 * col_total)
                dual_rate = (cover_moves + pair_moves) / (lane_total + 2.0 * col_total)
                target = jnp.sqrt((primal_rate + epsilon) / (dual_rate + epsilon))
                ratio = jnp.sqrt(ratio * target)
                fleet_dual, assign_dual = fleet_dual_new, assign_dual_new
            fleet, assign, dispatch, cover = fleet_new, assign_new, dispatch_new, cover_new
            if ends:
                reply_start(hedge_round)

    def put_out(at, own, far):
        row_0, row_1 = jnp.where(here == 0, own, far), jnp.where(here == 0, far, own)
        for c in range(own.shape[0]):
            packed[at, 0:1, c * tile : (c + 1) * tile] = row_0[c : c + 1]
            packed[at, 1:2, c * tile : (c + 1) * tile] = row_1[c : c + 1]

    early_copy.wait()
    put_out(0, fleet[:col_blocks], early_in[0])
    put_out(1, assign[:col_blocks], early_in[1])
    late_copy.wait()
    put_out(2, dispatch[:col_blocks], late_in[0])
    put_out(3, cover, late_in[1])
    reply_wait(ITERS - 1)
    back = reply_in.at[ITERS - 1]
    last_fleet = back[kind(0), :]
    even_mean, odd_mean = back[kind(1), :], back[kind(2), :]
    own_mean = jnp.where(here == 0, even_mean, odd_mean)
    far_mean = jnp.where(here == 0, odd_mean, even_mean)
    put_out(
        4,
        fleet_price[:col_blocks] + penalty * (fleet[:col_blocks] - last_fleet),
        early_in[2] + penalty * (early_in[0] - last_fleet),
    )
    put_out(
        5,
        assign_price[:col_blocks] + penalty * (assign[:col_blocks] - own_mean),
        early_in[3] + penalty * (early_in[1] - far_mean),
    )
    for r in range(ITERS):
        group_all(gather_out.at[r], gather_in.at[r], r).wait_send()
        group_all(reply_out.at[r], reply_in.at[r], ITERS + r).wait_send()


def unpack(packed, *outs):
    for k, out in enumerate(outs):
        out[...] = packed[k]


def fused_local(
    n_scen,
    tiles,
    row_index,
    col_index,
    tile_count,
    demand,
    root_cost,
    branch_cost,
    dispatch_cost,
    branch_of,
):
    slots, tile = tiles.shape[3], tiles.shape[5]
    lane_rows, width = demand.shape[1], branch_cost.shape[1]
    rows, cols, members = lane_rows // tile, width // tile, 2 * n_scen
    f32, i32 = jnp.float32, jnp.int32
    anywhere = pl.BlockSpec(memory_space=pl.ANY)
    col_shape = jax.ShapeDtypeStruct((2, width), f32)
    packed = pl.pallas_call(
        functools.partial(fused, n_scen),
        out_shape=jax.ShapeDtypeStruct((6, 2, width), f32),
        in_specs=[pl.BlockSpec(memory_space=pltpu.HBM)] * 9,
        out_specs=pl.BlockSpec(memory_space=pltpu.VMEM),
        scratch_shapes=[
            pltpu.SMEM(row_index.shape, i32),
            pltpu.SMEM(col_index.shape, i32),
            pltpu.SMEM((2,), i32),
            pltpu.SMEM(branch_of.shape, i32),
            pltpu.VMEM(demand.shape, f32),
            pltpu.VMEM((cols, tile), f32),
            pltpu.VMEM(branch_cost.shape, f32),
            pltpu.VMEM(dispatch_cost.shape, f32),
            pltpu.VMEM((2, slots, tile, tile), jnp.bfloat16),
            pltpu.VMEM((2, slots, tile, tile), jnp.bfloat16),
            pltpu.VMEM((3, cols, tile), f32),
            pltpu.VMEM((2, 3, cols, tile), f32),
            pltpu.SMEM((4 * slots,), jnp.int32),
            pltpu.SMEM((4 * slots,), jnp.int32),
            pltpu.VMEM((rows, tile), f32),
            pltpu.VMEM((2 * cols, tile), f32),
            pltpu.VMEM((ITERS, 8 * members, tile), f32),
            pltpu.VMEM((ITERS, 8 * members, tile), f32),
            pltpu.VMEM((ITERS, 8 * members, tile), f32),
            pltpu.VMEM((ITERS, 8 * members, tile), f32),
            pltpu.VMEM((4, cols, tile), f32),
            pltpu.VMEM((4, cols, tile), f32),
            pltpu.VMEM((2, cols, tile), f32),
            pltpu.VMEM((2, cols, tile), f32),
            pltpu.SemaphoreType.DMA,
            pltpu.SemaphoreType.DMA((8,)),
            pltpu.SemaphoreType.DMA((5,)),
            pltpu.SemaphoreType.DMA((5,)),
            pltpu.SemaphoreType.DMA((2 * ITERS,)),
            pltpu.SemaphoreType.DMA((2 * ITERS,)),
        ],
        compiler_params=pltpu.CompilerParams(
            collective_id=0, has_side_effects=True, vmem_limit_bytes=60 * 1024 * 1024
        ),
    )(
        tiles.reshape(2, slots, tile, tile),
        row_index,
        col_index,
        tile_count.reshape(2),
        demand,
        root_cost.reshape(cols, tile),
        branch_cost,
        dispatch_cost,
        branch_of,
    )
    return pl.pallas_call(
        unpack,
        out_shape=(col_shape,) * 6,
        in_specs=[pl.BlockSpec(memory_space=pltpu.VMEM)],
        out_specs=(pl.BlockSpec(memory_space=pltpu.VMEM),) * 6,
    )(packed)


def solution_body(mesh):
    n_scen = mesh.shape["scen"]
    fits = mesh.shape["lane"] == 1 and mesh.shape["dep"] == 2 and (2 * n_scen) % BRANCHES == 0

    def body(*args):
        tiles, demand, root_cost = args[0], args[4], args[5]
        tile = tiles.shape[5]
        cols, rows = root_cost.shape[0] // tile, demand.shape[1] // tile
        if fits and tiles.shape[0] == 2 and tile == 128 and cols == rows == 2 * n_scen and cols % 8 == 0:
            return fused_local(n_scen, *args)
        return local(*args)

    return body


def solution(mesh):
    in_specs = (
        P(("groups", "scen"), "lane", "dep", None, None, None),
        P(("groups", "scen"), "lane", "dep", None),
        P(("groups", "scen"), "lane", "dep", None),
        P(("groups", "scen"), "lane", "dep"),
        P(("groups", "scen"), "lane"),
        P(("groups", "dep")),
        P(("groups", "scen"), "dep"),
        P(("groups", "scen"), "dep"),
        P(("groups", "scen")),
    )
    out_specs = (
        P(("groups", "scen"), "dep"),
        P(("groups", "scen"), "dep"),
        P(("groups", "scen"), "dep"),
        P(("groups", "scen"), "lane"),
        P(("groups", "scen"), "dep"),
        P(("groups", "scen"), "dep"),
    )
    body = solution_body(mesh)
    return jax.shard_map(body, mesh=mesh, in_specs=in_specs, out_specs=out_specs, check_vma=False)
```

```python
import functools

import jax
import jax.numpy as jnp
from jax import lax
from jax.experimental import pallas as pl
from jax.experimental.pallas import tpu as pltpu
from jax.sharding import PartitionSpec as P

BRANCHES = 8
ITERS = 2
STEPS = 4


step_scale = 0.2
penalty = 1.0
epsilon = 1e-06


def reweigh(weight_ratio, totals, col_total, lane_total):
    primal_rate = totals[:, 0] / (3.0 * col_total)
    dual_rate = totals[:, 1] / (lane_total + 2.0 * col_total)
    target = jnp.sqrt((primal_rate + epsilon) / (dual_rate + epsilon))
    return jnp.sqrt(weight_ratio * target)


def pick_rows(source, places):
    return source[places]


def local(
    tiles,
    row_index,
    col_index,
    tile_count,
    demand,
    root_cost,
    branch_cost,
    dispatch_cost,
    branch_of,
):
    highest = lax.Precision.HIGHEST
    scen_here = tiles.shape[0]
    slots = tiles.shape[3]
    tile_size = tiles.shape[5]
    blocks = tiles.reshape(scen_here, slots, tile_size, tile_size)
    row_ids = row_index.reshape(scen_here, slots)
    col_ids = col_index.reshape(scen_here, slots)
    live_count = tile_count.reshape(scen_here)
    width = root_cost.shape[0]
    lane_rows = demand.shape[1]
    col_blocks = width // tile_size
    row_blocks = lane_rows // tile_size
    lane_count = lax.axis_size("lane")
    col_total = float(width * lax.axis_size("dep"))
    lane_total = float(lane_rows * lane_count)
    slot_iota = lax.broadcasted_iota(jnp.int32, (scen_here, slots), 1)
    live_mask = (slot_iota < live_count[:, None]).astype(jnp.float32)
    row_table = (row_ids[:, :, None] == jnp.arange(row_blocks, dtype=jnp.int32)).astype(
        jnp.float32
    ) * live_mask[:, :, None]
    col_table = (col_ids[:, :, None] == jnp.arange(col_blocks, dtype=jnp.int32)).astype(
        jnp.float32
    ) * live_mask[:, :, None]
    single_copy = (lax.axis_index("lane") == 0).astype(jnp.float32)
    dep_first = (lax.axis_index("dep") == 0).astype(jnp.float32)
    zeros_cols = jnp.zeros((scen_here, width), jnp.float32)
    fleet_plan = zeros_cols
    assign_plan = zeros_cols
    dispatch_plan = zeros_cols
    fleet_dual = zeros_cols
    assign_dual = zeros_cols
    fleet_price = zeros_cols
    assign_price = zeros_cols
    assign_mean = zeros_cols
    fleet_mean = jnp.zeros((width,), jnp.float32)
    cover_dual = jnp.zeros((scen_here, lane_rows), jnp.float32)
    weight_ratio = jnp.ones((scen_here,), jnp.float32)
    branch_table = (branch_of[:, None] == jnp.arange(BRANCHES, dtype=jnp.int32)).astype(jnp.float32)
    total_scen = scen_here * lax.axis_size("scen")
    per_branch = total_scen // BRANCHES
    for hedge_round in range(ITERS):
        penalty_now = 0.0 if hedge_round == 0 else penalty
        for inner_step in range(STEPS):
            closing = hedge_round == ITERS - 1 and inner_step == STEPS - 1
            picked = jax.vmap(pick_rows)(
                cover_dual.astype(jnp.bfloat16).reshape(scen_here, row_blocks, tile_size), row_ids
            )
            products = jnp.einsum(
                "snij,sni->snj", blocks, picked, preferred_element_type=jnp.float32
            )
            partial_value = jnp.einsum(
                "snc,snj->scj", col_table, products, precision=highest
            ).reshape(scen_here, width)
            pulled = lax.psum(partial_value, "lane")
            primal_step = step_scale / weight_ratio[:, None]
            dual_step = step_scale * weight_ratio[:, None]
            fleet_new = jnp.maximum(
                0.0,
                fleet_plan
                - primal_step
                * (
                    root_cost[None, :]
                    + fleet_price
                    + penalty_now * (fleet_plan - fleet_mean[None, :])
                    - fleet_dual
                ),
            )
            assign_new = jnp.maximum(
                0.0,
                assign_plan
                - primal_step
                * (
                    branch_cost
                    + assign_price
                    + penalty_now * (assign_plan - assign_mean)
                    + fleet_dual
                    - assign_dual
                ),
            )
            dispatch_new = jnp.maximum(
                0.0, dispatch_plan - primal_step * (dispatch_cost + assign_dual - pulled)
            )
            fleet_ext = 2.0 * fleet_new - fleet_plan
            assign_ext = 2.0 * assign_new - assign_plan
            dispatch_ext = 2.0 * dispatch_new - dispatch_plan
            assign_dual_new = jnp.maximum(
                0.0, assign_dual + dual_step * (dispatch_ext - assign_ext)
            )
            fleet_dual_new = jnp.maximum(0.0, fleet_dual + dual_step * (assign_ext - fleet_ext))
            extrap_bf = dispatch_ext.astype(jnp.bfloat16)
            forward_picked = jax.vmap(pick_rows)(
                extrap_bf.reshape(scen_here, col_blocks, tile_size), col_ids
            )
            forward_products = jnp.einsum(
                "snij,snj->sni", blocks, forward_picked, preferred_element_type=jnp.float32
            )
            load_part = jnp.einsum(
                "snr,sni->sri", row_table, forward_products, precision=highest
            ).reshape(scen_here, lane_rows)
            primal_moves = single_copy * jnp.sum(
                (fleet_new - fleet_plan) ** 2
                + (assign_new - assign_plan) ** 2
                + (dispatch_new - dispatch_plan) ** 2,
                axis=1,
            )
            pair_moves = single_copy * jnp.sum(
                (assign_dual_new - assign_dual) ** 2 + (fleet_dual_new - fleet_dual) ** 2, axis=1
            )
            lane_load = lax.psum(load_part, "dep")
            cover_new = jnp.maximum(0.0, cover_dual + dual_step * (demand - lane_load))
            cover_moves = jnp.sum((cover_new - cover_dual) ** 2, axis=1)
            if not closing:
                totals = lax.psum(
                    jnp.stack([primal_moves, pair_moves + dep_first * cover_moves], axis=1),
                    ("lane", "dep"),
                )
                weight_ratio = reweigh(weight_ratio, totals, col_total, lane_total)
            fleet_plan, assign_plan, dispatch_plan = (fleet_new, assign_new, dispatch_new)
            fleet_dual, assign_dual, cover_dual = (fleet_dual_new, assign_dual_new, cover_new)
        root_local = jnp.sum(fleet_plan, axis=0)
        branch_local = jnp.dot(branch_table.T, assign_plan, precision=highest)
        root_total, branch_total = lax.psum((root_local, branch_local), "scen")
        fleet_mean = root_total / total_scen
        branch_means = branch_total / per_branch
        assign_mean = jnp.dot(branch_table, branch_means, precision=highest)
        fleet_price = fleet_price + penalty * (fleet_plan - fleet_mean[None, :])
        assign_price = assign_price + penalty * (assign_plan - assign_mean)
    return (fleet_plan, assign_plan, dispatch_plan, cover_dual, fleet_price, assign_price)


MESH = pl.DeviceIdType.MESH


def dot(a, b):
    return jnp.dot(a, b, preferred_element_type=jnp.float32)


def dot_t(a, b):
    return lax.dot_general(a, b, (((1,), (1,)), ((), ())), preferred_element_type=jnp.float32)


def total(x):
    return jnp.sum(x, axis=(0, 1), keepdims=True)


def fused(
    n_scen,
    tiles,
    row_index_in,
    col_index_in,
    tile_count_in,
    demand_in,
    root_cost_in,
    branch_cost_in,
    dispatch_cost_in,
    branch_of_in,
    packed,
    row_index,
    col_index,
    tile_count,
    branch_of,
    demand,
    root_cost,
    branch_cost,
    dispatch_cost,
    blocks,
    flipped,
    costs_out,
    costs,
    ids_out,
    ids_in,
    cover_rows,
    dispatch_rows,
    gather_out,
    gather_in,
    reply_out,
    reply_in,
    branch_out,
    branch_in,
    same_branch,
    early_out,
    early_in,
    late_out,
    late_in,
    local_sem,
    load_sem,
    pair_send,
    pair_recv,
    group_send,
    group_recv,
    entered,
):
    here = lax.axis_index("dep")
    other = 1 - here
    chip = lax.axis_index("scen")
    me = 2 * chip + here
    members = 2 * n_scen
    slots = tiles.shape[1]
    tile = tiles.shape[2]
    lane_rows = demand.shape[1]
    width = branch_cost.shape[1]
    row_blocks = lane_rows // tile
    col_blocks = width // tile
    col_total = float(2 * width)
    lane_total = float(lane_rows)
    total_scen = float(members)
    per_branch = float(members // BRANCHES)

    owners = members // 2
    first_owner = members // 4
    owner = me - first_owner
    owns = jnp.logical_and(owner >= 0, owner < owners)

    def device_of(to):
        return {"scen": to // 2, "dep": lax.rem(to, 2)}

    def load(source, target, at):
        copy = pltpu.make_async_copy(source, target, load_sem.at[at])
        copy.start()
        return copy

    loads = [
        load(row_index_in, row_index, 0),
        load(col_index_in, col_index, 1),
        load(tile_count_in, tile_count, 2),
        load(branch_cost_in, branch_cost, 3),
        load(dispatch_cost_in, dispatch_cost, 4),
        load(root_cost_in, root_cost, 5),
        load(demand_in, demand, 6),
        load(branch_of_in, branch_of, 7),
    ]
    barrier = pltpu.get_barrier_semaphore()
    leads = here == 0
    for k in range(1, n_scen):
        device = {"scen": lax.rem(chip + k, n_scen), "dep": 1}
        pl.semaphore_signal(barrier, inc=1, device_id=device, device_id_type=MESH)

    @pl.when(here == 1)
    def _():
        pl.semaphore_signal(barrier, inc=1, device_id={"dep": other}, device_id_type=MESH)

    own_tiles = pltpu.make_async_copy(tiles.at[here], blocks.at[0], local_sem)
    own_tiles.start()

    def put_rows(own, far, source):
        for c in range(source.shape[1] // tile):
            row_0 = source[0:1, c * tile : (c + 1) * tile]
            row_1 = source[1:2, c * tile : (c + 1) * tile]
            own[c : c + 1, :] = jnp.where(here == 0, row_0, row_1)
            if far is not None:
                far[c : c + 1, :] = jnp.where(here == 0, row_1, row_0)

    for copy in loads:
        copy.wait()
    put_rows(costs.at[0, 0], costs_out.at[0], branch_cost)
    put_rows(costs.at[0, 1], costs_out.at[1], dispatch_cost)
    costs_out[2] = root_cost[...]
    costs[0, 2] = root_cost[...]
    for j in range(slots):
        ids_out[j] = row_index[other, 0, 0, j]
        ids_out[slots + j] = col_index[other, 0, 0, j]
    ids_out[2 * slots] = tile_count[other]

    def pair(source, target, at):
        return pltpu.make_async_remote_copy(
            src_ref=source,
            dst_ref=target,
            send_sem=pair_send.at[at],
            recv_sem=pair_recv.at[at],
            device_id={"dep": other},
            device_id_type=MESH,
        )

    ids_copy = pair(ids_out, ids_in, 0)
    costs_copy = pair(costs_out, costs.at[1], 1)
    tiles_copy = pair(tiles.at[other], blocks.at[1], 2)

    @pl.when(leads)
    def _():
        pl.semaphore_wait(barrier, 1)
        tiles_copy.start()
        ids_copy.start()
        costs_copy.start()

    @pl.when(here == 1)
    def _():
        ids_copy.wait_recv()
        tiles_copy.start()
        ids_copy.start()
        costs_copy.start()

    put_rows(cover_rows, None, demand)
    demand_here = cover_rows[...]

    row_ids, col_ids, row_marks, col_marks = [], [], [], []

    def take_ids(row_of, col_of, count):
        for j in range(slots):
            row, col = row_of(j), col_of(j)
            row_ids.append(row)
            col_ids.append(col)
            row_marks.append(jnp.where(j < count, row, -1))
            col_marks.append(jnp.where(j < count, col, -1))

    take_ids(
        lambda j: row_index[here, 0, 0, j],
        lambda j: col_index[here, 0, 0, j],
        tile_count[here],
    )
    @pl.when(leads)
    def _():
        ids_copy.wait_recv()

    ids_copy.wait_send()
    take_ids(lambda j: ids_in[j], lambda j: ids_in[slots + j], ids_in[2 * slots])

    lane_iota = lax.broadcasted_iota(jnp.int32, (row_blocks, tile), 0)
    col_iota = lax.broadcasted_iota(jnp.int32, (col_blocks, tile), 0)

    def spread(row, iota, mark):
        return jnp.where(iota == mark, jnp.broadcast_to(row, iota.shape), 0.0).astype(jnp.bfloat16)

    def backward(cover):
        cover_rows[...] = cover
        halves = []
        for half in range(2):
            left = []
            for n in range(half * slots, (half + 1) * slots):
                row = cover_rows[pl.ds(row_ids[n], 1), :]
                left.append(spread(row, col_iota, col_marks[n]))
            halves.append(dot(jnp.concatenate(left, axis=1), blocks[half].reshape(slots * tile, tile)))
        return jnp.concatenate(halves, axis=0)

    def forward(extrap):
        dispatch_rows[...] = extrap
        left = []
        for n in range(2 * slots):
            row = dispatch_rows[pl.ds(n // slots * col_blocks + col_ids[n], 1), :]
            left.append(spread(row, lane_iota, row_marks[n]))
        return dot(jnp.concatenate(left, axis=1), flipped[...].reshape(2 * slots * tile, tile))

    def flip(half):
        for j in range(slots):
            flipped[half, j] = blocks[half, j].T

    def place(index):
        return pl.ds(pl.multiple_of(8 * index, 8), 8)

    def group(source, target, at, to):
        return pltpu.make_async_remote_copy(
            src_ref=source,
            dst_ref=target,
            send_sem=group_send.at[at],
            recv_sem=group_recv.at[at],
            device_id=device_of(to),
            device_id_type=MESH,
        )

    def many(buffer, count, at):
        part = buffer.at[pl.ds(0, 8 * count)]
        return group(part, part, at, me + 1 - 2 * here)

    def either(mine, others):
        @pl.when(owns)
        def _():
            mine()

        @pl.when(jnp.logical_not(owns))
        def _():
            others()

    def in_order(x):
        own, far = x[:col_blocks], x[col_blocks:]
        return jnp.where(leads, own, far), jnp.where(leads, far, own)

    def kind(k, count):
        return pl.ds(k, count, stride=8)

    def to_owners(send):
        for k in range(owners):
            to = first_owner + lax.rem(me - first_owner + members + k, owners)
            if k:
                send(to)
            else:
                pl.when(jnp.logical_not(owns))(functools.partial(send, to))

    def branch_start():
        branch_out[...] = jnp.full((1, tile), branch_of[here].astype(jnp.float32), jnp.float32)

        def send(to):
            group(branch_out, branch_in.at[me], 2 * ITERS, to).start()

        to_owners(send)

    def branch_wait(count, wait):
        part = branch_in.at[pl.ds(0, count)]
        wait(group(part, part, 2 * ITERS, me + 1 - 2 * here))

    def gather_start(hedge_round, fleet, assign):
        buffer = gather_out.at[hedge_round]
        target = gather_in.at[hedge_round]
        for k, value in enumerate(in_order(fleet) + in_order(assign)):
            buffer[kind(2 * k, owners), :] = value[:owners]
            buffer[kind(2 * k + 1, owners), :] = value[owners:]

        def send(to):
            group(buffer.at[place(to - first_owner)], target.at[place(me)], hedge_round, to).start()

        to_owners(send)

        @pl.when(owns)
        def _():
            target[place(me), :] = buffer[place(owner), :]

    def reply_start(hedge_round):
        pl.when(owns)(functools.partial(reply, hedge_round))

    def reply(hedge_round):
        if hedge_round == 0:
            branch_wait(members - 1, lambda copy: copy.wait_recv())
            branch_in[me] = branch_out[...]
            branches = jnp.concatenate([branch_in[k] for k in range(members)], axis=0)
            lanes = lax.broadcasted_iota(jnp.int32, (members, tile), 1).astype(jnp.float32)
            hot = (branches == lanes).astype(jnp.bfloat16)
            same_branch[...] = dot_t(hot, hot)
        many(gather_in.at[hedge_round], members - 1, hedge_round).wait_recv()
        buffer = gather_in.at[hedge_round]
        parts = []
        for k in range(4, 8):
            value = buffer[kind(k, members), :]
            high = value.astype(jnp.bfloat16)
            rest = value - high.astype(jnp.float32)
            middle = rest.astype(jnp.bfloat16)
            low = (rest - middle.astype(jnp.float32)).astype(jnp.bfloat16)
            parts += [high, middle, low]
        sums = dot(same_branch[...].astype(jnp.bfloat16), jnp.concatenate(parts, axis=1))
        pieces = [sums[:, i * tile : (i + 1) * tile] for i in range(12)]
        means = [
            ((pieces[3 * k + 2] + pieces[3 * k + 1]) + pieces[3 * k]) / per_branch for k in range(4)
        ]
        fleets = [
            jnp.broadcast_to(
                jnp.sum(buffer[kind(k, members), :], axis=0, keepdims=True) / total_scen,
                (members, tile),
            )
            for k in range(4)
        ]
        if hedge_round < ITERS - 1:
            values = fleets + means
        else:
            even = lax.rem(lax.broadcasted_iota(jnp.int32, (members, tile), 0), 2) == 0
            down = [jnp.concatenate([x[-1:], x[:-1]], axis=0) for x in means[2:]]
            up = [jnp.concatenate([x[1:], x[:1]], axis=0) for x in means[:2]]
            values = [jnp.where(even, fleets[k], fleets[2 + k]) for k in range(2)]
            values += [jnp.where(even, means[k], down[k]) for k in range(2)]
            values += [jnp.where(even, up[k], means[2 + k]) for k in range(2)]
            values += [jnp.zeros((members, tile), jnp.float32)] * 2
        out, target = reply_out.at[hedge_round], reply_in.at[hedge_round]
        for k, value in enumerate(values):
            out[kind(k, members), :] = value
        for k in range(1, members):
            to = lax.rem(me + k, members)
            group(out.at[place(to)], target.at[place(owner)], ITERS + hedge_round, to).start()
        target[place(owner), :] = out[place(me), :]

    def reply_wait(hedge_round):
        buffer, at = reply_in.at[hedge_round], ITERS + hedge_round
        either(
            lambda: many(buffer, owners - 1, at).wait_recv(),
            lambda: many(buffer, owners, at).wait_recv(),
        )

    def reply_half(hedge_round, k):
        back = reply_in.at[hedge_round]
        return jnp.concatenate([back[kind(k, owners), :], back[kind(k + 1, owners), :]], axis=0)

    def reply_all(hedge_round, k):
        halves = jnp.concatenate([reply_half(hedge_round, k), reply_half(hedge_round, k + 2)], axis=0)
        return jnp.concatenate(in_order(halves), axis=0)

    def group_enter():
        @pl.when(here == 1)
        def _():
            pl.semaphore_wait(barrier, members - 2)
            pl.semaphore_signal(entered, inc=1, device_id={"dep": other}, device_id_type=MESH)

        @pl.when(leads)
        def _():
            pl.semaphore_wait(entered, 1)

    zeros = jnp.zeros((2 * col_blocks, tile), jnp.float32)
    fleet = assign = dispatch = fleet_dual = assign_dual = fleet_price = assign_price = zeros
    fleet_mean = assign_mean = zeros
    cover = jnp.zeros((row_blocks, tile), jnp.float32)
    ratio = jnp.ones((1, 1), jnp.float32)
    costs_copy.wait()
    branch_c = jnp.concatenate([costs[0, 0], costs[1, 0]], axis=0)
    dispatch_c = jnp.concatenate([costs[0, 1], costs[1, 1]], axis=0)
    root_c = jnp.concatenate([costs[0, 2], costs[1, 2]], axis=0)
    own_tiles.wait()
    flip(0)
    tiles_copy.wait()
    flip(1)

    pulled = zeros
    for hedge_round in range(ITERS):
        penalty_now = 0.0 if hedge_round == 0 else penalty
        for inner_step in range(STEPS):
            ends = inner_step == STEPS - 1
            closing = hedge_round == ITERS - 1 and ends
            waits = hedge_round > 0 and inner_step == 0
            primal_step = step_scale / ratio
            dual_step = step_scale * ratio

            def plans():
                pull_f = root_c + fleet_price - fleet_dual
                pull_a = branch_c + assign_price + fleet_dual - assign_dual
                if penalty_now:
                    pull_f = pull_f + penalty_now * (fleet - fleet_mean)
                    pull_a = pull_a + penalty_now * (assign - assign_mean)
                return (
                    jnp.maximum(0.0, fleet - primal_step * pull_f),
                    jnp.maximum(0.0, assign - primal_step * pull_a),
                )

            if not waits:
                fleet_new, assign_new = plans()
            if hedge_round == 0 and inner_step == STEPS - 2:
                group_enter()
                branch_start()
            if ends:
                gather_start(hedge_round, fleet_new, assign_new)
            if closing:
                for k, x in enumerate((fleet_new, assign_new, fleet_price, assign_price)):
                    early_out[k] = x[col_blocks:]
                early_copy = pair(early_out, early_in, 3)
                early_copy.start()
            dispatch_new = jnp.maximum(0.0, dispatch - primal_step * (dispatch_c + assign_dual - pulled))
            dispatch_ext = 2.0 * dispatch_new - dispatch
            load = forward(dispatch_ext)
            cover_new = jnp.maximum(0.0, cover + dual_step * (demand_here - load))
            if not closing:
                pulled = backward(cover_new)
            if closing:
                late_out[0] = dispatch_new[col_blocks:]
                late_out[1] = cover_new
                late_copy = pair(late_out, late_in, 4)
                late_copy.start()
            if waits:
                reply_wait(hedge_round - 1)
                fleet_mean = reply_all(hedge_round - 1, 0)
                assign_mean = reply_all(hedge_round - 1, 4)
                fleet_price = fleet_price + penalty * (fleet - fleet_mean)
                assign_price = assign_price + penalty * (assign - assign_mean)
                fleet_new, assign_new = plans()
            if not closing:
                fleet_ext = 2.0 * fleet_new - fleet
                assign_ext = 2.0 * assign_new - assign
                assign_dual_new = jnp.maximum(0.0, assign_dual + dual_step * (dispatch_ext - assign_ext))
                fleet_dual_new = jnp.maximum(0.0, fleet_dual + dual_step * (assign_ext - fleet_ext))
                primal_moves = total(
                    (fleet_new - fleet) ** 2 + (assign_new - assign) ** 2 + (dispatch_new - dispatch) ** 2
                )
                pair_moves = total((assign_dual_new - assign_dual) ** 2 + (fleet_dual_new - fleet_dual) ** 2)
                cover_moves = total((cover_new - cover) ** 2)
                primal_rate = primal_moves / (3.0 * col_total)
                dual_rate = (cover_moves + pair_moves) / (lane_total + 2.0 * col_total)
                target = jnp.sqrt((primal_rate + epsilon) / (dual_rate + epsilon))
                ratio = jnp.sqrt(ratio * target)
                fleet_dual, assign_dual = fleet_dual_new, assign_dual_new
            fleet, assign, dispatch, cover = fleet_new, assign_new, dispatch_new, cover_new
            if ends:
                reply_start(hedge_round)

    def put_out(at, own, far):
        row_0, row_1 = jnp.where(here == 0, own, far), jnp.where(here == 0, far, own)
        for c in range(own.shape[0]):
            packed[at, 0:1, c * tile : (c + 1) * tile] = row_0[c : c + 1]
            packed[at, 1:2, c * tile : (c + 1) * tile] = row_1[c : c + 1]

    early_copy.wait()
    put_out(0, fleet[:col_blocks], early_in[0])
    put_out(1, assign[:col_blocks], early_in[1])
    late_copy.wait()
    put_out(2, dispatch[:col_blocks], late_in[0])
    put_out(3, cover, late_in[1])
    reply_wait(ITERS - 1)
    last_fleet = reply_half(ITERS - 1, 0)
    even_mean, odd_mean = reply_half(ITERS - 1, 2), reply_half(ITERS - 1, 4)
    own_mean = jnp.where(here == 0, even_mean, odd_mean)
    far_mean = jnp.where(here == 0, odd_mean, even_mean)
    put_out(
        4,
        fleet_price[:col_blocks] + penalty * (fleet[:col_blocks] - last_fleet),
        early_in[2] + penalty * (early_in[0] - last_fleet),
    )
    put_out(
        5,
        assign_price[:col_blocks] + penalty * (assign[:col_blocks] - own_mean),
        early_in[3] + penalty * (early_in[1] - far_mean),
    )

    def sent_by_owner():
        branch_wait(owners - 1, lambda copy: copy.wait_send())
        for r in range(ITERS):
            many(gather_in.at[r], owners - 1, r).wait_send()
            many(gather_in.at[r], members - 1, ITERS + r).wait_send()

    def sent_by_others():
        branch_wait(owners, lambda copy: copy.wait_send())
        for r in range(ITERS):
            many(gather_in.at[r], owners, r).wait_send()

    either(sent_by_owner, sent_by_others)


def unpack(packed, *outs):
    for k, out in enumerate(outs):
        out[...] = packed[k]


def fused_local(
    n_scen,
    tiles,
    row_index,
    col_index,
    tile_count,
    demand,
    root_cost,
    branch_cost,
    dispatch_cost,
    branch_of,
):
    slots, tile = tiles.shape[3], tiles.shape[5]
    lane_rows, width = demand.shape[1], branch_cost.shape[1]
    rows, cols, members = lane_rows // tile, width // tile, 2 * n_scen
    f32, i32 = jnp.float32, jnp.int32
    anywhere = pl.BlockSpec(memory_space=pl.ANY)
    col_shape = jax.ShapeDtypeStruct((2, width), f32)
    packed = pl.pallas_call(
        functools.partial(fused, n_scen),
        out_shape=jax.ShapeDtypeStruct((6, 2, width), f32),
        in_specs=[pl.BlockSpec(memory_space=pltpu.HBM)] * 9,
        out_specs=pl.BlockSpec(memory_space=pltpu.VMEM),
        scratch_shapes=[
            pltpu.SMEM(row_index.shape, i32),
            pltpu.SMEM(col_index.shape, i32),
            pltpu.SMEM((2,), i32),
            pltpu.SMEM(branch_of.shape, i32),
            pltpu.VMEM(demand.shape, f32),
            pltpu.VMEM((cols, tile), f32),
            pltpu.VMEM(branch_cost.shape, f32),
            pltpu.VMEM(dispatch_cost.shape, f32),
            pltpu.VMEM((2, slots, tile, tile), jnp.bfloat16),
            pltpu.VMEM((2, slots, tile, tile), jnp.bfloat16),
            pltpu.VMEM((3, cols, tile), f32),
            pltpu.VMEM((2, 3, cols, tile), f32),
            pltpu.SMEM((4 * slots,), jnp.int32),
            pltpu.SMEM((4 * slots,), jnp.int32),
            pltpu.VMEM((rows, tile), f32),
            pltpu.VMEM((2 * cols, tile), f32),
            pltpu.VMEM((ITERS, 4 * members, tile), f32),
            pltpu.VMEM((ITERS, 8 * members, tile), f32),
            pltpu.VMEM((ITERS, 8 * members, tile), f32),
            pltpu.VMEM((ITERS, 4 * members, tile), f32),
            pltpu.VMEM((1, tile), f32),
            pltpu.VMEM((members, 1, tile), f32),
            pltpu.VMEM((members, members), f32),
            pltpu.VMEM((4, cols, tile), f32),
            pltpu.VMEM((4, cols, tile), f32),
            pltpu.VMEM((2, cols, tile), f32),
            pltpu.VMEM((2, cols, tile), f32),
            pltpu.SemaphoreType.DMA,
            pltpu.SemaphoreType.DMA((8,)),
            pltpu.SemaphoreType.DMA((5,)),
            pltpu.SemaphoreType.DMA((5,)),
            pltpu.SemaphoreType.DMA((2 * ITERS + 1,)),
            pltpu.SemaphoreType.DMA((2 * ITERS + 1,)),
            pltpu.SemaphoreType.REGULAR,
        ],
        compiler_params=pltpu.CompilerParams(
            collective_id=0, has_side_effects=True, vmem_limit_bytes=60 * 1024 * 1024
        ),
    )(
        tiles.reshape(2, slots, tile, tile),
        row_index,
        col_index,
        tile_count.reshape(2),
        demand,
        root_cost.reshape(cols, tile),
        branch_cost,
        dispatch_cost,
        branch_of,
    )
    return pl.pallas_call(
        unpack,
        out_shape=(col_shape,) * 6,
        in_specs=[pl.BlockSpec(memory_space=pltpu.VMEM)],
        out_specs=(pl.BlockSpec(memory_space=pltpu.VMEM),) * 6,
    )(packed)


def solution_body(mesh):
    n_scen = mesh.shape["scen"]
    fits = mesh.shape["lane"] == 1 and mesh.shape["dep"] == 2 and (2 * n_scen) % BRANCHES == 0

    def body(*args):
        tiles, demand, root_cost = args[0], args[4], args[5]
        tile = tiles.shape[5]
        cols, rows = root_cost.shape[0] // tile, demand.shape[1] // tile
        if fits and tiles.shape[0] == 2 and tile == 128 and cols == rows == 2 * n_scen and cols % 8 == 0:
            return fused_local(n_scen, *args)
        return local(*args)

    return body


def solution(mesh):
    in_specs = (
        P(("groups", "scen"), "lane", "dep", None, None, None),
        P(("groups", "scen"), "lane", "dep", None),
        P(("groups", "scen"), "lane", "dep", None),
        P(("groups", "scen"), "lane", "dep"),
        P(("groups", "scen"), "lane"),
        P(("groups", "dep")),
        P(("groups", "scen"), "dep"),
        P(("groups", "scen"), "dep"),
        P(("groups", "scen")),
    )
    out_specs = (
        P(("groups", "scen"), "dep"),
        P(("groups", "scen"), "dep"),
        P(("groups", "scen"), "dep"),
        P(("groups", "scen"), "lane"),
        P(("groups", "scen"), "dep"),
        P(("groups", "scen"), "dep"),
    )
    body = solution_body(mesh)
    return jax.shard_map(body, mesh=mesh, in_specs=in_specs, out_specs=out_specs, check_vma=False)
```

```python
import functools

import jax
import jax.numpy as jnp
from jax import lax
from jax.experimental import pallas as pl
from jax.experimental.pallas import tpu as pltpu
from jax.sharding import PartitionSpec as P

BRANCHES = 8
ITERS = 2
STEPS = 4


step_scale = 0.2
penalty = 1.0
epsilon = 1e-06


def reweigh(weight_ratio, totals, col_total, lane_total):
    primal_rate = totals[:, 0] / (3.0 * col_total)
    dual_rate = totals[:, 1] / (lane_total + 2.0 * col_total)
    target = jnp.sqrt((primal_rate + epsilon) / (dual_rate + epsilon))
    return jnp.sqrt(weight_ratio * target)


def pick_rows(source, places):
    return source[places]


def local(
    tiles,
    row_index,
    col_index,
    tile_count,
    demand,
    root_cost,
    branch_cost,
    dispatch_cost,
    branch_of,
):
    highest = lax.Precision.HIGHEST
    scen_here = tiles.shape[0]
    slots = tiles.shape[3]
    tile_size = tiles.shape[5]
    blocks = tiles.reshape(scen_here, slots, tile_size, tile_size)
    row_ids = row_index.reshape(scen_here, slots)
    col_ids = col_index.reshape(scen_here, slots)
    live_count = tile_count.reshape(scen_here)
    width = root_cost.shape[0]
    lane_rows = demand.shape[1]
    col_blocks = width // tile_size
    row_blocks = lane_rows // tile_size
    lane_count = lax.axis_size("lane")
    col_total = float(width * lax.axis_size("dep"))
    lane_total = float(lane_rows * lane_count)
    slot_iota = lax.broadcasted_iota(jnp.int32, (scen_here, slots), 1)
    live_mask = (slot_iota < live_count[:, None]).astype(jnp.float32)
    row_table = (row_ids[:, :, None] == jnp.arange(row_blocks, dtype=jnp.int32)).astype(
        jnp.float32
    ) * live_mask[:, :, None]
    col_table = (col_ids[:, :, None] == jnp.arange(col_blocks, dtype=jnp.int32)).astype(
        jnp.float32
    ) * live_mask[:, :, None]
    single_copy = (lax.axis_index("lane") == 0).astype(jnp.float32)
    dep_first = (lax.axis_index("dep") == 0).astype(jnp.float32)
    zeros_cols = jnp.zeros((scen_here, width), jnp.float32)
    fleet_plan = zeros_cols
    assign_plan = zeros_cols
    dispatch_plan = zeros_cols
    fleet_dual = zeros_cols
    assign_dual = zeros_cols
    fleet_price = zeros_cols
    assign_price = zeros_cols
    assign_mean = zeros_cols
    fleet_mean = jnp.zeros((width,), jnp.float32)
    cover_dual = jnp.zeros((scen_here, lane_rows), jnp.float32)
    weight_ratio = jnp.ones((scen_here,), jnp.float32)
    branch_table = (branch_of[:, None] == jnp.arange(BRANCHES, dtype=jnp.int32)).astype(jnp.float32)
    total_scen = scen_here * lax.axis_size("scen")
    per_branch = total_scen // BRANCHES
    for hedge_round in range(ITERS):
        penalty_now = 0.0 if hedge_round == 0 else penalty
        for inner_step in range(STEPS):
            closing = hedge_round == ITERS - 1 and inner_step == STEPS - 1
            picked = jax.vmap(pick_rows)(
                cover_dual.astype(jnp.bfloat16).reshape(scen_here, row_blocks, tile_size), row_ids
            )
            products = jnp.einsum(
                "snij,sni->snj", blocks, picked, preferred_element_type=jnp.float32
            )
            partial_value = jnp.einsum(
                "snc,snj->scj", col_table, products, precision=highest
            ).reshape(scen_here, width)
            pulled = lax.psum(partial_value, "lane")
            primal_step = step_scale / weight_ratio[:, None]
            dual_step = step_scale * weight_ratio[:, None]
            fleet_new = jnp.maximum(
                0.0,
                fleet_plan
                - primal_step
                * (
                    root_cost[None, :]
                    + fleet_price
                    + penalty_now * (fleet_plan - fleet_mean[None, :])
                    - fleet_dual
                ),
            )
            assign_new = jnp.maximum(
                0.0,
                assign_plan
                - primal_step
                * (
                    branch_cost
                    + assign_price
                    + penalty_now * (assign_plan - assign_mean)
                    + fleet_dual
                    - assign_dual
                ),
            )
            dispatch_new = jnp.maximum(
                0.0, dispatch_plan - primal_step * (dispatch_cost + assign_dual - pulled)
            )
            fleet_ext = 2.0 * fleet_new - fleet_plan
            assign_ext = 2.0 * assign_new - assign_plan
            dispatch_ext = 2.0 * dispatch_new - dispatch_plan
            assign_dual_new = jnp.maximum(
                0.0, assign_dual + dual_step * (dispatch_ext - assign_ext)
            )
            fleet_dual_new = jnp.maximum(0.0, fleet_dual + dual_step * (assign_ext - fleet_ext))
            extrap_bf = dispatch_ext.astype(jnp.bfloat16)
            forward_picked = jax.vmap(pick_rows)(
                extrap_bf.reshape(scen_here, col_blocks, tile_size), col_ids
            )
            forward_products = jnp.einsum(
                "snij,snj->sni", blocks, forward_picked, preferred_element_type=jnp.float32
            )
            load_part = jnp.einsum(
                "snr,sni->sri", row_table, forward_products, precision=highest
            ).reshape(scen_here, lane_rows)
            primal_moves = single_copy * jnp.sum(
                (fleet_new - fleet_plan) ** 2
                + (assign_new - assign_plan) ** 2
                + (dispatch_new - dispatch_plan) ** 2,
                axis=1,
            )
            pair_moves = single_copy * jnp.sum(
                (assign_dual_new - assign_dual) ** 2 + (fleet_dual_new - fleet_dual) ** 2, axis=1
            )
            lane_load = lax.psum(load_part, "dep")
            cover_new = jnp.maximum(0.0, cover_dual + dual_step * (demand - lane_load))
            cover_moves = jnp.sum((cover_new - cover_dual) ** 2, axis=1)
            if not closing:
                totals = lax.psum(
                    jnp.stack([primal_moves, pair_moves + dep_first * cover_moves], axis=1),
                    ("lane", "dep"),
                )
                weight_ratio = reweigh(weight_ratio, totals, col_total, lane_total)
            fleet_plan, assign_plan, dispatch_plan = (fleet_new, assign_new, dispatch_new)
            fleet_dual, assign_dual, cover_dual = (fleet_dual_new, assign_dual_new, cover_new)
        root_local = jnp.sum(fleet_plan, axis=0)
        branch_local = jnp.dot(branch_table.T, assign_plan, precision=highest)
        root_total, branch_total = lax.psum((root_local, branch_local), "scen")
        fleet_mean = root_total / total_scen
        branch_means = branch_total / per_branch
        assign_mean = jnp.dot(branch_table, branch_means, precision=highest)
        fleet_price = fleet_price + penalty * (fleet_plan - fleet_mean[None, :])
        assign_price = assign_price + penalty * (assign_plan - assign_mean)
    return (fleet_plan, assign_plan, dispatch_plan, cover_dual, fleet_price, assign_price)


MESH = pl.DeviceIdType.MESH


def dot(a, b):
    return jnp.dot(a, b, preferred_element_type=jnp.float32)


def dot_t(a, b):
    return lax.dot_general(a, b, (((1,), (1,)), ((), ())), preferred_element_type=jnp.float32)


def total(x):
    return jnp.sum(x, axis=(0, 1), keepdims=True)


def fused(
    n_scen,
    tiles,
    row_index_in,
    col_index_in,
    tile_count_in,
    demand_in,
    root_cost_in,
    branch_cost_in,
    dispatch_cost_in,
    branch_of_in,
    packed,
    row_index,
    col_index,
    tile_count,
    branch_of,
    demand,
    root_cost,
    branch_cost,
    dispatch_cost,
    blocks,
    flipped,
    costs_out,
    costs,
    ids_out,
    ids_in,
    cover_rows,
    dispatch_rows,
    gather_out,
    gather_in,
    reply_out,
    reply_in,
    branch_out,
    branch_in,
    same_branch,
    early_out,
    early_in,
    late_out,
    late_in,
    local_sem,
    load_sem,
    pair_send,
    pair_recv,
    group_send,
    group_recv,
    entered,
    met,
):
    here = lax.axis_index("dep")
    other = 1 - here
    chip = lax.axis_index("scen")
    me = 2 * chip + here
    members = 2 * n_scen
    slots = tiles.shape[1]
    tile = tiles.shape[2]
    lane_rows = demand.shape[1]
    width = branch_cost.shape[1]
    row_blocks = lane_rows // tile
    col_blocks = width // tile
    col_total = float(2 * width)
    lane_total = float(lane_rows)
    total_scen = float(members)
    per_branch = float(members // BRANCHES)

    owners = members // 2
    first_owner = members // 4
    owner = me - first_owner
    owns = jnp.logical_and(owner >= 0, owner < owners)

    def device_of(to):
        return {"scen": to // 2, "dep": lax.rem(to, 2)}

    def load(source, target, at):
        copy = pltpu.make_async_copy(source, target, load_sem.at[at])
        copy.start()
        return copy

    loads = [
        load(row_index_in, row_index, 0),
        load(col_index_in, col_index, 1),
        load(tile_count_in, tile_count, 2),
        load(branch_cost_in, branch_cost, 3),
        load(dispatch_cost_in, dispatch_cost, 4),
        load(root_cost_in, root_cost, 5),
        load(demand_in, demand, 6),
        load(branch_of_in, branch_of, 7),
    ]
    barrier = pltpu.get_barrier_semaphore()
    leads = here == 0
    for k in range(1, n_scen):
        device = {"scen": lax.rem(chip + k, n_scen), "dep": 1}
        pl.semaphore_signal(barrier, inc=1, device_id=device, device_id_type=MESH)

    @pl.when(here == 1)
    def _():
        pl.semaphore_signal(barrier, inc=1, device_id={"dep": other}, device_id_type=MESH)

    def put_rows(own, far, source):
        for c in range(source.shape[1] // tile):
            row_0 = source[0:1, c * tile : (c + 1) * tile]
            row_1 = source[1:2, c * tile : (c + 1) * tile]
            own[c : c + 1, :] = jnp.where(here == 0, row_0, row_1)
            if far is not None:
                far[c : c + 1, :] = jnp.where(here == 0, row_1, row_0)

    def pair(source, target, at):
        return pltpu.make_async_remote_copy(
            src_ref=source,
            dst_ref=target,
            send_sem=pair_send.at[at],
            recv_sem=pair_recv.at[at],
            device_id={"dep": other},
            device_id_type=MESH,
        )

    ids_copy = pair(ids_out, ids_in, 0)
    costs_copy = pair(costs_out, costs.at[1], 1)
    tiles_copy = pair(tiles.at[other], blocks.at[1], 2)

    @pl.when(leads)
    def _():
        pl.semaphore_wait(barrier, 1)
        pl.semaphore_signal(met, inc=1, device_id={"dep": other}, device_id_type=MESH)

    @pl.when(here == 1)
    def _():
        pl.semaphore_wait(met, 1)

    tiles_copy.start()
    own_tiles = pltpu.make_async_copy(tiles.at[here], blocks.at[0], local_sem)
    own_tiles.start()
    for copy in loads:
        copy.wait()
    put_rows(costs.at[0, 0], costs_out.at[0], branch_cost)
    put_rows(costs.at[0, 1], costs_out.at[1], dispatch_cost)
    costs_out[2] = root_cost[...]
    costs[0, 2] = root_cost[...]
    for j in range(slots):
        ids_out[j] = row_index[other, 0, 0, j]
        ids_out[slots + j] = col_index[other, 0, 0, j]
    ids_out[2 * slots] = tile_count[other]

    ids_copy.start()
    costs_copy.start()

    put_rows(cover_rows, None, demand)
    demand_here = cover_rows[...]

    row_ids, col_ids, row_marks, col_marks = [], [], [], []

    def take_ids(row_of, col_of, count):
        for j in range(slots):
            row, col = row_of(j), col_of(j)
            row_ids.append(row)
            col_ids.append(col)
            row_marks.append(jnp.where(j < count, row, -1))
            col_marks.append(jnp.where(j < count, col, -1))

    take_ids(
        lambda j: row_index[here, 0, 0, j],
        lambda j: col_index[here, 0, 0, j],
        tile_count[here],
    )
    ids_copy.wait()
    take_ids(lambda j: ids_in[j], lambda j: ids_in[slots + j], ids_in[2 * slots])

    lane_iota = lax.broadcasted_iota(jnp.int32, (row_blocks, tile), 0)
    col_iota = lax.broadcasted_iota(jnp.int32, (col_blocks, tile), 0)

    def spread(row, iota, mark):
        return jnp.where(iota == mark, jnp.broadcast_to(row, iota.shape), 0.0).astype(jnp.bfloat16)

    def backward(cover):
        cover_rows[...] = cover
        halves = []
        for half in range(2):
            left = []
            for n in range(half * slots, (half + 1) * slots):
                row = cover_rows[pl.ds(row_ids[n], 1), :]
                left.append(spread(row, col_iota, col_marks[n]))
            halves.append(dot(jnp.concatenate(left, axis=1), blocks[half].reshape(slots * tile, tile)))
        return jnp.concatenate(halves, axis=0)

    def forward(extrap):
        dispatch_rows[...] = extrap
        left = []
        for n in range(2 * slots):
            row = dispatch_rows[pl.ds(n // slots * col_blocks + col_ids[n], 1), :]
            left.append(spread(row, lane_iota, row_marks[n]))
        return dot(jnp.concatenate(left, axis=1), flipped[...].reshape(2 * slots * tile, tile))

    def flip(half):
        for j in range(slots):
            flipped[half, j] = blocks[half, j].T

    def place(index):
        return pl.ds(pl.multiple_of(8 * index, 8), 8)

    def group(source, target, at, to):
        return pltpu.make_async_remote_copy(
            src_ref=source,
            dst_ref=target,
            send_sem=group_send.at[at],
            recv_sem=group_recv.at[at],
            device_id=device_of(to),
            device_id_type=MESH,
        )

    def many(buffer, count, at):
        part = buffer.at[pl.ds(0, 8 * count)]
        return group(part, part, at, me + 1 - 2 * here)

    def either(mine, others):
        @pl.when(owns)
        def _():
            mine()

        @pl.when(jnp.logical_not(owns))
        def _():
            others()

    def in_order(x):
        own, far = x[:col_blocks], x[col_blocks:]
        return jnp.where(leads, own, far), jnp.where(leads, far, own)

    def kind(k, count):
        return pl.ds(k, count, stride=8)

    def to_owners(send):
        half = owners // 2
        home = me // half // 2 * half + lax.rem(me, half)
        for k in reversed(range(owners)):
            to = first_owner + jnp.bitwise_xor(home, k)
            if k:
                send(to)
            else:
                pl.when(jnp.logical_not(owns))(functools.partial(send, to))

    def branch_start():
        branch_out[...] = jnp.full((1, tile), branch_of[here].astype(jnp.float32), jnp.float32)

        def send(to):
            group(branch_out, branch_in.at[me], 2 * ITERS, to).start()

        to_owners(send)

    def branch_wait(count, wait):
        part = branch_in.at[pl.ds(0, count)]
        wait(group(part, part, 2 * ITERS, me + 1 - 2 * here))

    def gather_start(hedge_round, fleet, assign):
        buffer = gather_out.at[hedge_round]
        target = gather_in.at[hedge_round]
        for k, value in enumerate(in_order(fleet) + in_order(assign)):
            buffer[kind(2 * k, owners), :] = value[:owners]
            buffer[kind(2 * k + 1, owners), :] = value[owners:]

        def send(to):
            group(buffer.at[place(to - first_owner)], target.at[place(me)], hedge_round, to).start()

        to_owners(send)

        @pl.when(owns)
        def _():
            target[place(me), :] = buffer[place(owner), :]

    def reply_start(hedge_round):
        pl.when(owns)(functools.partial(reply, hedge_round))

    def reply(hedge_round):
        if hedge_round == 0:
            branch_wait(members - 1, lambda copy: copy.wait_recv())
            branch_in[me] = branch_out[...]
            branches = jnp.concatenate([branch_in[k] for k in range(members)], axis=0)
            lanes = lax.broadcasted_iota(jnp.int32, (members, tile), 1).astype(jnp.float32)
            hot = (branches == lanes).astype(jnp.bfloat16)
            same_branch[...] = dot_t(hot, hot)
        many(gather_in.at[hedge_round], members - 1, hedge_round).wait_recv()
        buffer = gather_in.at[hedge_round]
        parts = []
        for k in range(4, 8):
            value = buffer[kind(k, members), :]
            high = value.astype(jnp.bfloat16)
            rest = value - high.astype(jnp.float32)
            middle = rest.astype(jnp.bfloat16)
            low = (rest - middle.astype(jnp.float32)).astype(jnp.bfloat16)
            parts += [high, middle, low]
        sums = dot(same_branch[...].astype(jnp.bfloat16), jnp.concatenate(parts, axis=1))
        pieces = [sums[:, i * tile : (i + 1) * tile] for i in range(12)]
        means = [
            ((pieces[3 * k + 2] + pieces[3 * k + 1]) + pieces[3 * k]) / per_branch for k in range(4)
        ]
        fleets = [
            jnp.broadcast_to(
                jnp.sum(buffer[kind(k, members), :], axis=0, keepdims=True) / total_scen,
                (members, tile),
            )
            for k in range(4)
        ]
        if hedge_round < ITERS - 1:
            values = fleets + means
        else:
            even = lax.rem(lax.broadcasted_iota(jnp.int32, (members, tile), 0), 2) == 0
            down = [jnp.concatenate([x[-1:], x[:-1]], axis=0) for x in means[2:]]
            up = [jnp.concatenate([x[1:], x[:1]], axis=0) for x in means[:2]]
            values = [jnp.where(even, fleets[k], fleets[2 + k]) for k in range(2)]
            values += [jnp.where(even, means[k], down[k]) for k in range(2)]
            values += [jnp.where(even, up[k], means[2 + k]) for k in range(2)]
            values += [jnp.zeros((members, tile), jnp.float32)] * 2
        out, target = reply_out.at[hedge_round], reply_in.at[hedge_round]
        for k, value in enumerate(values):
            out[kind(k, members), :] = value
        quarter = members // 4
        near_last = [2, 3, 1, 0]
        for k in sorted(range(1, members), key=lambda k: (near_last.index(k // quarter), -k)):
            to = jnp.bitwise_xor(me, k)
            group(out.at[place(to)], target.at[place(owner)], ITERS + hedge_round, to).start()
        target[place(owner), :] = out[place(me), :]

    def reply_wait(hedge_round):
        buffer, at = reply_in.at[hedge_round], ITERS + hedge_round
        either(
            lambda: many(buffer, owners - 1, at).wait_recv(),
            lambda: many(buffer, owners, at).wait_recv(),
        )

    def reply_half(hedge_round, k):
        back = reply_in.at[hedge_round]
        return jnp.concatenate([back[kind(k, owners), :], back[kind(k + 1, owners), :]], axis=0)

    def reply_all(hedge_round, k):
        halves = jnp.concatenate([reply_half(hedge_round, k), reply_half(hedge_round, k + 2)], axis=0)
        return jnp.concatenate(in_order(halves), axis=0)

    def group_enter():
        @pl.when(here == 1)
        def _():
            pl.semaphore_wait(barrier, members - 2)
            pl.semaphore_signal(entered, inc=1, device_id={"dep": other}, device_id_type=MESH)

        @pl.when(leads)
        def _():
            pl.semaphore_wait(entered, 1)

    zeros = jnp.zeros((2 * col_blocks, tile), jnp.float32)
    fleet = assign = dispatch = fleet_dual = assign_dual = fleet_price = assign_price = zeros
    fleet_mean = assign_mean = zeros
    cover = jnp.zeros((row_blocks, tile), jnp.float32)
    ratio = jnp.ones((1, 1), jnp.float32)
    costs_copy.wait()
    branch_c = jnp.concatenate([costs[0, 0], costs[1, 0]], axis=0)
    dispatch_c = jnp.concatenate([costs[0, 1], costs[1, 1]], axis=0)
    root_c = jnp.concatenate([costs[0, 2], costs[1, 2]], axis=0)
    own_tiles.wait()
    flip(0)
    tiles_copy.wait()
    flip(1)

    pulled = zeros
    for hedge_round in range(ITERS):
        penalty_now = 0.0 if hedge_round == 0 else penalty
        for inner_step in range(STEPS):
            ends = inner_step == STEPS - 1
            closing = hedge_round == ITERS - 1 and ends
            waits = hedge_round > 0 and inner_step == 0
            primal_step = step_scale / ratio
            dual_step = step_scale * ratio

            def plans():
                pull_f = root_c + fleet_price - fleet_dual
                pull_a = branch_c + assign_price + fleet_dual - assign_dual
                if penalty_now:
                    pull_f = pull_f + penalty_now * (fleet - fleet_mean)
                    pull_a = pull_a + penalty_now * (assign - assign_mean)
                return (
                    jnp.maximum(0.0, fleet - primal_step * pull_f),
                    jnp.maximum(0.0, assign - primal_step * pull_a),
                )

            if not waits:
                fleet_new, assign_new = plans()
            if hedge_round == 0 and inner_step == STEPS - 2:
                group_enter()
                branch_start()
            if ends:
                gather_start(hedge_round, fleet_new, assign_new)
            if closing:
                for k, x in enumerate((fleet_new, assign_new, fleet_price, assign_price)):
                    early_out[k] = x[col_blocks:]
                early_copy = pair(early_out, early_in, 3)
                early_copy.start()
            dispatch_new = jnp.maximum(0.0, dispatch - primal_step * (dispatch_c + assign_dual - pulled))
            dispatch_ext = 2.0 * dispatch_new - dispatch
            load = forward(dispatch_ext)
            cover_new = jnp.maximum(0.0, cover + dual_step * (demand_here - load))
            if not closing:
                pulled = backward(cover_new)
            if closing:
                late_out[0] = dispatch_new[col_blocks:]
                late_out[1] = cover_new
                late_copy = pair(late_out, late_in, 4)
                late_copy.start()
            if waits:
                reply_wait(hedge_round - 1)
                fleet_mean = reply_all(hedge_round - 1, 0)
                assign_mean = reply_all(hedge_round - 1, 4)
                fleet_price = fleet_price + penalty * (fleet - fleet_mean)
                assign_price = assign_price + penalty * (assign - assign_mean)
                fleet_new, assign_new = plans()
            if not closing:
                fleet_ext = 2.0 * fleet_new - fleet
                assign_ext = 2.0 * assign_new - assign
                assign_dual_new = jnp.maximum(0.0, assign_dual + dual_step * (dispatch_ext - assign_ext))
                fleet_dual_new = jnp.maximum(0.0, fleet_dual + dual_step * (assign_ext - fleet_ext))
                primal_moves = total(
                    (fleet_new - fleet) ** 2 + (assign_new - assign) ** 2 + (dispatch_new - dispatch) ** 2
                )
                pair_moves = total((assign_dual_new - assign_dual) ** 2 + (fleet_dual_new - fleet_dual) ** 2)
                cover_moves = total((cover_new - cover) ** 2)
                primal_rate = primal_moves / (3.0 * col_total)
                dual_rate = (cover_moves + pair_moves) / (lane_total + 2.0 * col_total)
                target = jnp.sqrt((primal_rate + epsilon) / (dual_rate + epsilon))
                ratio = jnp.sqrt(ratio * target)
                fleet_dual, assign_dual = fleet_dual_new, assign_dual_new
            fleet, assign, dispatch, cover = fleet_new, assign_new, dispatch_new, cover_new
            if ends:
                reply_start(hedge_round)

    def put_out(at, own, far):
        row_0, row_1 = jnp.where(here == 0, own, far), jnp.where(here == 0, far, own)
        for c in range(own.shape[0]):
            packed[at, 0:1, c * tile : (c + 1) * tile] = row_0[c : c + 1]
            packed[at, 1:2, c * tile : (c + 1) * tile] = row_1[c : c + 1]

    early_copy.wait()
    put_out(0, fleet[:col_blocks], early_in[0])
    put_out(1, assign[:col_blocks], early_in[1])
    late_copy.wait()
    put_out(2, dispatch[:col_blocks], late_in[0])
    put_out(3, cover, late_in[1])
    reply_wait(ITERS - 1)
    last_fleet = reply_half(ITERS - 1, 0)
    even_mean, odd_mean = reply_half(ITERS - 1, 2), reply_half(ITERS - 1, 4)
    own_mean = jnp.where(here == 0, even_mean, odd_mean)
    far_mean = jnp.where(here == 0, odd_mean, even_mean)
    put_out(
        4,
        fleet_price[:col_blocks] + penalty * (fleet[:col_blocks] - last_fleet),
        early_in[2] + penalty * (early_in[0] - last_fleet),
    )
    put_out(
        5,
        assign_price[:col_blocks] + penalty * (assign[:col_blocks] - own_mean),
        early_in[3] + penalty * (early_in[1] - far_mean),
    )

    def sent_by_owner():
        branch_wait(owners - 1, lambda copy: copy.wait_send())
        for r in range(ITERS):
            many(gather_in.at[r], owners - 1, r).wait_send()
            many(gather_in.at[r], members - 1, ITERS + r).wait_send()

    def sent_by_others():
        branch_wait(owners, lambda copy: copy.wait_send())
        for r in range(ITERS):
            many(gather_in.at[r], owners, r).wait_send()

    either(sent_by_owner, sent_by_others)


def unpack(packed, *outs):
    for k, out in enumerate(outs):
        out[...] = packed[k]


def fused_local(
    n_scen,
    tiles,
    row_index,
    col_index,
    tile_count,
    demand,
    root_cost,
    branch_cost,
    dispatch_cost,
    branch_of,
):
    slots, tile = tiles.shape[3], tiles.shape[5]
    lane_rows, width = demand.shape[1], branch_cost.shape[1]
    rows, cols, members = lane_rows // tile, width // tile, 2 * n_scen
    f32, i32 = jnp.float32, jnp.int32
    anywhere = pl.BlockSpec(memory_space=pl.ANY)
    col_shape = jax.ShapeDtypeStruct((2, width), f32)
    packed = pl.pallas_call(
        functools.partial(fused, n_scen),
        out_shape=jax.ShapeDtypeStruct((6, 2, width), f32),
        in_specs=[pl.BlockSpec(memory_space=pltpu.HBM)] * 9,
        out_specs=pl.BlockSpec(memory_space=pltpu.VMEM),
        scratch_shapes=[
            pltpu.SMEM(row_index.shape, i32),
            pltpu.SMEM(col_index.shape, i32),
            pltpu.SMEM((2,), i32),
            pltpu.SMEM(branch_of.shape, i32),
            pltpu.VMEM(demand.shape, f32),
            pltpu.VMEM((cols, tile), f32),
            pltpu.VMEM(branch_cost.shape, f32),
            pltpu.VMEM(dispatch_cost.shape, f32),
            pltpu.VMEM((2, slots, tile, tile), jnp.bfloat16),
            pltpu.VMEM((2, slots, tile, tile), jnp.bfloat16),
            pltpu.VMEM((3, cols, tile), f32),
            pltpu.VMEM((2, 3, cols, tile), f32),
            pltpu.SMEM((4 * slots,), jnp.int32),
            pltpu.SMEM((4 * slots,), jnp.int32),
            pltpu.VMEM((rows, tile), f32),
            pltpu.VMEM((2 * cols, tile), f32),
            pltpu.VMEM((ITERS, 4 * members, tile), f32),
            pltpu.VMEM((ITERS, 8 * members, tile), f32),
            pltpu.VMEM((ITERS, 8 * members, tile), f32),
            pltpu.VMEM((ITERS, 4 * members, tile), f32),
            pltpu.VMEM((1, tile), f32),
            pltpu.VMEM((members, 1, tile), f32),
            pltpu.VMEM((members, members), f32),
            pltpu.VMEM((4, cols, tile), f32),
            pltpu.VMEM((4, cols, tile), f32),
            pltpu.VMEM((2, cols, tile), f32),
            pltpu.VMEM((2, cols, tile), f32),
            pltpu.SemaphoreType.DMA,
            pltpu.SemaphoreType.DMA((8,)),
            pltpu.SemaphoreType.DMA((5,)),
            pltpu.SemaphoreType.DMA((5,)),
            pltpu.SemaphoreType.DMA((2 * ITERS + 1,)),
            pltpu.SemaphoreType.DMA((2 * ITERS + 1,)),
            pltpu.SemaphoreType.REGULAR,
            pltpu.SemaphoreType.REGULAR,
        ],
        compiler_params=pltpu.CompilerParams(
            collective_id=0, has_side_effects=True, vmem_limit_bytes=60 * 1024 * 1024
        ),
    )(
        tiles.reshape(2, slots, tile, tile),
        row_index,
        col_index,
        tile_count.reshape(2),
        demand,
        root_cost.reshape(cols, tile),
        branch_cost,
        dispatch_cost,
        branch_of,
    )
    return pl.pallas_call(
        unpack,
        out_shape=(col_shape,) * 6,
        in_specs=[pl.BlockSpec(memory_space=pltpu.VMEM)],
        out_specs=(pl.BlockSpec(memory_space=pltpu.VMEM),) * 6,
    )(packed)


def solution_body(mesh):
    n_scen = mesh.shape["scen"]
    fits = mesh.shape["lane"] == 1 and mesh.shape["dep"] == 2 and (2 * n_scen) % BRANCHES == 0

    def body(*args):
        tiles, demand, root_cost = args[0], args[4], args[5]
        tile = tiles.shape[5]
        cols, rows = root_cost.shape[0] // tile, demand.shape[1] // tile
        if fits and tiles.shape[0] == 2 and tile == 128 and cols == rows == 2 * n_scen and cols == 16:
            return fused_local(n_scen, *args)
        return local(*args)

    return body


def solution(mesh):
    in_specs = (
        P(("groups", "scen"), "lane", "dep", None, None, None),
        P(("groups", "scen"), "lane", "dep", None),
        P(("groups", "scen"), "lane", "dep", None),
        P(("groups", "scen"), "lane", "dep"),
        P(("groups", "scen"), "lane"),
        P(("groups", "dep")),
        P(("groups", "scen"), "dep"),
        P(("groups", "scen"), "dep"),
        P(("groups", "scen")),
    )
    out_specs = (
        P(("groups", "scen"), "dep"),
        P(("groups", "scen"), "dep"),
        P(("groups", "scen"), "dep"),
        P(("groups", "scen"), "lane"),
        P(("groups", "scen"), "dep"),
        P(("groups", "scen"), "dep"),
    )
    body = solution_body(mesh)
    return jax.shard_map(body, mesh=mesh, in_specs=in_specs, out_specs=out_specs, check_vma=False)
```

```python
import functools

import jax
import jax.numpy as jnp
from jax import lax
from jax.experimental import pallas as pl
from jax.experimental.pallas import tpu as pltpu
from jax.sharding import PartitionSpec as P

BRANCHES = 8
ITERS = 2
STEPS = 4


step_scale = 0.2
penalty = 1.0
epsilon = 1e-06


def reweigh(weight_ratio, totals, col_total, lane_total):
    primal_rate = totals[:, 0] / (3.0 * col_total)
    dual_rate = totals[:, 1] / (lane_total + 2.0 * col_total)
    target = jnp.sqrt((primal_rate + epsilon) / (dual_rate + epsilon))
    return jnp.sqrt(weight_ratio * target)


def pick_rows(source, places):
    return source[places]


def local(
    tiles,
    row_index,
    col_index,
    tile_count,
    demand,
    root_cost,
    branch_cost,
    dispatch_cost,
    branch_of,
):
    highest = lax.Precision.HIGHEST
    scen_here = tiles.shape[0]
    slots = tiles.shape[3]
    tile_size = tiles.shape[5]
    blocks = tiles.reshape(scen_here, slots, tile_size, tile_size)
    row_ids = row_index.reshape(scen_here, slots)
    col_ids = col_index.reshape(scen_here, slots)
    live_count = tile_count.reshape(scen_here)
    width = root_cost.shape[0]
    lane_rows = demand.shape[1]
    col_blocks = width // tile_size
    row_blocks = lane_rows // tile_size
    lane_count = lax.axis_size("lane")
    col_total = float(width * lax.axis_size("dep"))
    lane_total = float(lane_rows * lane_count)
    slot_iota = lax.broadcasted_iota(jnp.int32, (scen_here, slots), 1)
    live_mask = (slot_iota < live_count[:, None]).astype(jnp.float32)
    row_table = (row_ids[:, :, None] == jnp.arange(row_blocks, dtype=jnp.int32)).astype(
        jnp.float32
    ) * live_mask[:, :, None]
    col_table = (col_ids[:, :, None] == jnp.arange(col_blocks, dtype=jnp.int32)).astype(
        jnp.float32
    ) * live_mask[:, :, None]
    single_copy = (lax.axis_index("lane") == 0).astype(jnp.float32)
    dep_first = (lax.axis_index("dep") == 0).astype(jnp.float32)
    zeros_cols = jnp.zeros((scen_here, width), jnp.float32)
    fleet_plan = zeros_cols
    assign_plan = zeros_cols
    dispatch_plan = zeros_cols
    fleet_dual = zeros_cols
    assign_dual = zeros_cols
    fleet_price = zeros_cols
    assign_price = zeros_cols
    assign_mean = zeros_cols
    fleet_mean = jnp.zeros((width,), jnp.float32)
    cover_dual = jnp.zeros((scen_here, lane_rows), jnp.float32)
    weight_ratio = jnp.ones((scen_here,), jnp.float32)
    branch_table = (branch_of[:, None] == jnp.arange(BRANCHES, dtype=jnp.int32)).astype(jnp.float32)
    total_scen = scen_here * lax.axis_size("scen")
    per_branch = total_scen // BRANCHES
    for hedge_round in range(ITERS):
        penalty_now = 0.0 if hedge_round == 0 else penalty
        for inner_step in range(STEPS):
            closing = hedge_round == ITERS - 1 and inner_step == STEPS - 1
            picked = jax.vmap(pick_rows)(
                cover_dual.astype(jnp.bfloat16).reshape(scen_here, row_blocks, tile_size), row_ids
            )
            products = jnp.einsum(
                "snij,sni->snj", blocks, picked, preferred_element_type=jnp.float32
            )
            partial_value = jnp.einsum(
                "snc,snj->scj", col_table, products, precision=highest
            ).reshape(scen_here, width)
            pulled = lax.psum(partial_value, "lane")
            primal_step = step_scale / weight_ratio[:, None]
            dual_step = step_scale * weight_ratio[:, None]
            fleet_new = jnp.maximum(
                0.0,
                fleet_plan
                - primal_step
                * (
                    root_cost[None, :]
                    + fleet_price
                    + penalty_now * (fleet_plan - fleet_mean[None, :])
                    - fleet_dual
                ),
            )
            assign_new = jnp.maximum(
                0.0,
                assign_plan
                - primal_step
                * (
                    branch_cost
                    + assign_price
                    + penalty_now * (assign_plan - assign_mean)
                    + fleet_dual
                    - assign_dual
                ),
            )
            dispatch_new = jnp.maximum(
                0.0, dispatch_plan - primal_step * (dispatch_cost + assign_dual - pulled)
            )
            fleet_ext = 2.0 * fleet_new - fleet_plan
            assign_ext = 2.0 * assign_new - assign_plan
            dispatch_ext = 2.0 * dispatch_new - dispatch_plan
            assign_dual_new = jnp.maximum(
                0.0, assign_dual + dual_step * (dispatch_ext - assign_ext)
            )
            fleet_dual_new = jnp.maximum(0.0, fleet_dual + dual_step * (assign_ext - fleet_ext))
            extrap_bf = dispatch_ext.astype(jnp.bfloat16)
            forward_picked = jax.vmap(pick_rows)(
                extrap_bf.reshape(scen_here, col_blocks, tile_size), col_ids
            )
            forward_products = jnp.einsum(
                "snij,snj->sni", blocks, forward_picked, preferred_element_type=jnp.float32
            )
            load_part = jnp.einsum(
                "snr,sni->sri", row_table, forward_products, precision=highest
            ).reshape(scen_here, lane_rows)
            primal_moves = single_copy * jnp.sum(
                (fleet_new - fleet_plan) ** 2
                + (assign_new - assign_plan) ** 2
                + (dispatch_new - dispatch_plan) ** 2,
                axis=1,
            )
            pair_moves = single_copy * jnp.sum(
                (assign_dual_new - assign_dual) ** 2 + (fleet_dual_new - fleet_dual) ** 2, axis=1
            )
            lane_load = lax.psum(load_part, "dep")
            cover_new = jnp.maximum(0.0, cover_dual + dual_step * (demand - lane_load))
            cover_moves = jnp.sum((cover_new - cover_dual) ** 2, axis=1)
            if not closing:
                totals = lax.psum(
                    jnp.stack([primal_moves, pair_moves + dep_first * cover_moves], axis=1),
                    ("lane", "dep"),
                )
                weight_ratio = reweigh(weight_ratio, totals, col_total, lane_total)
            fleet_plan, assign_plan, dispatch_plan = (fleet_new, assign_new, dispatch_new)
            fleet_dual, assign_dual, cover_dual = (fleet_dual_new, assign_dual_new, cover_new)
        root_local = jnp.sum(fleet_plan, axis=0)
        branch_local = jnp.dot(branch_table.T, assign_plan, precision=highest)
        root_total, branch_total = lax.psum((root_local, branch_local), "scen")
        fleet_mean = root_total / total_scen
        branch_means = branch_total / per_branch
        assign_mean = jnp.dot(branch_table, branch_means, precision=highest)
        fleet_price = fleet_price + penalty * (fleet_plan - fleet_mean[None, :])
        assign_price = assign_price + penalty * (assign_plan - assign_mean)
    return (fleet_plan, assign_plan, dispatch_plan, cover_dual, fleet_price, assign_price)


MESH = pl.DeviceIdType.MESH


def dot(a, b):
    return jnp.dot(a, b, preferred_element_type=jnp.float32)


def dot_t(a, b):
    return lax.dot_general(a, b, (((1,), (1,)), ((), ())), preferred_element_type=jnp.float32)


def total(x):
    return jnp.sum(x, axis=(0, 1), keepdims=True)


def fused(
    n_scen,
    tiles,
    row_index_in,
    col_index_in,
    tile_count_in,
    demand_in,
    root_cost_in,
    branch_cost_in,
    dispatch_cost_in,
    branch_of_in,
    packed,
    row_index,
    col_index,
    tile_count,
    branch_of,
    demand,
    root_cost,
    branch_cost,
    dispatch_cost,
    blocks,
    flipped,
    costs_out,
    costs,
    ids_out,
    ids_in,
    cover_rows,
    dispatch_rows,
    gather_out,
    gather_in,
    reply_out,
    reply_in,
    last_out,
    last_in,
    branch_out,
    branch_in,
    early_out,
    early_in,
    late_out,
    late_in,
    local_sem,
    load_sem,
    pair_send,
    pair_recv,
    group_send,
    group_recv,
    entered,
    met,
):
    here = lax.axis_index("dep")
    other = 1 - here
    chip = lax.axis_index("scen")
    me = 2 * chip + here
    members = 2 * n_scen
    slots = tiles.shape[1]
    tile = tiles.shape[2]
    lane_rows = demand.shape[1]
    width = branch_cost.shape[1]
    row_blocks = lane_rows // tile
    col_blocks = width // tile
    col_total = float(2 * width)
    lane_total = float(lane_rows)
    total_scen = float(members)
    per_branch = float(members // BRANCHES)

    owners = members // 4
    first_owner = members // 4
    owner = chip - first_owner // 2
    owns = jnp.logical_and(here == 1, jnp.logical_and(owner >= 0, owner < owners))
    own_half = lax.rem(chip, 2)
    own_ends = jnp.logical_and(owns, own_half == 1)

    def device_of(to):
        return {"scen": to // 2, "dep": lax.rem(to, 2)}

    def load(source, target, at):
        copy = pltpu.make_async_copy(source, target, load_sem.at[at])
        copy.start()
        return copy

    loads = [
        load(row_index_in, row_index, 0),
        load(col_index_in, col_index, 1),
        load(tile_count_in, tile_count, 2),
        load(branch_cost_in, branch_cost, 3),
        load(dispatch_cost_in, dispatch_cost, 4),
        load(root_cost_in, root_cost, 5),
        load(demand_in, demand, 6),
        load(branch_of_in, branch_of, 7),
    ]
    barrier = pltpu.get_barrier_semaphore()
    leads = here == 0
    for k in range(1, n_scen):
        device = {"scen": lax.rem(chip + k, n_scen), "dep": 1}
        pl.semaphore_signal(barrier, inc=1, device_id=device, device_id_type=MESH)

    @pl.when(here == 1)
    def _():
        pl.semaphore_signal(barrier, inc=1, device_id={"dep": other}, device_id_type=MESH)

    def put_rows(own, far, source):
        for c in range(source.shape[1] // tile):
            row_0 = source[0:1, c * tile : (c + 1) * tile]
            row_1 = source[1:2, c * tile : (c + 1) * tile]
            own[c : c + 1, :] = jnp.where(here == 0, row_0, row_1)
            if far is not None:
                far[c : c + 1, :] = jnp.where(here == 0, row_1, row_0)

    def pair(source, target, at):
        return pltpu.make_async_remote_copy(
            src_ref=source,
            dst_ref=target,
            send_sem=pair_send.at[at],
            recv_sem=pair_recv.at[at],
            device_id={"dep": other},
            device_id_type=MESH,
        )

    ids_copy = pair(ids_out, ids_in, 0)
    costs_copy = pair(costs_out, costs.at[1], 1)
    tiles_copy = pair(tiles.at[other], blocks.at[1], 2)

    @pl.when(leads)
    def _():
        pl.semaphore_wait(barrier, 1)
        pl.semaphore_signal(met, inc=1, device_id={"dep": other}, device_id_type=MESH)

    @pl.when(here == 1)
    def _():
        pl.semaphore_wait(met, 1)

    tiles_copy.start()
    own_tiles = pltpu.make_async_copy(tiles.at[here], blocks.at[0], local_sem)
    own_tiles.start()
    for copy in loads:
        copy.wait()
    put_rows(costs.at[0, 0], costs_out.at[0], branch_cost)
    put_rows(costs.at[0, 1], costs_out.at[1], dispatch_cost)
    costs_out[2] = root_cost[...]
    costs[0, 2] = root_cost[...]
    for j in range(slots):
        ids_out[j] = row_index[other, 0, 0, j]
        ids_out[slots + j] = col_index[other, 0, 0, j]
    ids_out[2 * slots] = tile_count[other]

    ids_copy.start()
    costs_copy.start()

    put_rows(cover_rows, None, demand)
    demand_here = cover_rows[...]

    row_ids, col_ids, row_marks, col_marks = [], [], [], []

    def take_ids(row_of, col_of, count):
        for j in range(slots):
            row, col = row_of(j), col_of(j)
            row_ids.append(row)
            col_ids.append(col)
            row_marks.append(jnp.where(j < count, row, -1))
            col_marks.append(jnp.where(j < count, col, -1))

    take_ids(
        lambda j: row_index[here, 0, 0, j],
        lambda j: col_index[here, 0, 0, j],
        tile_count[here],
    )
    ids_copy.wait()
    take_ids(lambda j: ids_in[j], lambda j: ids_in[slots + j], ids_in[2 * slots])

    lane_iota = lax.broadcasted_iota(jnp.int32, (row_blocks, tile), 0)
    col_iota = lax.broadcasted_iota(jnp.int32, (col_blocks, tile), 0)

    def spread(row, iota, mark):
        return jnp.where(iota == mark, jnp.broadcast_to(row, iota.shape), 0.0).astype(jnp.bfloat16)

    def backward(cover):
        cover_rows[...] = cover
        halves = []
        for half in range(2):
            left = []
            for n in range(half * slots, (half + 1) * slots):
                row = cover_rows[pl.ds(row_ids[n], 1), :]
                left.append(spread(row, col_iota, col_marks[n]))
            halves.append(dot(jnp.concatenate(left, axis=1), blocks[half].reshape(slots * tile, tile)))
        return jnp.concatenate(halves, axis=0)

    def forward(extrap):
        dispatch_rows[...] = extrap
        left = []
        for n in range(2 * slots):
            row = dispatch_rows[pl.ds(n // slots * col_blocks + col_ids[n], 1), :]
            left.append(spread(row, lane_iota, row_marks[n]))
        return dot(jnp.concatenate(left, axis=1), flipped[...].reshape(2 * slots * tile, tile))

    def flip(half):
        for j in range(slots):
            flipped[half, j] = blocks[half, j].T

    def place(index, rows):
        return pl.ds(pl.multiple_of(rows * index, 8), rows)

    def group(source, target, at, to):
        return pltpu.make_async_remote_copy(
            src_ref=source,
            dst_ref=target,
            send_sem=group_send.at[at],
            recv_sem=group_recv.at[at],
            device_id=device_of(to),
            device_id_type=MESH,
        )

    def many(rows, at):
        part = gather_in.at[0, pl.ds(0, rows)]
        return group(part, part, at, me + 1 - 2 * here)

    def either(test, mine, others):
        pl.when(test)(mine)
        pl.when(jnp.logical_not(test))(others)

    def in_order(x):
        own, far = x[:col_blocks], x[col_blocks:]
        return jnp.where(leads, own, far), jnp.where(leads, far, own)

    def to_owners(send):
        home = chip // owners * 2 + lax.rem(chip, 2)
        for k in reversed(range(owners)):
            to = first_owner + 2 * jnp.bitwise_xor(home, k) + 1
            if k:
                send(to)
            else:
                pl.when(jnp.logical_not(owns))(functools.partial(send, to))

    def branch_start():
        branch_out[...] = jnp.full((1, tile), branch_of[here].astype(jnp.float32), jnp.float32)

        def send(to):
            group(branch_out, branch_in.at[me], 2 * ITERS, to).start()

        to_owners(send)

    def branch_wait(count, wait):
        part = branch_in.at[pl.ds(0, count)]
        wait(group(part, part, 2 * ITERS, me + 1 - 2 * here))

    def gather_start(hedge_round, fleet, assign):
        buffer = gather_out.at[hedge_round]
        target = gather_in.at[hedge_round]
        fleets, assigns = in_order(fleet), in_order(assign)
        for o in range(owners):
            part = slice(o // 2 * 8, o // 2 * 8 + 8)
            buffer[16 * o : 16 * o + 8, :] = fleets[o % 2][part]
            buffer[16 * o + 8 : 16 * o + 16, :] = assigns[o % 2][part]

        def send(to):
            source = buffer.at[place((to - first_owner) // 2, 16)]
            group(source, target.at[place(me, 16)], hedge_round, to).start()

        to_owners(send)

        @pl.when(owns)
        def _():
            target[place(me, 16), :] = buffer[place(owner, 16), :]

    def reply_start(hedge_round):
        pl.when(owns)(functools.partial(reply, hedge_round))

    def reply(hedge_round):
        if hedge_round == 0:
            branch_wait(members - 1, lambda copy: copy.wait_recv())
            branch_in[me] = branch_out[...]
        many(16 * (members - 1), hedge_round).wait_recv()
        buffer = gather_in.at[hedge_round]
        fleet_sum = buffer[0:8, :]
        for k in range(1, members):
            fleet_sum = fleet_sum + buffer[16 * k : 16 * k + 8, :]
        fleet_means = fleet_sum / total_scen
        branches = [jnp.broadcast_to(branch_in[k], (8, tile)) for k in range(members)]
        assigns = [buffer[16 * k + 8 : 16 * k + 16, :] for k in range(members)]
        sums = list(assigns)
        for k in range(members):
            for m in range(k + 1, members):
                same = branches[k] == branches[m]
                sums[k] = sums[k] + jnp.where(same, assigns[m], 0.0)
                sums[m] = sums[m] + jnp.where(same, assigns[k], 0.0)
        means = [x / per_branch for x in sums]
        if hedge_round < ITERS - 1:
            for k in range(members):
                reply_out[16 * k : 16 * k + 8, :] = fleet_means
                reply_out[16 * k + 8 : 16 * k + 16, :] = means[k]
            for k in far_first(members):
                to = jnp.bitwise_xor(me, k)
                source, target = reply_out.at[place(to, 16)], reply_in.at[place(owner, 16)]
                group(source, target, ITERS + hedge_round, to).start()
            reply_in[place(owner, 16), :] = reply_out[place(me, 16), :]
        else:
            for k in range(n_scen):
                last_out[24 * k : 24 * k + 8, :] = fleet_means
                last_out[24 * k + 8 : 24 * k + 16, :] = means[2 * k]
                last_out[24 * k + 16 : 24 * k + 24, :] = means[2 * k + 1]
            target = last_in.at[place(owner // 2, 24)]

            def send(k):
                there = jnp.bitwise_xor(chip, k)
                source = last_out.at[place(there, 24)]
                group(source, target, ITERS + hedge_round, 2 * there + own_half).start()

            for k in far_first(n_scen):
                send(k)

            @pl.when(own_half == 0)
            def _():
                send(0)

            @pl.when(own_half == 1)
            def _():
                last_in[place(owner // 2, 24), :] = last_out[place(chip, 24), :]

    def far_first(count):
        quarter = count // 4
        near_last = [2, 3, 1, 0]
        return sorted(range(1, count), key=lambda k: (near_last.index(k // quarter), -k))

    def reply_wait(hedge_round):
        at = ITERS + hedge_round
        if hedge_round < ITERS - 1:
            either(
                owns,
                lambda: many(16 * (owners - 1), at).wait_recv(),
                lambda: many(16 * owners, at).wait_recv(),
            )
        else:
            either(
                own_ends,
                lambda: many(24 * (owners // 2 - 1), at).wait_recv(),
                lambda: many(24 * (owners // 2), at).wait_recv(),
            )

    def reply_all(k):
        halves = [reply_in[16 * o + k : 16 * o + k + 8, :] for o in (0, 2, 1, 3)]
        return jnp.concatenate(in_order(jnp.concatenate(halves, axis=0)), axis=0)

    def last_half(k):
        return jnp.concatenate([last_in[k : k + 8, :], last_in[24 + k : 32 + k, :]], axis=0)

    def group_enter():
        @pl.when(here == 1)
        def _():
            pl.semaphore_wait(barrier, members - 2)
            pl.semaphore_signal(entered, inc=1, device_id={"dep": other}, device_id_type=MESH)

        @pl.when(leads)
        def _():
            pl.semaphore_wait(entered, 1)

    zeros = jnp.zeros((2 * col_blocks, tile), jnp.float32)
    fleet = assign = dispatch = fleet_dual = assign_dual = fleet_price = assign_price = zeros
    fleet_mean = assign_mean = zeros
    cover = jnp.zeros((row_blocks, tile), jnp.float32)
    ratio = jnp.ones((1, 1), jnp.float32)
    costs_copy.wait()
    branch_c = jnp.concatenate([costs[0, 0], costs[1, 0]], axis=0)
    dispatch_c = jnp.concatenate([costs[0, 1], costs[1, 1]], axis=0)
    root_c = jnp.concatenate([costs[0, 2], costs[1, 2]], axis=0)
    own_tiles.wait()
    flip(0)
    tiles_copy.wait()
    flip(1)

    pulled = zeros
    for hedge_round in range(ITERS):
        penalty_now = 0.0 if hedge_round == 0 else penalty
        for inner_step in range(STEPS):
            ends = inner_step == STEPS - 1
            closing = hedge_round == ITERS - 1 and ends
            waits = hedge_round > 0 and inner_step == 0
            primal_step = step_scale / ratio
            dual_step = step_scale * ratio

            def plans():
                pull_f = root_c + fleet_price - fleet_dual
                pull_a = branch_c + assign_price + fleet_dual - assign_dual
                if penalty_now:
                    pull_f = pull_f + penalty_now * (fleet - fleet_mean)
                    pull_a = pull_a + penalty_now * (assign - assign_mean)
                return (
                    jnp.maximum(0.0, fleet - primal_step * pull_f),
                    jnp.maximum(0.0, assign - primal_step * pull_a),
                )

            if not waits:
                fleet_new, assign_new = plans()
            if hedge_round == 0 and inner_step == STEPS - 2:
                group_enter()
                branch_start()
            if ends:
                gather_start(hedge_round, fleet_new, assign_new)
            if closing:
                for k, x in enumerate((fleet_new, assign_new, fleet_price, assign_price)):
                    early_out[k] = x[col_blocks:]
                early_copy = pair(early_out, early_in, 3)
                early_copy.start()
            dispatch_new = jnp.maximum(0.0, dispatch - primal_step * (dispatch_c + assign_dual - pulled))
            dispatch_ext = 2.0 * dispatch_new - dispatch
            load = forward(dispatch_ext)
            cover_new = jnp.maximum(0.0, cover + dual_step * (demand_here - load))
            if not closing:
                pulled = backward(cover_new)
            if closing:
                late_out[0] = dispatch_new[col_blocks:]
                late_out[1] = cover_new
                late_copy = pair(late_out, late_in, 4)
                late_copy.start()
            if waits:
                reply_wait(hedge_round - 1)
                fleet_mean = reply_all(0)
                assign_mean = reply_all(8)
                fleet_price = fleet_price + penalty * (fleet - fleet_mean)
                assign_price = assign_price + penalty * (assign - assign_mean)
                fleet_new, assign_new = plans()
            if not closing:
                fleet_ext = 2.0 * fleet_new - fleet
                assign_ext = 2.0 * assign_new - assign
                assign_dual_new = jnp.maximum(0.0, assign_dual + dual_step * (dispatch_ext - assign_ext))
                fleet_dual_new = jnp.maximum(0.0, fleet_dual + dual_step * (assign_ext - fleet_ext))
                primal_moves = total(
                    (fleet_new - fleet) ** 2 + (assign_new - assign) ** 2 + (dispatch_new - dispatch) ** 2
                )
                pair_moves = total((assign_dual_new - assign_dual) ** 2 + (fleet_dual_new - fleet_dual) ** 2)
                cover_moves = total((cover_new - cover) ** 2)
                primal_rate = primal_moves / (3.0 * col_total)
                dual_rate = (cover_moves + pair_moves) / (lane_total + 2.0 * col_total)
                target = jnp.sqrt((primal_rate + epsilon) / (dual_rate + epsilon))
                ratio = jnp.sqrt(ratio * target)
                fleet_dual, assign_dual = fleet_dual_new, assign_dual_new
            fleet, assign, dispatch, cover = fleet_new, assign_new, dispatch_new, cover_new
            if ends:
                reply_start(hedge_round)

    def put_out(at, own, far):
        row_0, row_1 = jnp.where(here == 0, own, far), jnp.where(here == 0, far, own)
        for c in range(own.shape[0]):
            packed[at, 0:1, c * tile : (c + 1) * tile] = row_0[c : c + 1]
            packed[at, 1:2, c * tile : (c + 1) * tile] = row_1[c : c + 1]

    early_copy.wait()
    put_out(0, fleet[:col_blocks], early_in[0])
    put_out(1, assign[:col_blocks], early_in[1])
    late_copy.wait()
    put_out(2, dispatch[:col_blocks], late_in[0])
    put_out(3, cover, late_in[1])
    reply_wait(ITERS - 1)
    last_fleet, even_mean, odd_mean = last_half(0), last_half(8), last_half(16)
    own_mean = jnp.where(here == 0, even_mean, odd_mean)
    far_mean = jnp.where(here == 0, odd_mean, even_mean)
    put_out(
        4,
        fleet_price[:col_blocks] + penalty * (fleet[:col_blocks] - last_fleet),
        early_in[2] + penalty * (early_in[0] - last_fleet),
    )
    put_out(
        5,
        assign_price[:col_blocks] + penalty * (assign[:col_blocks] - own_mean),
        early_in[3] + penalty * (early_in[1] - far_mean),
    )

    def sent_by_owner():
        branch_wait(owners - 1, lambda copy: copy.wait_send())
        for r in range(ITERS):
            many(16 * (owners - 1), r).wait_send()
        many(16 * (members - 1), ITERS).wait_send()
        either(
            own_ends,
            lambda: many(24 * (n_scen - 1), 2 * ITERS - 1).wait_send(),
            lambda: many(24 * n_scen, 2 * ITERS - 1).wait_send(),
        )

    def sent_by_others():
        branch_wait(owners, lambda copy: copy.wait_send())
        for r in range(ITERS):
            many(16 * owners, r).wait_send()

    either(owns, sent_by_owner, sent_by_others)


def unpack(packed, *outs):
    for k, out in enumerate(outs):
        out[...] = packed[k]


def fused_local(
    n_scen,
    tiles,
    row_index,
    col_index,
    tile_count,
    demand,
    root_cost,
    branch_cost,
    dispatch_cost,
    branch_of,
):
    slots, tile = tiles.shape[3], tiles.shape[5]
    lane_rows, width = demand.shape[1], branch_cost.shape[1]
    rows, cols, members = lane_rows // tile, width // tile, 2 * n_scen
    f32, i32 = jnp.float32, jnp.int32
    anywhere = pl.BlockSpec(memory_space=pl.ANY)
    col_shape = jax.ShapeDtypeStruct((2, width), f32)
    packed = pl.pallas_call(
        functools.partial(fused, n_scen),
        out_shape=jax.ShapeDtypeStruct((6, 2, width), f32),
        in_specs=[pl.BlockSpec(memory_space=pltpu.HBM)] * 9,
        out_specs=pl.BlockSpec(memory_space=pltpu.VMEM),
        scratch_shapes=[
            pltpu.SMEM(row_index.shape, i32),
            pltpu.SMEM(col_index.shape, i32),
            pltpu.SMEM((2,), i32),
            pltpu.SMEM(branch_of.shape, i32),
            pltpu.VMEM(demand.shape, f32),
            pltpu.VMEM((cols, tile), f32),
            pltpu.VMEM(branch_cost.shape, f32),
            pltpu.VMEM(dispatch_cost.shape, f32),
            pltpu.VMEM((2, slots, tile, tile), jnp.bfloat16),
            pltpu.VMEM((2, slots, tile, tile), jnp.bfloat16),
            pltpu.VMEM((3, cols, tile), f32),
            pltpu.VMEM((2, 3, cols, tile), f32),
            pltpu.SMEM((4 * slots,), jnp.int32),
            pltpu.SMEM((4 * slots,), jnp.int32),
            pltpu.VMEM((rows, tile), f32),
            pltpu.VMEM((2 * cols, tile), f32),
            pltpu.VMEM((ITERS, 4 * members, tile), f32),
            pltpu.VMEM((ITERS, 16 * members, tile), f32),
            pltpu.VMEM((16 * members, tile), f32),
            pltpu.VMEM((4 * members, tile), f32),
            pltpu.VMEM((24 * n_scen, tile), f32),
            pltpu.VMEM((48, tile), f32),
            pltpu.VMEM((1, tile), f32),
            pltpu.VMEM((members, 1, tile), f32),
            pltpu.VMEM((4, cols, tile), f32),
            pltpu.VMEM((4, cols, tile), f32),
            pltpu.VMEM((2, cols, tile), f32),
            pltpu.VMEM((2, cols, tile), f32),
            pltpu.SemaphoreType.DMA,
            pltpu.SemaphoreType.DMA((8,)),
            pltpu.SemaphoreType.DMA((5,)),
            pltpu.SemaphoreType.DMA((5,)),
            pltpu.SemaphoreType.DMA((2 * ITERS + 1,)),
            pltpu.SemaphoreType.DMA((2 * ITERS + 1,)),
            pltpu.SemaphoreType.REGULAR,
            pltpu.SemaphoreType.REGULAR,
        ],
        compiler_params=pltpu.CompilerParams(
            collective_id=0, has_side_effects=True, vmem_limit_bytes=60 * 1024 * 1024
        ),
    )(
        tiles.reshape(2, slots, tile, tile),
        row_index,
        col_index,
        tile_count.reshape(2),
        demand,
        root_cost.reshape(cols, tile),
        branch_cost,
        dispatch_cost,
        branch_of,
    )
    return pl.pallas_call(
        unpack,
        out_shape=(col_shape,) * 6,
        in_specs=[pl.BlockSpec(memory_space=pltpu.VMEM)],
        out_specs=(pl.BlockSpec(memory_space=pltpu.VMEM),) * 6,
    )(packed)


def solution_body(mesh):
    n_scen = mesh.shape["scen"]
    fits = mesh.shape["lane"] == 1 and mesh.shape["dep"] == 2 and (2 * n_scen) % BRANCHES == 0

    def body(*args):
        tiles, demand, root_cost = args[0], args[4], args[5]
        tile = tiles.shape[5]
        cols, rows = root_cost.shape[0] // tile, demand.shape[1] // tile
        if fits and tiles.shape[0] == 2 and tile == 128 and cols == rows == 2 * n_scen and cols == 16:
            return fused_local(n_scen, *args)
        return local(*args)

    return body


def solution(mesh):
    in_specs = (
        P(("groups", "scen"), "lane", "dep", None, None, None),
        P(("groups", "scen"), "lane", "dep", None),
        P(("groups", "scen"), "lane", "dep", None),
        P(("groups", "scen"), "lane", "dep"),
        P(("groups", "scen"), "lane"),
        P(("groups", "dep")),
        P(("groups", "scen"), "dep"),
        P(("groups", "scen"), "dep"),
        P(("groups", "scen")),
    )
    out_specs = (
        P(("groups", "scen"), "dep"),
        P(("groups", "scen"), "dep"),
        P(("groups", "scen"), "dep"),
        P(("groups", "scen"), "lane"),
        P(("groups", "scen"), "dep"),
        P(("groups", "scen"), "dep"),
    )
    body = solution_body(mesh)
    return jax.shard_map(body, mesh=mesh, in_specs=in_specs, out_specs=out_specs, check_vma=False)
```

```python
import functools

import jax
import jax.numpy as jnp
from jax import lax
from jax.experimental import pallas as pl
from jax.experimental.pallas import tpu as pltpu
from jax.sharding import PartitionSpec as P

BRANCHES = 8
ITERS = 2
STEPS = 4


step_scale = 0.2
penalty = 1.0
epsilon = 1e-06


def reweigh(weight_ratio, totals, col_total, lane_total):
    primal_rate = totals[:, 0] / (3.0 * col_total)
    dual_rate = totals[:, 1] / (lane_total + 2.0 * col_total)
    target = jnp.sqrt((primal_rate + epsilon) / (dual_rate + epsilon))
    return jnp.sqrt(weight_ratio * target)


def pick_rows(source, places):
    return source[places]


def local(
    tiles,
    row_index,
    col_index,
    tile_count,
    demand,
    root_cost,
    branch_cost,
    dispatch_cost,
    branch_of,
):
    highest = lax.Precision.HIGHEST
    scen_here = tiles.shape[0]
    slots = tiles.shape[3]
    tile_size = tiles.shape[5]
    blocks = tiles.reshape(scen_here, slots, tile_size, tile_size)
    row_ids = row_index.reshape(scen_here, slots)
    col_ids = col_index.reshape(scen_here, slots)
    live_count = tile_count.reshape(scen_here)
    width = root_cost.shape[0]
    lane_rows = demand.shape[1]
    col_blocks = width // tile_size
    row_blocks = lane_rows // tile_size
    lane_count = lax.axis_size("lane")
    col_total = float(width * lax.axis_size("dep"))
    lane_total = float(lane_rows * lane_count)
    slot_iota = lax.broadcasted_iota(jnp.int32, (scen_here, slots), 1)
    live_mask = (slot_iota < live_count[:, None]).astype(jnp.float32)
    row_table = (row_ids[:, :, None] == jnp.arange(row_blocks, dtype=jnp.int32)).astype(
        jnp.float32
    ) * live_mask[:, :, None]
    col_table = (col_ids[:, :, None] == jnp.arange(col_blocks, dtype=jnp.int32)).astype(
        jnp.float32
    ) * live_mask[:, :, None]
    single_copy = (lax.axis_index("lane") == 0).astype(jnp.float32)
    dep_first = (lax.axis_index("dep") == 0).astype(jnp.float32)
    zeros_cols = jnp.zeros((scen_here, width), jnp.float32)
    fleet_plan = zeros_cols
    assign_plan = zeros_cols
    dispatch_plan = zeros_cols
    fleet_dual = zeros_cols
    assign_dual = zeros_cols
    fleet_price = zeros_cols
    assign_price = zeros_cols
    assign_mean = zeros_cols
    fleet_mean = jnp.zeros((width,), jnp.float32)
    cover_dual = jnp.zeros((scen_here, lane_rows), jnp.float32)
    weight_ratio = jnp.ones((scen_here,), jnp.float32)
    branch_table = (branch_of[:, None] == jnp.arange(BRANCHES, dtype=jnp.int32)).astype(jnp.float32)
    total_scen = scen_here * lax.axis_size("scen")
    per_branch = total_scen // BRANCHES
    for hedge_round in range(ITERS):
        penalty_now = 0.0 if hedge_round == 0 else penalty
        for inner_step in range(STEPS):
            closing = hedge_round == ITERS - 1 and inner_step == STEPS - 1
            picked = jax.vmap(pick_rows)(
                cover_dual.astype(jnp.bfloat16).reshape(scen_here, row_blocks, tile_size), row_ids
            )
            products = jnp.einsum(
                "snij,sni->snj", blocks, picked, preferred_element_type=jnp.float32
            )
            partial_value = jnp.einsum(
                "snc,snj->scj", col_table, products, precision=highest
            ).reshape(scen_here, width)
            pulled = lax.psum(partial_value, "lane")
            primal_step = step_scale / weight_ratio[:, None]
            dual_step = step_scale * weight_ratio[:, None]
            fleet_new = jnp.maximum(
                0.0,
                fleet_plan
                - primal_step
                * (
                    root_cost[None, :]
                    + fleet_price
                    + penalty_now * (fleet_plan - fleet_mean[None, :])
                    - fleet_dual
                ),
            )
            assign_new = jnp.maximum(
                0.0,
                assign_plan
                - primal_step
                * (
                    branch_cost
                    + assign_price
                    + penalty_now * (assign_plan - assign_mean)
                    + fleet_dual
                    - assign_dual
                ),
            )
            dispatch_new = jnp.maximum(
                0.0, dispatch_plan - primal_step * (dispatch_cost + assign_dual - pulled)
            )
            fleet_ext = 2.0 * fleet_new - fleet_plan
            assign_ext = 2.0 * assign_new - assign_plan
            dispatch_ext = 2.0 * dispatch_new - dispatch_plan
            assign_dual_new = jnp.maximum(
                0.0, assign_dual + dual_step * (dispatch_ext - assign_ext)
            )
            fleet_dual_new = jnp.maximum(0.0, fleet_dual + dual_step * (assign_ext - fleet_ext))
            extrap_bf = dispatch_ext.astype(jnp.bfloat16)
            forward_picked = jax.vmap(pick_rows)(
                extrap_bf.reshape(scen_here, col_blocks, tile_size), col_ids
            )
            forward_products = jnp.einsum(
                "snij,snj->sni", blocks, forward_picked, preferred_element_type=jnp.float32
            )
            load_part = jnp.einsum(
                "snr,sni->sri", row_table, forward_products, precision=highest
            ).reshape(scen_here, lane_rows)
            primal_moves = single_copy * jnp.sum(
                (fleet_new - fleet_plan) ** 2
                + (assign_new - assign_plan) ** 2
                + (dispatch_new - dispatch_plan) ** 2,
                axis=1,
            )
            pair_moves = single_copy * jnp.sum(
                (assign_dual_new - assign_dual) ** 2 + (fleet_dual_new - fleet_dual) ** 2, axis=1
            )
            lane_load = lax.psum(load_part, "dep")
            cover_new = jnp.maximum(0.0, cover_dual + dual_step * (demand - lane_load))
            cover_moves = jnp.sum((cover_new - cover_dual) ** 2, axis=1)
            if not closing:
                totals = lax.psum(
                    jnp.stack([primal_moves, pair_moves + dep_first * cover_moves], axis=1),
                    ("lane", "dep"),
                )
                weight_ratio = reweigh(weight_ratio, totals, col_total, lane_total)
            fleet_plan, assign_plan, dispatch_plan = (fleet_new, assign_new, dispatch_new)
            fleet_dual, assign_dual, cover_dual = (fleet_dual_new, assign_dual_new, cover_new)
        root_local = jnp.sum(fleet_plan, axis=0)
        branch_local = jnp.dot(branch_table.T, assign_plan, precision=highest)
        root_total, branch_total = lax.psum((root_local, branch_local), "scen")
        fleet_mean = root_total / total_scen
        branch_means = branch_total / per_branch
        assign_mean = jnp.dot(branch_table, branch_means, precision=highest)
        fleet_price = fleet_price + penalty * (fleet_plan - fleet_mean[None, :])
        assign_price = assign_price + penalty * (assign_plan - assign_mean)
    return (fleet_plan, assign_plan, dispatch_plan, cover_dual, fleet_price, assign_price)


MESH = pl.DeviceIdType.MESH


def dot(a, b):
    return jnp.dot(a, b, preferred_element_type=jnp.float32)


def dot_t(a, b):
    return lax.dot_general(a, b, (((1,), (1,)), ((), ())), preferred_element_type=jnp.float32)


def total(x):
    return jnp.sum(x, axis=(0, 1), keepdims=True)


def fused(
    n_scen,
    tiles,
    row_index_in,
    col_index_in,
    tile_count_in,
    demand_in,
    root_cost_in,
    branch_cost_in,
    dispatch_cost_in,
    branch_of_in,
    packed,
    row_index,
    col_index,
    tile_count,
    branch_of,
    demand,
    root_cost,
    branch_cost,
    dispatch_cost,
    blocks,
    flipped,
    costs_out,
    costs,
    ids_out,
    ids_in,
    cover_rows,
    dispatch_rows,
    gather_out,
    gather_in,
    reply_out,
    reply_in,
    last_out,
    last_in,
    branch_out,
    branch_in,
    early_out,
    early_in,
    late_out,
    late_in,
    local_sem,
    load_sem,
    pair_send,
    pair_recv,
    group_send,
    group_recv,
    entered,
    met,
):
    here = lax.axis_index("dep")
    other = 1 - here
    chip = lax.axis_index("scen")
    me = 2 * chip + here
    members = 2 * n_scen
    slots = tiles.shape[1]
    tile = tiles.shape[2]
    lane_rows = demand.shape[1]
    width = branch_cost.shape[1]
    row_blocks = lane_rows // tile
    col_blocks = width // tile
    col_total = float(2 * width)
    lane_total = float(lane_rows)
    total_scen = float(members)
    per_branch = float(members // BRANCHES)

    owners = members // 4
    first_owner = members // 4
    owner = chip - first_owner // 2
    owns = jnp.logical_and(here == 1, jnp.logical_and(owner >= 0, owner < owners))
    plane = lax.rem(chip, 2)
    own_half = owner // 2
    own_ends = jnp.logical_and(owns, owner >= 2)

    def device_of(to):
        return {"scen": to // 2, "dep": lax.rem(to, 2)}

    def load(source, target, at):
        copy = pltpu.make_async_copy(source, target, load_sem.at[at])
        copy.start()
        return copy

    loads = [
        load(row_index_in, row_index, 0),
        load(col_index_in, col_index, 1),
        load(tile_count_in, tile_count, 2),
        load(branch_cost_in, branch_cost, 3),
        load(dispatch_cost_in, dispatch_cost, 4),
        load(root_cost_in, root_cost, 5),
        load(demand_in, demand, 6),
        load(branch_of_in, branch_of, 7),
    ]
    barrier = pltpu.get_barrier_semaphore()
    leads = here == 0
    for k in range(1, n_scen):
        device = {"scen": lax.rem(chip + k, n_scen), "dep": 1}
        pl.semaphore_signal(barrier, inc=1, device_id=device, device_id_type=MESH)

    @pl.when(here == 1)
    def _():
        pl.semaphore_signal(barrier, inc=1, device_id={"dep": other}, device_id_type=MESH)

    def put_rows(own, far, source):
        for c in range(source.shape[1] // tile):
            row_0 = source[0:1, c * tile : (c + 1) * tile]
            row_1 = source[1:2, c * tile : (c + 1) * tile]
            own[c : c + 1, :] = jnp.where(here == 0, row_0, row_1)
            if far is not None:
                far[c : c + 1, :] = jnp.where(here == 0, row_1, row_0)

    def pair(source, target, at):
        return pltpu.make_async_remote_copy(
            src_ref=source,
            dst_ref=target,
            send_sem=pair_send.at[at],
            recv_sem=pair_recv.at[at],
            device_id={"dep": other},
            device_id_type=MESH,
        )

    ids_copy = pair(ids_out, ids_in, 0)
    costs_copy = pair(costs_out, costs.at[1], 1)
    tiles_copy = pair(tiles.at[other], blocks.at[1], 2)

    @pl.when(leads)
    def _():
        pl.semaphore_wait(barrier, 1)
        pl.semaphore_signal(met, inc=1, device_id={"dep": other}, device_id_type=MESH)

    @pl.when(here == 1)
    def _():
        pl.semaphore_wait(met, 1)

    tiles_copy.start()
    own_tiles = pltpu.make_async_copy(tiles.at[here], blocks.at[0], local_sem)
    own_tiles.start()
    for copy in loads:
        copy.wait()
    put_rows(costs.at[0, 0], costs_out.at[0], branch_cost)
    put_rows(costs.at[0, 1], costs_out.at[1], dispatch_cost)
    costs_out[2] = root_cost[...]
    costs[0, 2] = root_cost[...]
    for j in range(slots):
        ids_out[j] = row_index[other, 0, 0, j]
        ids_out[slots + j] = col_index[other, 0, 0, j]
    ids_out[2 * slots] = tile_count[other]

    ids_copy.start()
    costs_copy.start()

    put_rows(cover_rows, None, demand)
    demand_here = cover_rows[...]

    row_ids, col_ids, row_marks, col_marks = [], [], [], []

    def take_ids(row_of, col_of, count):
        for j in range(slots):
            row, col = row_of(j), col_of(j)
            row_ids.append(row)
            col_ids.append(col)
            row_marks.append(jnp.where(j < count, row, -1))
            col_marks.append(jnp.where(j < count, col, -1))

    take_ids(
        lambda j: row_index[here, 0, 0, j],
        lambda j: col_index[here, 0, 0, j],
        tile_count[here],
    )
    ids_copy.wait()
    take_ids(lambda j: ids_in[j], lambda j: ids_in[slots + j], ids_in[2 * slots])

    lane_iota = lax.broadcasted_iota(jnp.int32, (row_blocks, tile), 0)
    col_iota = lax.broadcasted_iota(jnp.int32, (col_blocks, tile), 0)

    def spread(row, iota, mark):
        return jnp.where(iota == mark, jnp.broadcast_to(row, iota.shape), 0.0).astype(jnp.bfloat16)

    def backward(cover):
        cover_rows[...] = cover
        halves = []
        for half in range(2):
            left = []
            for n in range(half * slots, (half + 1) * slots):
                row = cover_rows[pl.ds(row_ids[n], 1), :]
                left.append(spread(row, col_iota, col_marks[n]))
            halves.append(dot(jnp.concatenate(left, axis=1), blocks[half].reshape(slots * tile, tile)))
        return jnp.concatenate(halves, axis=0)

    def forward(extrap):
        dispatch_rows[...] = extrap
        left = []
        for n in range(2 * slots):
            row = dispatch_rows[pl.ds(n // slots * col_blocks + col_ids[n], 1), :]
            left.append(spread(row, lane_iota, row_marks[n]))
        return dot(jnp.concatenate(left, axis=1), flipped[...].reshape(2 * slots * tile, tile))

    def flip(half):
        for j in range(slots):
            flipped[half, j] = blocks[half, j].T

    def place(index, rows):
        return pl.ds(pl.multiple_of(rows * index, 8), rows)

    def group(source, target, at, to):
        return pltpu.make_async_remote_copy(
            src_ref=source,
            dst_ref=target,
            send_sem=group_send.at[at],
            recv_sem=group_recv.at[at],
            device_id=device_of(to),
            device_id_type=MESH,
        )

    def many(rows, at):
        part = gather_in.at[0, pl.ds(0, rows)]
        return group(part, part, at, me + 1 - 2 * here)

    def either(test, mine, others):
        pl.when(test)(mine)
        pl.when(jnp.logical_not(test))(others)

    def in_order(x):
        own, far = x[:col_blocks], x[col_blocks:]
        return jnp.where(leads, own, far), jnp.where(leads, far, own)

    def to_owners(send):
        home = chip // owners * 2 + lax.rem(chip, 2)
        for k in reversed(range(owners)):
            to = first_owner + 2 * jnp.bitwise_xor(home, k) + 1
            if k:
                send(to)
            else:
                pl.when(jnp.logical_not(owns))(functools.partial(send, to))

    def branch_start():
        branch_out[...] = jnp.full((1, tile), branch_of[here].astype(jnp.float32), jnp.float32)

        def send(to):
            group(branch_out, branch_in.at[me], 2 * ITERS, to).start()

        to_owners(send)

    def branch_wait(count, wait):
        part = branch_in.at[pl.ds(0, count)]
        wait(group(part, part, 2 * ITERS, me + 1 - 2 * here))

    def gather_start(hedge_round, fleet, assign):
        buffer = gather_out.at[hedge_round]
        target = gather_in.at[hedge_round]
        fleets, assigns = in_order(fleet), in_order(assign)
        for half in range(2):
            buffer[32 * half : 32 * half + 16, :] = fleets[half]
            buffer[32 * half + 16 : 32 * half + 32, :] = assigns[half]

        def send(to):
            source = buffer.at[place((to - first_owner) // 4, 32)]
            group(source, target.at[place(me, 32)], hedge_round, to).start()

        to_owners(send)

        @pl.when(owns)
        def _():
            target[place(me, 32), :] = buffer[place(own_half, 32), :]

    def reply_start(hedge_round):
        pl.when(owns)(functools.partial(reply, hedge_round))

    def reply(hedge_round):
        if hedge_round == 0:
            branch_wait(members - 1, lambda copy: copy.wait_recv())
            branch_in[me] = branch_out[...]
        many(32 * (members - 1), hedge_round).wait_recv()
        buffer = gather_in.at[hedge_round]
        branches = [jnp.broadcast_to(branch_in[k], (8, tile)) for k in range(members)]
        near = plane == 0
        last = hedge_round == ITERS - 1
        for part in (0, 8):
            fleet_sum = buffer[part : part + 8, :]
            for k in range(1, members):
                fleet_sum = fleet_sum + buffer[32 * k + part : 32 * k + part + 8, :]
            fleet_means = fleet_sum / total_scen
            assigns = [buffer[32 * k + 16 + part : 32 * k + 24 + part, :] for k in range(members)]
            sums = list(assigns)
            for k in range(members):
                for m in range(k + 1, members):
                    same = branches[k] == branches[m]
                    sums[k] = sums[k] + jnp.where(same, assigns[m], 0.0)
                    sums[m] = sums[m] + jnp.where(same, assigns[k], 0.0)
            for z in range(n_scen // 2):
                pair_means = [
                    jnp.where(near, sums[4 * z + c], sums[4 * z + 2 + c]) / per_branch for c in range(2)
                ]
                if last:
                    at = 48 * z + part
                    last_out[at : at + 8, :] = fleet_means
                    last_out[at + 16 : at + 24, :] = pair_means[0]
                    last_out[at + 32 : at + 40, :] = pair_means[1]
                else:
                    for c in range(2):
                        at = 32 * (2 * z + c) + part
                        reply_out[at : at + 8, :] = fleet_means
                        reply_out[at + 16 : at + 24, :] = pair_means[c]
        if last:
            def send(k):
                there = jnp.bitwise_xor(chip // 2, k)
                source = last_out.at[place(there, 48)]
                to = 4 * there + 2 * plane + own_half
                group(source, last_in, ITERS + hedge_round, to).start()

            for k in (2, 3, 1):
                send(k)

            @pl.when(own_half == 0)
            def _():
                send(0)

            @pl.when(own_half == 1)
            def _():
                last_in[...] = last_out[place(chip // 2, 48), :]
        else:
            slot = chip // 2 * 2 + 1
            for k in (5, 4, 7, 6, 3, 2, 1):
                there = jnp.bitwise_xor(slot, k)
                to = there // 2 * 4 + 2 * plane + lax.rem(there, 2)
                source, target = reply_out.at[place(there, 32)], reply_in.at[place(own_half, 32)]
                group(source, target, ITERS + hedge_round, to).start()
            reply_in[place(own_half, 32), :] = reply_out[place(slot, 32), :]

    def reply_wait(hedge_round):
        at = ITERS + hedge_round
        if hedge_round < ITERS - 1:
            either(owns, lambda: many(32, at).wait_recv(), lambda: many(64, at).wait_recv())
        else:
            pl.when(jnp.logical_not(own_ends))(lambda: many(48, at).wait_recv())

    def reply_all(k):
        halves = [reply_in[k : k + 16, :], reply_in[32 + k : 48 + k, :]]
        return jnp.concatenate(in_order(jnp.concatenate(halves, axis=0)), axis=0)

    def last_half(k):
        return last_in[k : k + 16, :]

    def group_enter():
        @pl.when(here == 1)
        def _():
            pl.semaphore_wait(barrier, members - 2)
            pl.semaphore_signal(entered, inc=1, device_id={"dep": other}, device_id_type=MESH)

        @pl.when(leads)
        def _():
            pl.semaphore_wait(entered, 1)

    zeros = jnp.zeros((2 * col_blocks, tile), jnp.float32)
    fleet = assign = dispatch = fleet_dual = assign_dual = fleet_price = assign_price = zeros
    fleet_mean = assign_mean = zeros
    cover = jnp.zeros((row_blocks, tile), jnp.float32)
    ratio = jnp.ones((1, 1), jnp.float32)
    costs_copy.wait()
    branch_c = jnp.concatenate([costs[0, 0], costs[1, 0]], axis=0)
    dispatch_c = jnp.concatenate([costs[0, 1], costs[1, 1]], axis=0)
    root_c = jnp.concatenate([costs[0, 2], costs[1, 2]], axis=0)
    own_tiles.wait()
    flip(0)
    tiles_copy.wait()
    flip(1)

    pulled = zeros
    for hedge_round in range(ITERS):
        penalty_now = 0.0 if hedge_round == 0 else penalty
        for inner_step in range(STEPS):
            ends = inner_step == STEPS - 1
            closing = hedge_round == ITERS - 1 and ends
            waits = hedge_round > 0 and inner_step == 0
            primal_step = step_scale / ratio
            dual_step = step_scale * ratio

            def plans():
                pull_f = root_c + fleet_price - fleet_dual
                pull_a = branch_c + assign_price + fleet_dual - assign_dual
                if penalty_now:
                    pull_f = pull_f + penalty_now * (fleet - fleet_mean)
                    pull_a = pull_a + penalty_now * (assign - assign_mean)
                return (
                    jnp.maximum(0.0, fleet - primal_step * pull_f),
                    jnp.maximum(0.0, assign - primal_step * pull_a),
                )

            if not waits:
                fleet_new, assign_new = plans()
            if hedge_round == 0 and inner_step == STEPS - 2:
                group_enter()
                branch_start()
            if ends:
                gather_start(hedge_round, fleet_new, assign_new)
            if closing:
                for k, x in enumerate((fleet_new, assign_new, fleet_price, assign_price)):
                    early_out[k] = x[col_blocks:]
                early_copy = pair(early_out, early_in, 3)
                early_copy.start()
            dispatch_new = jnp.maximum(0.0, dispatch - primal_step * (dispatch_c + assign_dual - pulled))
            dispatch_ext = 2.0 * dispatch_new - dispatch
            load = forward(dispatch_ext)
            cover_new = jnp.maximum(0.0, cover + dual_step * (demand_here - load))
            if not closing:
                pulled = backward(cover_new)
            if closing:
                late_out[0] = dispatch_new[col_blocks:]
                late_out[1] = cover_new
                late_copy = pair(late_out, late_in, 4)
                late_copy.start()
            if waits:
                reply_wait(hedge_round - 1)
                fleet_mean = reply_all(0)
                assign_mean = reply_all(16)
                fleet_price = fleet_price + penalty * (fleet - fleet_mean)
                assign_price = assign_price + penalty * (assign - assign_mean)
                fleet_new, assign_new = plans()
            if not closing:
                fleet_ext = 2.0 * fleet_new - fleet
                assign_ext = 2.0 * assign_new - assign
                assign_dual_new = jnp.maximum(0.0, assign_dual + dual_step * (dispatch_ext - assign_ext))
                fleet_dual_new = jnp.maximum(0.0, fleet_dual + dual_step * (assign_ext - fleet_ext))
                primal_moves = total(
                    (fleet_new - fleet) ** 2 + (assign_new - assign) ** 2 + (dispatch_new - dispatch) ** 2
                )
                pair_moves = (assign_dual_new - assign_dual) ** 2 + (fleet_dual_new - fleet_dual) ** 2
                dual_moves = total(pair_moves[:row_blocks] + pair_moves[row_blocks:] + (cover_new - cover) ** 2)
                primal_rate = primal_moves / (3.0 * col_total)
                dual_rate = dual_moves / (lane_total + 2.0 * col_total)
                target = jnp.sqrt((primal_rate + epsilon) / (dual_rate + epsilon))
                ratio = jnp.sqrt(ratio * target)
                fleet_dual, assign_dual = fleet_dual_new, assign_dual_new
            fleet, assign, dispatch, cover = fleet_new, assign_new, dispatch_new, cover_new
            if ends:
                reply_start(hedge_round)

    def put_out(at, own, far):
        row_0, row_1 = jnp.where(here == 0, own, far), jnp.where(here == 0, far, own)
        for c in range(own.shape[0]):
            packed[at, 0:1, c * tile : (c + 1) * tile] = row_0[c : c + 1]
            packed[at, 1:2, c * tile : (c + 1) * tile] = row_1[c : c + 1]

    early_copy.wait()
    put_out(0, fleet[:col_blocks], early_in[0])
    put_out(1, assign[:col_blocks], early_in[1])
    late_copy.wait()
    put_out(2, dispatch[:col_blocks], late_in[0])
    put_out(3, cover, late_in[1])
    reply_wait(ITERS - 1)
    last_fleet, even_mean, odd_mean = last_half(0), last_half(16), last_half(32)
    own_mean = jnp.where(here == 0, even_mean, odd_mean)
    far_mean = jnp.where(here == 0, odd_mean, even_mean)
    put_out(
        4,
        fleet_price[:col_blocks] + penalty * (fleet[:col_blocks] - last_fleet),
        early_in[2] + penalty * (early_in[0] - last_fleet),
    )
    put_out(
        5,
        assign_price[:col_blocks] + penalty * (assign[:col_blocks] - own_mean),
        early_in[3] + penalty * (early_in[1] - far_mean),
    )

    def sent_by_owner():
        branch_wait(owners - 1, lambda copy: copy.wait_send())
        for r in range(ITERS):
            many(32 * (owners - 1), r).wait_send()
        many(32 * (n_scen - 1), ITERS).wait_send()
        either(
            own_ends,
            lambda: many(48 * (n_scen // 2 - 1), 2 * ITERS - 1).wait_send(),
            lambda: many(48 * (n_scen // 2), 2 * ITERS - 1).wait_send(),
        )

    def sent_by_others():
        branch_wait(owners, lambda copy: copy.wait_send())
        for r in range(ITERS):
            many(32 * owners, r).wait_send()

    either(owns, sent_by_owner, sent_by_others)


def unpack(packed, *outs):
    for k, out in enumerate(outs):
        out[...] = packed[k]


def fused_local(
    n_scen,
    tiles,
    row_index,
    col_index,
    tile_count,
    demand,
    root_cost,
    branch_cost,
    dispatch_cost,
    branch_of,
):
    slots, tile = tiles.shape[3], tiles.shape[5]
    lane_rows, width = demand.shape[1], branch_cost.shape[1]
    rows, cols, members = lane_rows // tile, width // tile, 2 * n_scen
    f32, i32 = jnp.float32, jnp.int32
    anywhere = pl.BlockSpec(memory_space=pl.ANY)
    col_shape = jax.ShapeDtypeStruct((2, width), f32)
    packed = pl.pallas_call(
        functools.partial(fused, n_scen),
        out_shape=jax.ShapeDtypeStruct((6, 2, width), f32),
        in_specs=[pl.BlockSpec(memory_space=pltpu.HBM)] * 9,
        out_specs=pl.BlockSpec(memory_space=pltpu.VMEM),
        scratch_shapes=[
            pltpu.SMEM(row_index.shape, i32),
            pltpu.SMEM(col_index.shape, i32),
            pltpu.SMEM((2,), i32),
            pltpu.SMEM(branch_of.shape, i32),
            pltpu.VMEM(demand.shape, f32),
            pltpu.VMEM((cols, tile), f32),
            pltpu.VMEM(branch_cost.shape, f32),
            pltpu.VMEM(dispatch_cost.shape, f32),
            pltpu.VMEM((2, slots, tile, tile), jnp.bfloat16),
            pltpu.VMEM((2, slots, tile, tile), jnp.bfloat16),
            pltpu.VMEM((3, cols, tile), f32),
            pltpu.VMEM((2, 3, cols, tile), f32),
            pltpu.SMEM((4 * slots,), jnp.int32),
            pltpu.SMEM((4 * slots,), jnp.int32),
            pltpu.VMEM((rows, tile), f32),
            pltpu.VMEM((2 * cols, tile), f32),
            pltpu.VMEM((ITERS, 4 * members, tile), f32),
            pltpu.VMEM((ITERS, 32 * members, tile), f32),
            pltpu.VMEM((16 * members, tile), f32),
            pltpu.VMEM((4 * members, tile), f32),
            pltpu.VMEM((24 * n_scen, tile), f32),
            pltpu.VMEM((48, tile), f32),
            pltpu.VMEM((1, tile), f32),
            pltpu.VMEM((members, 1, tile), f32),
            pltpu.VMEM((4, cols, tile), f32),
            pltpu.VMEM((4, cols, tile), f32),
            pltpu.VMEM((2, cols, tile), f32),
            pltpu.VMEM((2, cols, tile), f32),
            pltpu.SemaphoreType.DMA,
            pltpu.SemaphoreType.DMA((8,)),
            pltpu.SemaphoreType.DMA((5,)),
            pltpu.SemaphoreType.DMA((5,)),
            pltpu.SemaphoreType.DMA((2 * ITERS + 1,)),
            pltpu.SemaphoreType.DMA((2 * ITERS + 1,)),
            pltpu.SemaphoreType.REGULAR,
            pltpu.SemaphoreType.REGULAR,
        ],
        compiler_params=pltpu.CompilerParams(
            collective_id=0, has_side_effects=True, vmem_limit_bytes=60 * 1024 * 1024
        ),
    )(
        tiles.reshape(2, slots, tile, tile),
        row_index,
        col_index,
        tile_count.reshape(2),
        demand,
        root_cost.reshape(cols, tile),
        branch_cost,
        dispatch_cost,
        branch_of,
    )
    return pl.pallas_call(
        unpack,
        out_shape=(col_shape,) * 6,
        in_specs=[pl.BlockSpec(memory_space=pltpu.VMEM)],
        out_specs=(pl.BlockSpec(memory_space=pltpu.VMEM),) * 6,
    )(packed)


def solution_body(mesh):
    n_scen = mesh.shape["scen"]
    fits = mesh.shape["lane"] == 1 and mesh.shape["dep"] == 2 and (2 * n_scen) % BRANCHES == 0

    def body(*args):
        tiles, demand, root_cost = args[0], args[4], args[5]
        tile = tiles.shape[5]
        cols, rows = root_cost.shape[0] // tile, demand.shape[1] // tile
        if fits and tiles.shape[0] == 2 and tile == 128 and cols == rows == 2 * n_scen and cols == 16:
            return fused_local(n_scen, *args)
        return local(*args)

    return body


def solution(mesh):
    in_specs = (
        P(("groups", "scen"), "lane", "dep", None, None, None),
        P(("groups", "scen"), "lane", "dep", None),
        P(("groups", "scen"), "lane", "dep", None),
        P(("groups", "scen"), "lane", "dep"),
        P(("groups", "scen"), "lane"),
        P(("groups", "dep")),
        P(("groups", "scen"), "dep"),
        P(("groups", "scen"), "dep"),
        P(("groups", "scen")),
    )
    out_specs = (
        P(("groups", "scen"), "dep"),
        P(("groups", "scen"), "dep"),
        P(("groups", "scen"), "dep"),
        P(("groups", "scen"), "lane"),
        P(("groups", "scen"), "dep"),
        P(("groups", "scen"), "dep"),
    )
    body = solution_body(mesh)
    return jax.shard_map(body, mesh=mesh, in_specs=in_specs, out_specs=out_specs, check_vma=False)
```

```python
import functools

import jax
import jax.numpy as jnp
from jax import lax
from jax.experimental import pallas as pl
from jax.experimental.pallas import tpu as pltpu
from jax.sharding import PartitionSpec as P

BRANCHES = 8
ITERS = 2
STEPS = 4


step_scale = 0.2
penalty = 1.0
epsilon = 1e-06


def reweigh(weight_ratio, totals, col_total, lane_total):
    primal_rate = totals[:, 0] / (3.0 * col_total)
    dual_rate = totals[:, 1] / (lane_total + 2.0 * col_total)
    target = jnp.sqrt((primal_rate + epsilon) / (dual_rate + epsilon))
    return jnp.sqrt(weight_ratio * target)


def pick_rows(source, places):
    return source[places]


def local(
    tiles,
    row_index,
    col_index,
    tile_count,
    demand,
    root_cost,
    branch_cost,
    dispatch_cost,
    branch_of,
):
    highest = lax.Precision.HIGHEST
    scen_here = tiles.shape[0]
    slots = tiles.shape[3]
    tile_size = tiles.shape[5]
    blocks = tiles.reshape(scen_here, slots, tile_size, tile_size)
    row_ids = row_index.reshape(scen_here, slots)
    col_ids = col_index.reshape(scen_here, slots)
    live_count = tile_count.reshape(scen_here)
    width = root_cost.shape[0]
    lane_rows = demand.shape[1]
    col_blocks = width // tile_size
    row_blocks = lane_rows // tile_size
    lane_count = lax.axis_size("lane")
    col_total = float(width * lax.axis_size("dep"))
    lane_total = float(lane_rows * lane_count)
    slot_iota = lax.broadcasted_iota(jnp.int32, (scen_here, slots), 1)
    live_mask = (slot_iota < live_count[:, None]).astype(jnp.float32)
    row_table = (row_ids[:, :, None] == jnp.arange(row_blocks, dtype=jnp.int32)).astype(
        jnp.float32
    ) * live_mask[:, :, None]
    col_table = (col_ids[:, :, None] == jnp.arange(col_blocks, dtype=jnp.int32)).astype(
        jnp.float32
    ) * live_mask[:, :, None]
    single_copy = (lax.axis_index("lane") == 0).astype(jnp.float32)
    dep_first = (lax.axis_index("dep") == 0).astype(jnp.float32)
    zeros_cols = jnp.zeros((scen_here, width), jnp.float32)
    fleet_plan = zeros_cols
    assign_plan = zeros_cols
    dispatch_plan = zeros_cols
    fleet_dual = zeros_cols
    assign_dual = zeros_cols
    fleet_price = zeros_cols
    assign_price = zeros_cols
    assign_mean = zeros_cols
    fleet_mean = jnp.zeros((width,), jnp.float32)
    cover_dual = jnp.zeros((scen_here, lane_rows), jnp.float32)
    weight_ratio = jnp.ones((scen_here,), jnp.float32)
    branch_table = (branch_of[:, None] == jnp.arange(BRANCHES, dtype=jnp.int32)).astype(jnp.float32)
    total_scen = scen_here * lax.axis_size("scen")
    per_branch = total_scen // BRANCHES
    for hedge_round in range(ITERS):
        penalty_now = 0.0 if hedge_round == 0 else penalty
        for inner_step in range(STEPS):
            closing = hedge_round == ITERS - 1 and inner_step == STEPS - 1
            picked = jax.vmap(pick_rows)(
                cover_dual.astype(jnp.bfloat16).reshape(scen_here, row_blocks, tile_size), row_ids
            )
            products = jnp.einsum(
                "snij,sni->snj", blocks, picked, preferred_element_type=jnp.float32
            )
            partial_value = jnp.einsum(
                "snc,snj->scj", col_table, products, precision=highest
            ).reshape(scen_here, width)
            pulled = lax.psum(partial_value, "lane")
            primal_step = step_scale / weight_ratio[:, None]
            dual_step = step_scale * weight_ratio[:, None]
            fleet_new = jnp.maximum(
                0.0,
                fleet_plan
                - primal_step
                * (
                    root_cost[None, :]
                    + fleet_price
                    + penalty_now * (fleet_plan - fleet_mean[None, :])
                    - fleet_dual
                ),
            )
            assign_new = jnp.maximum(
                0.0,
                assign_plan
                - primal_step
                * (
                    branch_cost
                    + assign_price
                    + penalty_now * (assign_plan - assign_mean)
                    + fleet_dual
                    - assign_dual
                ),
            )
            dispatch_new = jnp.maximum(
                0.0, dispatch_plan - primal_step * (dispatch_cost + assign_dual - pulled)
            )
            fleet_ext = 2.0 * fleet_new - fleet_plan
            assign_ext = 2.0 * assign_new - assign_plan
            dispatch_ext = 2.0 * dispatch_new - dispatch_plan
            assign_dual_new = jnp.maximum(
                0.0, assign_dual + dual_step * (dispatch_ext - assign_ext)
            )
            fleet_dual_new = jnp.maximum(0.0, fleet_dual + dual_step * (assign_ext - fleet_ext))
            extrap_bf = dispatch_ext.astype(jnp.bfloat16)
            forward_picked = jax.vmap(pick_rows)(
                extrap_bf.reshape(scen_here, col_blocks, tile_size), col_ids
            )
            forward_products = jnp.einsum(
                "snij,snj->sni", blocks, forward_picked, preferred_element_type=jnp.float32
            )
            load_part = jnp.einsum(
                "snr,sni->sri", row_table, forward_products, precision=highest
            ).reshape(scen_here, lane_rows)
            primal_moves = single_copy * jnp.sum(
                (fleet_new - fleet_plan) ** 2
                + (assign_new - assign_plan) ** 2
                + (dispatch_new - dispatch_plan) ** 2,
                axis=1,
            )
            pair_moves = single_copy * jnp.sum(
                (assign_dual_new - assign_dual) ** 2 + (fleet_dual_new - fleet_dual) ** 2, axis=1
            )
            lane_load = lax.psum(load_part, "dep")
            cover_new = jnp.maximum(0.0, cover_dual + dual_step * (demand - lane_load))
            cover_moves = jnp.sum((cover_new - cover_dual) ** 2, axis=1)
            if not closing:
                totals = lax.psum(
                    jnp.stack([primal_moves, pair_moves + dep_first * cover_moves], axis=1),
                    ("lane", "dep"),
                )
                weight_ratio = reweigh(weight_ratio, totals, col_total, lane_total)
            fleet_plan, assign_plan, dispatch_plan = (fleet_new, assign_new, dispatch_new)
            fleet_dual, assign_dual, cover_dual = (fleet_dual_new, assign_dual_new, cover_new)
        root_local = jnp.sum(fleet_plan, axis=0)
        branch_local = jnp.dot(branch_table.T, assign_plan, precision=highest)
        root_total, branch_total = lax.psum((root_local, branch_local), "scen")
        fleet_mean = root_total / total_scen
        branch_means = branch_total / per_branch
        assign_mean = jnp.dot(branch_table, branch_means, precision=highest)
        fleet_price = fleet_price + penalty * (fleet_plan - fleet_mean[None, :])
        assign_price = assign_price + penalty * (assign_plan - assign_mean)
    return (fleet_plan, assign_plan, dispatch_plan, cover_dual, fleet_price, assign_price)


MESH = pl.DeviceIdType.MESH


def dot(a, b):
    return jnp.dot(a, b, preferred_element_type=jnp.float32)


def dot_t(a, b):
    return lax.dot_general(a, b, (((1,), (1,)), ((), ())), preferred_element_type=jnp.float32)


def total(x):
    return jnp.sum(x, axis=(0, 1), keepdims=True)


def fused(
    n_scen,
    tiles,
    row_index_in,
    col_index_in,
    tile_count_in,
    demand_in,
    root_cost_in,
    branch_cost_in,
    dispatch_cost_in,
    branch_of_in,
    packed,
    row_index,
    col_index,
    tile_count,
    branch_of,
    demand,
    root_cost,
    branch_cost,
    dispatch_cost,
    blocks,
    flipped,
    costs_out,
    costs,
    ids_out,
    ids_in,
    cover_rows,
    dispatch_rows,
    gather_out,
    gather_in,
    reply_out,
    reply_in,
    last_out,
    last_in,
    branch_out,
    branch_in,
    early_out,
    early_in,
    late_out,
    late_in,
    local_sem,
    load_sem,
    pair_send,
    pair_recv,
    group_send,
    group_recv,
    entered,
    met,
):
    here = lax.axis_index("dep")
    other = 1 - here
    chip = lax.axis_index("scen")
    me = 2 * chip + here
    members = 2 * n_scen
    slots = tiles.shape[1]
    tile = tiles.shape[2]
    lane_rows = demand.shape[1]
    width = branch_cost.shape[1]
    row_blocks = lane_rows // tile
    col_blocks = width // tile
    col_total = float(2 * width)
    lane_total = float(lane_rows)
    total_scen = float(members)
    per_branch = float(members // BRANCHES)

    owners = members // 4
    first_owner = members // 4
    owner = chip - first_owner // 2
    owns = jnp.logical_and(here == 1, jnp.logical_and(owner >= 0, owner < owners))
    plane = lax.rem(chip, 2)
    own_half = owner // 2
    own_ends = jnp.logical_and(owns, owner >= 2)

    def device_of(to):
        return {"scen": to // 2, "dep": lax.rem(to, 2)}

    def load(source, target, at):
        copy = pltpu.make_async_copy(source, target, load_sem.at[at])
        copy.start()
        return copy

    loads = [
        load(row_index_in, row_index, 0),
        load(col_index_in, col_index, 1),
        load(tile_count_in, tile_count, 2),
        load(branch_cost_in, branch_cost, 3),
        load(dispatch_cost_in, dispatch_cost, 4),
        load(root_cost_in, root_cost, 5),
        load(demand_in, demand, 6),
        load(branch_of_in, branch_of, 7),
    ]
    barrier = pltpu.get_barrier_semaphore()
    leads = here == 0
    for k in range(1, n_scen):
        device = {"scen": lax.rem(chip + k, n_scen), "dep": 1}
        pl.semaphore_signal(barrier, inc=1, device_id=device, device_id_type=MESH)

    @pl.when(here == 1)
    def _():
        pl.semaphore_signal(barrier, inc=1, device_id={"dep": other}, device_id_type=MESH)

    def put_rows(own, far, source):
        for c in range(source.shape[1] // tile):
            row_0 = source[0:1, c * tile : (c + 1) * tile]
            row_1 = source[1:2, c * tile : (c + 1) * tile]
            own[c : c + 1, :] = jnp.where(here == 0, row_0, row_1)
            if far is not None:
                far[c : c + 1, :] = jnp.where(here == 0, row_1, row_0)

    def pair(source, target, at):
        return pltpu.make_async_remote_copy(
            src_ref=source,
            dst_ref=target,
            send_sem=pair_send.at[at],
            recv_sem=pair_recv.at[at],
            device_id={"dep": other},
            device_id_type=MESH,
        )

    ids_copy = pair(ids_out, ids_in, 0)
    costs_copy = pair(costs_out, costs.at[1], 1)
    tiles_copy = pair(tiles.at[other], blocks.at[1], 2)

    @pl.when(leads)
    def _():
        pl.semaphore_wait(barrier, 1)
        pl.semaphore_signal(met, inc=1, device_id={"dep": other}, device_id_type=MESH)

    @pl.when(here == 1)
    def _():
        pl.semaphore_wait(met, 1)

    tiles_copy.start()
    own_tiles = pltpu.make_async_copy(tiles.at[here], blocks.at[0], local_sem)
    own_tiles.start()
    for copy in loads:
        copy.wait()
    put_rows(costs.at[0, 0], costs_out.at[0], branch_cost)
    put_rows(costs.at[0, 1], costs_out.at[1], dispatch_cost)
    costs_out[2] = root_cost[...]
    costs[0, 2] = root_cost[...]
    for j in range(slots):
        ids_out[j] = row_index[other, 0, 0, j]
        ids_out[slots + j] = col_index[other, 0, 0, j]
    ids_out[2 * slots] = tile_count[other]

    ids_copy.start()
    costs_copy.start()

    put_rows(cover_rows, None, demand)
    demand_here = cover_rows[...]

    row_ids, col_ids, row_marks, col_marks = [], [], [], []

    def take_ids(row_of, col_of, count):
        for j in range(slots):
            row, col = row_of(j), col_of(j)
            row_ids.append(row)
            col_ids.append(col)
            row_marks.append(jnp.where(j < count, row, -1))
            col_marks.append(jnp.where(j < count, col, -1))

    take_ids(
        lambda j: row_index[here, 0, 0, j],
        lambda j: col_index[here, 0, 0, j],
        tile_count[here],
    )
    ids_copy.wait()
    take_ids(lambda j: ids_in[j], lambda j: ids_in[slots + j], ids_in[2 * slots])

    lane_iota = lax.broadcasted_iota(jnp.int32, (row_blocks, tile), 0)
    col_iota = lax.broadcasted_iota(jnp.int32, (col_blocks, tile), 0)

    def spread(row, iota, mark):
        return jnp.where(iota == mark, jnp.broadcast_to(row, iota.shape), 0.0).astype(jnp.bfloat16)

    def backward(cover):
        cover_rows[...] = cover
        halves = []
        for half in range(2):
            left = []
            for n in range(half * slots, (half + 1) * slots):
                row = cover_rows[pl.ds(row_ids[n], 1), :]
                left.append(spread(row, col_iota, col_marks[n]))
            halves.append(dot(jnp.concatenate(left, axis=1), blocks[half].reshape(slots * tile, tile)))
        return jnp.concatenate(halves, axis=0)

    def forward(extrap):
        dispatch_rows[...] = extrap
        left = []
        for n in range(2 * slots):
            row = dispatch_rows[pl.ds(n // slots * col_blocks + col_ids[n], 1), :]
            left.append(spread(row, lane_iota, row_marks[n]))
        return dot(jnp.concatenate(left, axis=1), flipped[...].reshape(2 * slots * tile, tile))

    def flip(half):
        for j in range(slots):
            flipped[half, j] = blocks[half, j].T

    def place(index, rows):
        return pl.ds(pl.multiple_of(rows * index, 8), rows)

    def group(source, target, at, to):
        return pltpu.make_async_remote_copy(
            src_ref=source,
            dst_ref=target,
            send_sem=group_send.at[at],
            recv_sem=group_recv.at[at],
            device_id=device_of(to),
            device_id_type=MESH,
        )

    def many(rows, at):
        part = gather_in.at[0, pl.ds(0, rows)]
        return group(part, part, at, me + 1 - 2 * here)

    def either(test, mine, others):
        pl.when(test)(mine)
        pl.when(jnp.logical_not(test))(others)

    def in_order(x):
        own, far = x[:col_blocks], x[col_blocks:]
        return jnp.where(leads, own, far), jnp.where(leads, far, own)

    def to_owners(send):
        home = chip // owners * 2 + lax.rem(chip, 2)
        for k in reversed(range(owners)):
            to = first_owner + 2 * jnp.bitwise_xor(home, k) + 1
            if k:
                send(to)
            else:
                pl.when(jnp.logical_not(owns))(functools.partial(send, to))

    def branch_start():
        branch_out[...] = jnp.full((1, tile), branch_of[here].astype(jnp.float32), jnp.float32)

        def send(to):
            group(branch_out, branch_in.at[me], 2 * ITERS, to).start()

        to_owners(send)

    def branch_wait(count, wait):
        part = branch_in.at[pl.ds(0, count)]
        wait(group(part, part, 2 * ITERS, me + 1 - 2 * here))

    def gather_start(hedge_round, fleet, assign):
        buffer = gather_out.at[hedge_round]
        target = gather_in.at[hedge_round]
        fleets, assigns = in_order(fleet), in_order(assign)
        for half in range(2):
            buffer[32 * half : 32 * half + 16, :] = fleets[half]
            buffer[32 * half + 16 : 32 * half + 32, :] = assigns[half]

        def send(to):
            source = buffer.at[place((to - first_owner) // 4, 32)]
            group(source, target.at[place(me, 32)], hedge_round, to).start()

        to_owners(send)

        @pl.when(owns)
        def _():
            target[place(me, 32), :] = buffer[place(own_half, 32), :]

    def reply_start(hedge_round):
        pl.when(owns)(functools.partial(reply, hedge_round))

    def reply(hedge_round):
        if hedge_round == 0:
            branch_wait(members - 1, lambda copy: copy.wait_recv())
            branch_in[me] = branch_out[...]
        many(32 * (members - 1), hedge_round).wait_recv()
        buffer = gather_in.at[hedge_round]
        branches = [jnp.broadcast_to(branch_in[k], (8, tile)) for k in range(members)]
        near = plane == 0
        last = hedge_round == ITERS - 1
        for part in (0, 8):
            fleet_sum = buffer[part : part + 8, :]
            for k in range(1, members):
                fleet_sum = fleet_sum + buffer[32 * k + part : 32 * k + part + 8, :]
            fleet_means = fleet_sum / total_scen
            assigns = [buffer[32 * k + 16 + part : 32 * k + 24 + part, :] for k in range(members)]
            sums = list(assigns)
            for k in range(members):
                for m in range(k + 1, members):
                    same = branches[k] == branches[m]
                    sums[k] = sums[k] + jnp.where(same, assigns[m], 0.0)
                    sums[m] = sums[m] + jnp.where(same, assigns[k], 0.0)
            for z in range(n_scen // 2):
                pair_means = [
                    jnp.where(near, sums[4 * z + c], sums[4 * z + 2 + c]) / per_branch for c in range(2)
                ]
                if last:
                    at = 48 * z + part
                    last_out[at : at + 8, :] = fleet_means
                    last_out[at + 16 : at + 24, :] = pair_means[0]
                    last_out[at + 32 : at + 40, :] = pair_means[1]
                else:
                    for c in range(2):
                        at = 32 * (2 * z + c) + part
                        reply_out[at : at + 8, :] = fleet_means
                        reply_out[at + 16 : at + 24, :] = pair_means[c]
        if last:
            def send(k):
                there = jnp.bitwise_xor(chip // 2, k)
                source = last_out.at[place(there, 48)]
                to = 4 * there + 2 * plane + own_half
                group(source, last_in, ITERS + hedge_round, to).start()

            for k in (2, 3, 1):
                send(k)

            @pl.when(own_half == 0)
            def _():
                send(0)

            @pl.when(own_half == 1)
            def _():
                last_in[...] = last_out[place(chip // 2, 48), :]
        else:
            slot = chip // 2 * 2 + 1
            for k in (5, 4, 7, 6, 3, 2, 1):
                there = jnp.bitwise_xor(slot, k)
                to = there // 2 * 4 + 2 * plane + lax.rem(there, 2)
                source, target = reply_out.at[place(there, 32)], reply_in.at[place(own_half, 32)]
                group(source, target, ITERS + hedge_round, to).start()
            reply_in[place(own_half, 32), :] = reply_out[place(slot, 32), :]

    def reply_wait(hedge_round):
        at = ITERS + hedge_round
        if hedge_round < ITERS - 1:
            either(owns, lambda: many(32, at).wait_recv(), lambda: many(64, at).wait_recv())
        else:
            pl.when(jnp.logical_not(own_ends))(lambda: many(48, at).wait_recv())

    def reply_all(k):
        halves = [reply_in[k : k + 16, :], reply_in[32 + k : 48 + k, :]]
        return jnp.concatenate(in_order(jnp.concatenate(halves, axis=0)), axis=0)

    def last_half(k):
        return last_in[k : k + 16, :]

    def group_enter():
        @pl.when(here == 1)
        def _():
            pl.semaphore_wait(barrier, members - 2)
            pl.semaphore_signal(entered, inc=1, device_id={"dep": other}, device_id_type=MESH)

        @pl.when(leads)
        def _():
            pl.semaphore_wait(entered, 1)

    zeros = jnp.zeros((2 * col_blocks, tile), jnp.float32)
    fleet = assign = dispatch = fleet_dual = assign_dual = fleet_price = assign_price = zeros
    fleet_mean = assign_mean = zeros
    cover = jnp.zeros((row_blocks, tile), jnp.float32)
    ratio = jnp.ones((1, 1), jnp.float32)
    costs_copy.wait()
    branch_c = jnp.concatenate([costs[0, 0], costs[1, 0]], axis=0)
    dispatch_c = jnp.concatenate([costs[0, 1], costs[1, 1]], axis=0)
    root_c = jnp.concatenate([costs[0, 2], costs[1, 2]], axis=0)
    own_tiles.wait()
    flip(0)
    tiles_copy.wait()
    flip(1)

    pulled = zeros
    for hedge_round in range(ITERS):
        penalty_now = 0.0 if hedge_round == 0 else penalty
        for inner_step in range(STEPS):
            ends = inner_step == STEPS - 1
            closing = hedge_round == ITERS - 1 and ends
            waits = hedge_round > 0 and inner_step == 0
            primal_step = step_scale / ratio
            dual_step = step_scale * ratio

            def plans():
                pull_f = root_c + fleet_price - fleet_dual
                pull_a = branch_c + assign_price + fleet_dual - assign_dual
                if penalty_now:
                    pull_f = pull_f + penalty_now * (fleet - fleet_mean)
                    pull_a = pull_a + penalty_now * (assign - assign_mean)
                return (
                    jnp.maximum(0.0, fleet - primal_step * pull_f),
                    jnp.maximum(0.0, assign - primal_step * pull_a),
                )

            if not waits:
                fleet_new, assign_new = plans()
            if hedge_round == 0 and inner_step == STEPS - 1:
                group_enter()
                branch_start()
            if ends:
                gather_start(hedge_round, fleet_new, assign_new)
            if closing:
                for k, x in enumerate((fleet_new, assign_new, fleet_price, assign_price)):
                    early_out[k] = x[col_blocks:]
                early_copy = pair(early_out, early_in, 3)
                early_copy.start()
            dispatch_new = jnp.maximum(0.0, dispatch - primal_step * (dispatch_c + assign_dual - pulled))
            dispatch_ext = 2.0 * dispatch_new - dispatch
            load = forward(dispatch_ext)
            cover_new = jnp.maximum(0.0, cover + dual_step * (demand_here - load))
            if not closing:
                pulled = backward(cover_new)
            if closing:
                late_out[0] = dispatch_new[col_blocks:]
                late_out[1] = cover_new
                late_copy = pair(late_out, late_in, 4)
                late_copy.start()
            if waits:
                reply_wait(hedge_round - 1)
                fleet_mean = reply_all(0)
                assign_mean = reply_all(16)
                fleet_price = fleet_price + penalty * (fleet - fleet_mean)
                assign_price = assign_price + penalty * (assign - assign_mean)
                fleet_new, assign_new = plans()
            if not closing:
                fleet_ext = 2.0 * fleet_new - fleet
                assign_ext = 2.0 * assign_new - assign
                assign_dual_new = jnp.maximum(0.0, assign_dual + dual_step * (dispatch_ext - assign_ext))
                fleet_dual_new = jnp.maximum(0.0, fleet_dual + dual_step * (assign_ext - fleet_ext))
                primal_moves = total(
                    (fleet_new - fleet) ** 2 + (assign_new - assign) ** 2 + (dispatch_new - dispatch) ** 2
                )
                pair_moves = (assign_dual_new - assign_dual) ** 2 + (fleet_dual_new - fleet_dual) ** 2
                dual_moves = total(pair_moves[:row_blocks] + pair_moves[row_blocks:] + (cover_new - cover) ** 2)
                primal_rate = primal_moves / (3.0 * col_total)
                dual_rate = dual_moves / (lane_total + 2.0 * col_total)
                target = jnp.sqrt((primal_rate + epsilon) / (dual_rate + epsilon))
                ratio = jnp.sqrt(ratio * target)
                fleet_dual, assign_dual = fleet_dual_new, assign_dual_new
            fleet, assign, dispatch, cover = fleet_new, assign_new, dispatch_new, cover_new
            if ends:
                reply_start(hedge_round)

    def put_out(at, own, far):
        row_0, row_1 = jnp.where(here == 0, own, far), jnp.where(here == 0, far, own)
        for c in range(own.shape[0]):
            packed[at, 0:1, c * tile : (c + 1) * tile] = row_0[c : c + 1]
            packed[at, 1:2, c * tile : (c + 1) * tile] = row_1[c : c + 1]

    early_copy.wait()
    put_out(0, fleet[:col_blocks], early_in[0])
    put_out(1, assign[:col_blocks], early_in[1])
    late_copy.wait()
    put_out(2, dispatch[:col_blocks], late_in[0])
    put_out(3, cover, late_in[1])
    reply_wait(ITERS - 1)
    last_fleet, even_mean, odd_mean = last_half(0), last_half(16), last_half(32)
    own_mean = jnp.where(here == 0, even_mean, odd_mean)
    far_mean = jnp.where(here == 0, odd_mean, even_mean)
    put_out(
        4,
        fleet_price[:col_blocks] + penalty * (fleet[:col_blocks] - last_fleet),
        early_in[2] + penalty * (early_in[0] - last_fleet),
    )
    put_out(
        5,
        assign_price[:col_blocks] + penalty * (assign[:col_blocks] - own_mean),
        early_in[3] + penalty * (early_in[1] - far_mean),
    )

    def sent_by_owner():
        branch_wait(owners - 1, lambda copy: copy.wait_send())
        for r in range(ITERS):
            many(32 * (owners - 1), r).wait_send()
        many(32 * (n_scen - 1), ITERS).wait_send()
        either(
            own_ends,
            lambda: many(48 * (n_scen // 2 - 1), 2 * ITERS - 1).wait_send(),
            lambda: many(48 * (n_scen // 2), 2 * ITERS - 1).wait_send(),
        )

    def sent_by_others():
        branch_wait(owners, lambda copy: copy.wait_send())
        for r in range(ITERS):
            many(32 * owners, r).wait_send()

    either(owns, sent_by_owner, sent_by_others)


def unpack(packed, *outs):
    for k, out in enumerate(outs):
        out[...] = packed[k]


def fused_local(
    n_scen,
    tiles,
    row_index,
    col_index,
    tile_count,
    demand,
    root_cost,
    branch_cost,
    dispatch_cost,
    branch_of,
):
    slots, tile = tiles.shape[3], tiles.shape[5]
    lane_rows, width = demand.shape[1], branch_cost.shape[1]
    rows, cols, members = lane_rows // tile, width // tile, 2 * n_scen
    f32, i32 = jnp.float32, jnp.int32
    anywhere = pl.BlockSpec(memory_space=pl.ANY)
    col_shape = jax.ShapeDtypeStruct((2, width), f32)
    packed = pl.pallas_call(
        functools.partial(fused, n_scen),
        out_shape=jax.ShapeDtypeStruct((6, 2, width), f32),
        in_specs=[pl.BlockSpec(memory_space=pltpu.HBM)] * 9,
        out_specs=pl.BlockSpec(memory_space=pltpu.VMEM),
        scratch_shapes=[
            pltpu.SMEM(row_index.shape, i32),
            pltpu.SMEM(col_index.shape, i32),
            pltpu.SMEM((2,), i32),
            pltpu.SMEM(branch_of.shape, i32),
            pltpu.VMEM(demand.shape, f32),
            pltpu.VMEM((cols, tile), f32),
            pltpu.VMEM(branch_cost.shape, f32),
            pltpu.VMEM(dispatch_cost.shape, f32),
            pltpu.VMEM((2, slots, tile, tile), jnp.bfloat16),
            pltpu.VMEM((2, slots, tile, tile), jnp.bfloat16),
            pltpu.VMEM((3, cols, tile), f32),
            pltpu.VMEM((2, 3, cols, tile), f32),
            pltpu.SMEM((4 * slots,), jnp.int32),
            pltpu.SMEM((4 * slots,), jnp.int32),
            pltpu.VMEM((rows, tile), f32),
            pltpu.VMEM((2 * cols, tile), f32),
            pltpu.VMEM((ITERS, 4 * members, tile), f32),
            pltpu.VMEM((ITERS, 32 * members, tile), f32),
            pltpu.VMEM((16 * members, tile), f32),
            pltpu.VMEM((4 * members, tile), f32),
            pltpu.VMEM((24 * n_scen, tile), f32),
            pltpu.VMEM((48, tile), f32),
            pltpu.VMEM((1, tile), f32),
            pltpu.VMEM((members, 1, tile), f32),
            pltpu.VMEM((4, cols, tile), f32),
            pltpu.VMEM((4, cols, tile), f32),
            pltpu.VMEM((2, cols, tile), f32),
            pltpu.VMEM((2, cols, tile), f32),
            pltpu.SemaphoreType.DMA,
            pltpu.SemaphoreType.DMA((8,)),
            pltpu.SemaphoreType.DMA((5,)),
            pltpu.SemaphoreType.DMA((5,)),
            pltpu.SemaphoreType.DMA((2 * ITERS + 1,)),
            pltpu.SemaphoreType.DMA((2 * ITERS + 1,)),
            pltpu.SemaphoreType.REGULAR,
            pltpu.SemaphoreType.REGULAR,
        ],
        compiler_params=pltpu.CompilerParams(
            collective_id=0, has_side_effects=True, vmem_limit_bytes=60 * 1024 * 1024
        ),
    )(
        tiles.reshape(2, slots, tile, tile),
        row_index,
        col_index,
        tile_count.reshape(2),
        demand,
        root_cost.reshape(cols, tile),
        branch_cost,
        dispatch_cost,
        branch_of,
    )
    return pl.pallas_call(
        unpack,
        out_shape=(col_shape,) * 6,
        in_specs=[pl.BlockSpec(memory_space=pltpu.VMEM)],
        out_specs=(pl.BlockSpec(memory_space=pltpu.VMEM),) * 6,
    )(packed)


def solution_body(mesh):
    n_scen = mesh.shape["scen"]
    fits = mesh.shape["lane"] == 1 and mesh.shape["dep"] == 2 and (2 * n_scen) % BRANCHES == 0

    def body(*args):
        tiles, demand, root_cost = args[0], args[4], args[5]
        tile = tiles.shape[5]
        cols, rows = root_cost.shape[0] // tile, demand.shape[1] // tile
        if fits and tiles.shape[0] == 2 and tile == 128 and cols == rows == 2 * n_scen and cols == 16:
            return fused_local(n_scen, *args)
        return local(*args)

    return body


def solution(mesh):
    in_specs = (
        P(("groups", "scen"), "lane", "dep", None, None, None),
        P(("groups", "scen"), "lane", "dep", None),
        P(("groups", "scen"), "lane", "dep", None),
        P(("groups", "scen"), "lane", "dep"),
        P(("groups", "scen"), "lane"),
        P(("groups", "dep")),
        P(("groups", "scen"), "dep"),
        P(("groups", "scen"), "dep"),
        P(("groups", "scen")),
    )
    out_specs = (
        P(("groups", "scen"), "dep"),
        P(("groups", "scen"), "dep"),
        P(("groups", "scen"), "dep"),
        P(("groups", "scen"), "lane"),
        P(("groups", "scen"), "dep"),
        P(("groups", "scen"), "dep"),
    )
    body = solution_body(mesh)
    return jax.shard_map(body, mesh=mesh, in_specs=in_specs, out_specs=out_specs, check_vma=False)
```
